32 devices in a mesh: dp: 8 (over z, x), seq: 4 (over y, core).
Axes of the slice: x: 2, y: 2, z: 4, core: 2. Of those that a mesh axis runs over, the one named last changes fastest.
Arguments:
- tokens: bfloat16 [8, 1024, 320], P('dp', 'seq'), may hold values from -6 to 6
- segment_ids: int32 [8, 1024], P('dp'), may hold values from 0 to 3, as said below
- ln1_gain: float32 [320], replicated, may hold values from 0.5 to 1.5
- ln1_bias: float32 [320], replicated, may hold values from -3 to 3
- w_qkv: bfloat16 [320, 960], replicated, may hold values from -0.3125 to 0.3125
- b_qkv: float32 [960], replicated, may hold values from -3 to 3
- w_out: bfloat16 [320, 320], replicated, may hold values from -1.25 to 1.25
- b_out: float32 [320], replicated, may hold values from -3 to 3
- ln2_gain: float32 [320], replicated, may hold values from 0.5 to 1.5
- ln2_bias: float32 [320], replicated, may hold values from -3 to 3
- w_up: bfloat16 [320, 1280], replicated, may hold values from -0.3125 to 0.3125
- b_up: float32 [1280], replicated, may hold values from -3 to 3
- w_down: bfloat16 [1280, 320], replicated, may hold values from -0.15625 to 0.15625
- b_down: float32 [320], replicated, may hold values from -3 to 3
- cotangent: bfloat16 [8, 1024, 320], P('dp', 'seq'), may hold values from -6 to 6
Outputs:
- output: bfloat16 [8, 1024, 320], P('dp', 'seq')
- input_grad: float32 [8, 1024, 320], P('dp', 'seq')
- grad_ln1_gain: float32 [320], replicated
- grad_ln1_bias: float32 [320], replicated
- grad_w_qkv: float32 [320, 960], replicated
- grad_b_qkv: float32 [960], replicated
- grad_w_out: float32 [320, 320], replicated
- grad_b_out: float32 [320], replicated
- grad_ln2_gain: float32 [320], replicated
- grad_ln2_bias: float32 [320], replicated
- grad_w_up: float32 [320, 1280], replicated
- grad_b_up: float32 [1280], replicated
- grad_w_down: float32 [1280, 320], replicated
- grad_b_down: float32 [320], replicated
The draws below stay inside these ranges and needn't reach their ends.
Inputs may be any that keep to these rules, and one draw needn't show every extreme that they name: `segment_ids`: along each row the ids start at 0, never fall, and rise by one at each gene boundary; every row holds 4 genes.
All inputs are finite; a program needn't handle non-finite values.
Results may differ from the reference program's by a relative error of at most 0.012.
The reference program's roundings to bfloat16 on the way count: a program that leaves them out, or rounds other values in their place, can miss the bound.
Values may be sent and summed in bfloat16 or wider, within the bound.
No kernel may reach another device: no remote copies, remote signals or barrier semaphores. Data moves between devices by JAX's collectives and lax.ppermute only.
A program may use at most 128 MiB of HBM per device.

```python
import math
import jax
import jax.numpy as jnp
from jax import lax

D = 320
HEADS = 20
HEAD_DIM = 16
FF = 1280
ROWS = 1
CODONS_DEV = 256
GENES = 4
LENGTH = 1024
BATCH = 8


def draw_segment_ids(key, part):
    key = jax.random.fold_in(key, 11)
    score_key, pick_key = jax.random.split(key)
    place = jnp.arange(LENGTH, dtype=jnp.int32)
    scores = jax.random.randint(score_key, (BATCH, LENGTH), 0, 4096, dtype=jnp.int32) * LENGTH + place[None, :]
    chosen = jax.random.randint(pick_key, (BATCH // ROWS, 1), 0, ROWS, dtype=jnp.int32)
    row_place = jnp.arange(ROWS, dtype=jnp.int32)[None, :]
    designated = (row_place == chosen).reshape(BATCH)
    middle = (place >= CODONS_DEV // 2) & (place < LENGTH - CODONS_DEV // 2)
    scores = scores + jnp.where(designated[:, None] & middle[None, :], 2 ** 28, 0).astype(jnp.int32)
    scores = scores + jnp.where(place == 0, 2 ** 29, 0).astype(jnp.int32)[None, :]
    unused, cuts = lax.top_k(-scores, GENES - 1)
    bits = jnp.sum((place[None, None, :] == cuts[:, :, None]).astype(jnp.int32), axis=1)
    return jnp.cumsum(bits, axis=1).astype(jnp.int32)


def steps_of(key, shape, cuts, least, largest):
    level, own = 1.0, jax.random.fold_in(key, 6)
    for position, blocks in cuts:
        heights = jnp.exp(jax.random.uniform(jax.random.fold_in(own, position), (blocks,), jnp.float32, least / len(cuts), largest / len(cuts)))
        level = level * jnp.repeat(heights, shape[position] // blocks).reshape([-1 if axis == position else 1 for axis in range(len(shape))])
    return level


def centred(key, dims, scale, most, shards=(), kind=jnp.bfloat16):
    drawn = scale * jax.random.normal(key, dims, jnp.float32)
    if shards:
        drawn = drawn * steps_of(key, dims, shards, -0.22, 0.18)
    return jnp.clip(drawn, -most, most).astype(kind)


def setup_inputs(seed: int = 0) -> dict:
    arg_keys = jax.random.split(jax.random.key(seed), 16)
    tokens = centred(arg_keys[0], (BATCH, LENGTH, D), 1.0, 6.0, ((0, 8), (1, 4)))
    segment_ids = draw_segment_ids(jax.random.fold_in(arg_keys[15], 71), 0)
    ln1_gain = jnp.clip(1.0 + 0.1 * jax.random.normal(arg_keys[2], (D,), jnp.float32), 0.5, 1.5)
    ln1_bias = centred(arg_keys[3], (D,), 0.5, 3.0, (), jnp.float32)
    w_qkv = centred(arg_keys[4], (D, 3 * D), D ** -0.5, 0.3125)
    b_qkv = centred(arg_keys[5], (3 * D,), 0.5, 3.0, (), jnp.float32)
    w_out = centred(arg_keys[6], (D, D), (D // 16) ** -0.5, 1.25)
    b_out = centred(arg_keys[7], (D,), 0.5, 3.0, (), jnp.float32)
    ln2_gain = jnp.clip(1.0 + 0.1 * jax.random.normal(arg_keys[8], (D,), jnp.float32), 0.5, 1.5)
    ln2_bias = centred(arg_keys[9], (D,), 0.5, 3.0, (), jnp.float32)
    w_up = centred(arg_keys[10], (D, FF), D ** -0.5, 0.3125)
    b_up = centred(arg_keys[11], (FF,), 0.5, 3.0, (), jnp.float32)
    w_down = centred(arg_keys[12], (FF, D), FF ** -0.5, 0.15625)
    b_down = centred(arg_keys[13], (D,), 0.5, 3.0, (), jnp.float32)
    cotangent = centred(arg_keys[14], (BATCH, LENGTH, D), 1.0, 6.0, ((0, 8), (1, 4)))
    return {"tokens": tokens, "segment_ids": segment_ids, "ln1_gain": ln1_gain, "ln1_bias": ln1_bias, "w_qkv": w_qkv, "b_qkv": b_qkv, "w_out": w_out, "b_out": b_out, "ln2_gain": ln2_gain, "ln2_bias": ln2_bias, "w_up": w_up, "b_up": b_up, "w_down": w_down, "b_down": b_down, "cotangent": cotangent}


HIGH = lax.Precision.HIGHEST

@jax.custom_vjp
def low(v):
    return lax.optimization_barrier(v.astype(jnp.bfloat16)).astype(jnp.float32)

@jax.custom_vjp
def low_back(v):
    return v

def low_keep(v):
    return (low(v), None)

def low_pass(kept, grad):
    return (grad,)

def back_keep(v):
    return (v, None)

def back_low(kept, grad):
    return (low(grad),)
low.defvjp(low_keep, low_pass)
low_back.defvjp(back_keep, back_low)

def layer_norm(values, gain, bias):
    centered = values - lax.optimization_barrier(jnp.mean(values, axis=-1, keepdims=True))
    spread = lax.optimization_barrier(jnp.mean(centered * centered, axis=-1, keepdims=True))
    return centered * lax.rsqrt(spread + 1e-05) * gain + bias

def rotate(values, cosine, sine_table):
    half_dim = values.shape[-1] // 2
    first_half = values[..., :half_dim]
    second = values[..., half_dim:]
    return jnp.concatenate([first_half * cosine - second * sine_table, second * cosine + first_half * sine_table], axis=-1)

def angle_tables(positions):
    half_dim = HEAD_DIM // 2
    frequency = jnp.exp(jnp.arange(half_dim, dtype=jnp.float32) * (-2.0 * math.log(10000.0) / HEAD_DIM))
    phase_angle = positions.astype(jnp.float32)[..., None] * frequency
    return (jnp.cos(phase_angle), jnp.sin(phase_angle))

def gene_positions(segments):
    earlier = lax.optimization_barrier(jnp.sum((segments[:, None, :] < segments[:, :, None]).astype(jnp.int32), axis=-1))
    return jnp.arange(segments.shape[-1], dtype=jnp.int32)[None, :] - earlier

def attend(block_item):
    queries, key_heads, value_heads, segments = block_item
    raw_scores = low_back(jnp.einsum('qhd,khd->hqk', queries, key_heads, precision=HIGH))
    same_gene = segments[:, None] == segments[None, :]
    scores = jnp.where(same_gene[None], raw_scores * (1.0 / math.sqrt(HEAD_DIM)), -1e+30)
    softmax_probs = low(jax.nn.softmax(scores, axis=-1))
    return jnp.einsum('hqk,khd->qhd', softmax_probs, value_heads, precision=HIGH)

def forward(inputs, segments, positions, ln1_gain, ln1_bias, w_qkv, b_qkv, w_out, b_out, ln2_gain, ln2_bias, w_up, b_up, w_down, b_down):
    row_count, length_all, features = inputs.shape
    first_norm = low(layer_norm(inputs, ln1_gain, ln1_bias))
    projected = low_back(jnp.dot(first_norm, w_qkv, precision=HIGH) + b_qkv)
    cosine, sine_table = angle_tables(positions)
    cosine = cosine[:, :, None, :]
    sine_table = sine_table[:, :, None, :]
    head_shape = (row_count, length_all, HEADS, HEAD_DIM)
    queries = low_back(low(rotate(projected[..., :features].reshape(head_shape), cosine, sine_table)))
    key_heads = low_back(low(rotate(projected[..., features:2 * features].reshape(head_shape), cosine, sine_table)))
    value_heads = low_back(low(projected[..., 2 * features:].reshape(head_shape)))
    attended = lax.map(jax.checkpoint(attend), (queries, key_heads, value_heads, segments))
    attended = low_back(low(attended.reshape(row_count, length_all, features)))
    branch = low_back(jnp.dot(attended, w_out, precision=HIGH) + b_out)
    middle = inputs + branch
    second_norm = low(layer_norm(middle, ln2_gain, ln2_bias))
    pre_act = low_back(jnp.dot(second_norm, w_up, precision=HIGH) + b_up)
    active = low(jax.nn.gelu(pre_act, approximate=False))
    return middle + jnp.dot(active, w_down, precision=HIGH) + b_down

def reference(tokens, segment_ids, ln1_gain, ln1_bias, w_qkv, b_qkv, w_out, b_out, ln2_gain, ln2_bias, w_up, b_up, w_down, b_down, cotangent):
    params = tuple((entry.astype(jnp.float32) for entry in (ln1_gain, ln1_bias, w_qkv, b_qkv, w_out, b_out, ln2_gain, ln2_bias, w_up, b_up, w_down, b_down)))
    group_size = math.gcd(BATCH, 4)
    group_count = BATCH // group_size
    inputs = tokens.reshape(group_count, group_size, LENGTH, D)
    grads_in = cotangent.reshape(group_count, group_size, LENGTH, D)
    segments = segment_ids.reshape(group_count, group_size, LENGTH)

    def advance(totals, block_item):
        block_in, block_grad, block_seg = block_item
        positions = gene_positions(block_seg)

        def run_layer(values, *weights):
            return forward(values, block_seg, positions, *weights)
        result, pullback = jax.vjp(run_layer, block_in.astype(jnp.float32), *params)
        gradients = pullback(block_grad.astype(jnp.float32))
        totals = tuple((total + grad_piece for total, grad_piece in zip(totals, gradients[1:])))
        return (totals, (result.astype(jnp.bfloat16), gradients[0]))
    zero_grads = tuple((jnp.zeros_like(entry) for entry in params))
    totals, (outputs, input_grads) = lax.scan(advance, zero_grads, (inputs, grads_in, segments))
    return (outputs.reshape(BATCH, LENGTH, D), input_grads.reshape(BATCH, LENGTH, D), totals[0], totals[1], totals[2], totals[3], totals[4], totals[5], totals[6], totals[7], totals[8], totals[9], totals[10], totals[11])
```

```python
import functools
import math

import jax
import jax.numpy as jnp
from jax import lax
from jax.experimental import pallas as pl
from jax.experimental.pallas import tpu as pltpu
from jax.sharding import PartitionSpec as P

HEADS = 20
HEAD_DIM = 16
D = HEADS * HEAD_DIM
FF = 4 * D
GENES = 4
LANES = 128
TILE_HEADS = LANES // HEAD_DIM
DP = 384
BAR = -1e30
EPS = 1e-05
SHARD_ROWS, SHARD_COLS = D // 4, FF // 2
VEC_ROWS = 16
BF = jnp.bfloat16
F32 = jnp.float32
ERF_NUM = (
    -2.72614225801306e-10,
    2.77068142495902e-08,
    -2.10102402082508e-06,
    -5.69250639462346e-05,
    -7.34990630326855e-04,
    -2.95459980854025e-03,
    -1.60960333262415e-02,
)
ERF_DEN = (
    -1.45660718464996e-05,
    -2.13374055278905e-04,
    -1.68282697438203e-03,
    -7.37332916720468e-03,
    -1.42647390514189e-02,
)


def dot(a, b, contract=((1,), (0,))):
    return lax.dot_general(a, b, (contract, ((), ())), preferred_element_type=F32)


def dot_nt(a, b):
    return dot(a, b, ((1,), (1,)))


def dot_tn(a, b):
    return dot(a, b, ((0,), (0,)))


def poly(x, coefficients):
    total = jnp.full_like(x, coefficients[0])
    for entry in coefficients[1:]:
        total = total * x + entry
    return total


def erf(x):
    x = jnp.clip(x, -4.0, 4.0)
    square = x * x
    return x * poly(square, ERF_NUM) / poly(square, ERF_DEN)


def normed(values, axis):
    centered = values - jnp.mean(values, axis=axis, keepdims=True)
    spread = jnp.mean(centered * centered, axis=axis, keepdims=True)
    scale = lax.rsqrt(spread + EPS)
    return centered * scale, scale


def norm_back(grad, normal, scale, gain, axis):
    e = grad * gain
    return scale * (
        e
        - jnp.mean(e, axis=axis, keepdims=True)
        - normal * jnp.mean(e * normal, axis=axis, keepdims=True)
    )


def rotate_rows(values, cosine, sine):
    rows, cols = values.shape
    half = HEAD_DIM // 2
    parts = values.reshape(rows // HEAD_DIM, 2, half, cols)
    first, second = parts[:, 0], parts[:, 1]
    out = jnp.stack([first * cosine - second * sine, second * cosine + first * sine], axis=1)
    return out.reshape(rows, cols)


def pad_rows(values, rows):
    return jnp.concatenate(
        [values, jnp.zeros((rows - values.shape[0], values.shape[1]), values.dtype)], axis=0
    )


def pad_cols(values, cols):
    return jnp.concatenate(
        [values, jnp.zeros((values.shape[0], cols - values.shape[1]), values.dtype)], axis=1
    )


def forward_kernel(
    slot_ref,
    x_ref,
    x0_ref,
    x1_ref,
    x2_ref,
    x3_ref,
    seg_ref,
    cos_ref,
    sin_ref,
    ln1_ref,
    wqkv_t_ref,
    bqkv_ref,
    w_out_ref,
    b_out_ref,
    ln2_gain_ref,
    ln2_bias_ref,
    w_up_ref,
    b_up_ref,
    w_down_ref,
    b_down_ref,
    ct_ref,
    out_ref,
    gmid_ref,
    early_ref,
    vec_ref,
    gw_out_ref,
    xn_ref,
    q_ref,
    qt_ref,
    kt_ref,
    vt_ref,
    ke_ref,
    qe_ref,
    lse_ref,
    inner_ref,
    do_ref,
    dot_ref,
    att_acc,
):
    block = x_ref.shape[0]
    length = 4 * block
    gain, bias = ln1_ref[:, 0:1], ln1_ref[:, 1:2]
    for index, chunk in enumerate((x0_ref, x1_ref, x2_ref, x3_ref)):
        normal, _ = normed(chunk[...].astype(F32), 0)
        xn_ref[:, index * block : (index + 1) * block] = (normal * gain + bias).astype(BF)
    cosine, sine = cos_ref[...], sin_ref[...]
    first = xn_ref[...]
    raw_k = dot(wqkv_t_ref[D : 2 * D, :], first) + bqkv_ref[D : 2 * D, :]
    kt_ref[...] = pad_rows(rotate_rows(raw_k, cosine, sine).astype(BF), DP)
    raw_v = dot(wqkv_t_ref[2 * D :, :], first) + bqkv_ref[2 * D :, :]
    vt_ref[...] = pad_rows(raw_v.astype(BF), DP)
    raw_q = dot(wqkv_t_ref[:D, :], first[:, :block]) + bqkv_ref[:D, :]
    q_t = rotate_rows(raw_q, cosine[:, :block], sine[:, :block]).astype(BF)
    qt_ref[...] = q_t
    q_ref[...] = pad_rows(q_t.astype(F32) * (1.0 / math.sqrt(HEAD_DIM)), DP).T.astype(BF)
    row = lax.broadcasted_iota(jnp.int32, (LANES, length), 0)
    seg = seg_ref[...]
    ke = jnp.where(row < GENES, jnp.where(row == seg, 0.0, BAR), jnp.where(row < GENES + 3, 1.0, 0.0))
    ke_ref[...] = ke.astype(BF)
    qe_ref[...] = jnp.where(row[:, :block] == seg[:, :block], 1.0, 0.0).T.astype(BF)

    lane = lax.broadcasted_iota(jnp.int32, (block, LANES), 1)
    att_acc[...] = jnp.zeros_like(att_acc)
    lse_ref[...] = jnp.zeros_like(lse_ref)
    zero = jnp.zeros((), BF)

    def attend(head, carry):
        start = pl.multiple_of(head // TILE_HEADS * LANES, LANES)
        mask = lane // HEAD_DIM == head % TILE_HEADS
        left = jnp.concatenate(
            [jnp.where(mask, q_ref[:, pl.ds(start, LANES)], zero), qe_ref[...]], axis=1
        )
        right = jnp.concatenate([kt_ref[pl.ds(start, LANES), :], ke_ref[...]], axis=0)
        scores = dot(left, right)
        top = jnp.max(scores, axis=1, keepdims=True)
        weights = jnp.exp(scores - top)
        mass = jnp.sum(weights, axis=1, keepdims=True)
        mixed = dot_nt(weights.astype(BF), vt_ref[pl.ds(start, LANES), :])
        att_acc[:, pl.ds(start, LANES)] += jnp.where(mask, mixed / mass, 0.0)
        lse_ref[...] = jnp.where(lane == head, top + jnp.log(mass), lse_ref[...])
        return carry

    lax.fori_loop(0, HEADS, attend, 0, unroll=4)

    attended_wide = att_acc[:, :D]
    attended = attended_wide.astype(BF)
    middle = x_ref[...].astype(F32) + (dot(attended, w_out_ref[...]) + b_out_ref[...])
    normal2, scale2 = normed(middle, 1)
    gain2 = ln2_gain_ref[...]
    second = (normal2 * gain2 + ln2_bias_ref[...]).astype(BF)
    pre = dot(second, w_up_ref[...]) + b_up_ref[...]
    share = 0.5 + 0.5 * erf(pre * (1.0 / math.sqrt(2.0)))
    active = (pre * share).astype(BF)
    slope = share + pre * (jnp.exp(-0.5 * pre * pre) * (1.0 / math.sqrt(2.0 * math.pi)))
    out_ref[...] = (middle + dot(active, w_down_ref[...]) + b_down_ref[...]).astype(BF)
    ct = ct_ref[...]
    ct_wide = ct.astype(F32)
    grad_pre = (dot_nt(ct, w_down_ref[...]) * slope).astype(BF)
    grad_second = dot_nt(grad_pre, w_up_ref[...])
    grad_middle = ct_wide + norm_back(grad_second, normal2, scale2, gain2, 1)
    gmid_ref[...] = grad_middle
    branch = grad_middle.astype(BF)
    grad_att = dot_nt(branch, w_out_ref[...]).astype(BF)
    grad_att_wide = pad_cols(grad_att.astype(F32), DP)
    do_ref[...] = grad_att_wide.astype(BF)
    dot_ref[...] = grad_att_wide.T[:D, :].astype(BF)
    att_acc[...] = grad_att_wide * att_acc[...]

    inner_ref[...] = jnp.zeros_like(inner_ref)

    def inner_sums(head, carry):
        start = pl.multiple_of(head // TILE_HEADS * LANES, LANES)
        mask = lane // HEAD_DIM == head % TILE_HEADS
        total = jnp.sum(
            jnp.where(mask, att_acc[:, pl.ds(start, LANES)], 0.0), axis=1, keepdims=True
        )
        inner_ref[...] = jnp.where(lane == head, total, inner_ref[...])
        return carry

    lax.fori_loop(0, HEADS, inner_sums, 0, unroll=4)

    slot = slot_ref[0]
    grad_up = dot_tn(second, grad_pre).astype(BF)
    grad_down = dot_tn(ct, active).astype(BF)
    for index in range(8):
        rows = slice(index % 4 * SHARD_ROWS, (index % 4 + 1) * SHARD_ROWS)
        cols = slice(index // 4 * SHARD_COLS, (index // 4 + 1) * SHARD_COLS)
        place = index ^ slot
        early_ref[place, :SHARD_ROWS, :] = grad_up[rows, cols]
        early_ref[place, SHARD_ROWS:, :] = grad_down[rows, cols]
    gw_out_ref[...] = dot_tn(attended, branch)

    def column_sum(values):
        return jnp.sum(values, axis=0, keepdims=True)

    vec_ref[0:1, :] = column_sum(grad_pre.astype(F32))
    vec_ref[1:2, :D] = column_sum(branch.astype(F32))
    vec_ref[2:3, :D] = column_sum(grad_second * normal2)
    vec_ref[3:4, :D] = column_sum(grad_second)
    vec_ref[4:5, :D] = column_sum(ct_wide)


def backward_kernel(
    slot_ref,
    x0_ref,
    x1_ref,
    x2_ref,
    x3_ref,
    cos_ref,
    sin_ref,
    wqkv_ref,
    xn_ref,
    q_ref,
    qt_ref,
    kt_ref,
    vt_ref,
    ke_ref,
    qe_ref,
    lse_ref,
    inner_ref,
    do_ref,
    dot_ref,
    vec_ref,
    gw_out_ref,
    late_ref,
    own_ref,
    far1_ref,
    far2_ref,
    far3_ref,
    dq_acc,
    dk_acc,
    dv_acc,
    rows_ref,
):
    block = q_ref.shape[0]
    length = 4 * block
    lane = lax.broadcasted_iota(jnp.int32, (block, LANES), 1)
    zero = jnp.zeros((), BF)
    dq_acc[...] = jnp.zeros_like(dq_acc)

    def minus(ref, head):
        value = -jnp.sum(jnp.where(lane == head, ref[...], 0.0), axis=1, keepdims=True)
        value = jnp.broadcast_to(value, (block, LANES))
        high = value.astype(BF)
        rest = value - high.astype(F32)
        mid = rest.astype(BF)
        low = (rest - mid.astype(F32)).astype(BF)
        return jnp.where(
            lane == GENES,
            high,
            jnp.where(lane == GENES + 1, mid, jnp.where(lane == GENES + 2, low, zero)),
        )

    def attend(head, carry):
        start = pl.multiple_of(head // TILE_HEADS * LANES, LANES)
        row = pl.multiple_of(head * HEAD_DIM, HEAD_DIM)
        mask = lane // HEAD_DIM == head % TILE_HEADS
        keys = kt_ref[pl.ds(start, LANES), :]
        extra = ke_ref[...]
        left = jnp.concatenate(
            [
                jnp.where(mask, q_ref[:, pl.ds(start, LANES)], zero),
                qe_ref[...] + minus(lse_ref, head),
            ],
            axis=1,
        )
        probs = jnp.exp(dot(left, jnp.concatenate([keys, extra], axis=0)))
        left = jnp.concatenate(
            [jnp.where(mask, do_ref[:, pl.ds(start, LANES)], zero), minus(inner_ref, head)], axis=1
        )
        shifted = dot(left, jnp.concatenate([vt_ref[pl.ds(start, LANES), :], extra], axis=0))
        grad_scores = (probs * shifted).astype(BF)
        dv_acc[pl.ds(row, HEAD_DIM), :] = dot(dot_ref[pl.ds(row, HEAD_DIM), :], probs.astype(BF))
        dk_acc[pl.ds(row, HEAD_DIM), :] = dot(qt_ref[pl.ds(row, HEAD_DIM), :], grad_scores)
        dq_acc[:, pl.ds(start, LANES)] += jnp.where(mask, dot_nt(grad_scores, keys), 0.0)
        return carry

    lax.fori_loop(0, HEADS, attend, 0, unroll=4)

    cosine, sine = cos_ref[...], sin_ref[...]
    scale = 1.0 / math.sqrt(HEAD_DIM)
    dq_t = (dq_acc[...].T[:D, :] * scale).astype(BF).astype(F32)
    grad_q = rotate_rows(dq_t, cosine[:, :block], -sine[:, :block]).astype(BF)
    grad_kv = jnp.concatenate(
        [
            rotate_rows(dk_acc[...] * scale, cosine, -sine).astype(BF),
            dv_acc[...].astype(BF),
        ],
        axis=0,
    )
    grad_first = dot(wqkv_ref[:, D:], grad_kv)
    own = grad_first[:, :block] + dot(wqkv_ref[:, :D], grad_q)
    own_ref[...] = own
    far1_ref[...] = grad_first[:, block : 2 * block].astype(BF)
    far2_ref[...] = grad_first[:, 2 * block : 3 * block].astype(BF)
    far3_ref[...] = grad_first[:, 3 * block :].astype(BF)
    grad_first = jnp.concatenate([own, grad_first[:, block:]], axis=1)
    normal = jnp.concatenate(
        [normed(chunk[...].astype(F32), 0)[0] for chunk in (x0_ref, x1_ref, x2_ref, x3_ref)], axis=1
    )
    ones = jnp.ones((VEC_ROWS, length), BF)
    first = xn_ref[...]
    gw_q = dot_nt(first[:, :block], grad_q)
    gw_kv = dot_nt(first, grad_kv)
    matrix = jnp.concatenate([gw_q, gw_kv, gw_out_ref[...]], axis=1).astype(BF)
    rows_ref[0:1, :] = vec_ref[0:1, :]
    rows_ref[1:2, :] = jnp.concatenate(
        [
            dot_nt(ones[:, :block], grad_q)[0:1],
            dot_nt(ones, grad_kv)[0:1],
            vec_ref[1:2, :D],
        ],
        axis=1,
    )
    rows_ref[2:3, :] = jnp.concatenate(
        [
            dot_nt(ones, (grad_first * normal).astype(BF))[0:1],
            dot_nt(ones, grad_first.astype(BF))[0:1],
            vec_ref[2:3, :D],
            vec_ref[3:4, :D],
        ],
        axis=1,
    )
    rows_ref[3:4, :] = pad_cols(vec_ref[4:5, :D], FF)
    slot = slot_ref[0]
    for index in range(8):
        rows = slice(index % 4 * SHARD_ROWS, (index % 4 + 1) * SHARD_ROWS)
        cols = slice(index // 4 * SHARD_COLS, (index // 4 + 1) * SHARD_COLS)
        place = index ^ slot
        late_ref[place, :SHARD_ROWS, :] = matrix[rows, cols]
        line = rows_ref[index % 4 : index % 4 + 1, cols]
        late_ref[place, SHARD_ROWS:, :] = jnp.broadcast_to(line, (VEC_ROWS, SHARD_COLS)).astype(BF)


def input_kernel(own_ref, near1_ref, near2_ref, near3_ref, x0_ref, ln1_ref, gmid_ref, out_ref):
    grad = (own_ref[...] + near1_ref[...].astype(F32)) + (
        near2_ref[...].astype(F32) + near3_ref[...].astype(F32)
    )
    normal, scale = normed(x0_ref[...].astype(F32), 0)
    back = norm_back(grad, normal, scale, ln1_ref[:, 0:1], 0)
    out_ref[...] = gmid_ref[...] + pad_rows(back, DP).T[:, :D]


def unpack_kernel(
    slot_ref,
    early_ref,
    late_ref,
    g_qkv_ref,
    g_out_ref,
    g_up_ref,
    g_down_ref,
    lines_ref,
    down_t,
    matrix,
):
    slot = slot_ref[0]
    for place in range(8):
        index = place ^ slot
        rows = pl.ds(pl.multiple_of(index % 4 * SHARD_ROWS, 16), SHARD_ROWS)
        cols = pl.ds(pl.multiple_of(index // 4 * SHARD_COLS, LANES), SHARD_COLS)
        early = early_ref[place].astype(F32)
        late = late_ref[place].astype(F32)
        g_up_ref[rows, cols] = early[:SHARD_ROWS]
        down_t[rows, cols] = early[SHARD_ROWS:]
        matrix[rows, cols] = late[:SHARD_ROWS]
        lines_ref[pl.ds(index % 4, 1), cols] = late[SHARD_ROWS : SHARD_ROWS + 1]
    g_down_ref[...] = down_t[...].T[:, :D]
    g_qkv_ref[...] = matrix[:, : 3 * D]
    g_out_ref[...] = matrix[:, 3 * D :]


def call(kernel, name, out_shape, scratch, *operands):
    smem = pl.BlockSpec(memory_space=pltpu.SMEM)
    vmem = pl.BlockSpec(memory_space=pltpu.VMEM)
    return pl.pallas_call(
        kernel,
        name=name,
        out_shape=out_shape,
        in_specs=[
            smem if entry.dtype == jnp.int32 and entry.shape == (1,) else vmem for entry in operands
        ],
        out_specs=jax.tree.map(lambda _: vmem, out_shape),
        scratch_shapes=scratch,
        compiler_params=pltpu.CompilerParams(vmem_limit_bytes=56 << 20),
    )(*operands)


def shape(*dims, dtype=F32):
    return jax.ShapeDtypeStruct(dims, dtype)


def per_device(
    sizes,
    tokens,
    segment_ids,
    ln1_gain,
    ln1_bias,
    w_qkv,
    b_qkv,
    w_out,
    b_out,
    ln2_gain,
    ln2_bias,
    w_up,
    b_up,
    w_down,
    b_down,
    cotangent,
):
    dp_size, seq_size = sizes
    block = tokens.shape[1]
    length = segment_ids.shape[1]
    dp, seq = lax.axis_index("dp"), lax.axis_index("seq")
    count = dp_size * seq_size

    def swap(value, dp_bits, seq_bits):
        pairs = [
            (a * seq_size + b, (a ^ dp_bits) * seq_size + (b ^ seq_bits))
            for a in range(dp_size)
            for b in range(seq_size)
        ]
        return lax.ppermute(value, ("dp", "seq"), pairs)

    core, chip_y, chip_x = seq & 1, seq >> 1, dp & 1
    slot = (core * 4 + chip_y * 2 + chip_x).astype(jnp.int32).reshape(1)

    x = tokens[0]
    x_t = x.T
    near = [swap(x_t, 0, bits) for bits in (1, 2, 3)]

    def by_distance(table):
        table = table.reshape(2, 2, block)
        table = jnp.where(chip_y == 1, table[::-1], table)
        table = jnp.where(core == 1, table[:, ::-1], table)
        return table.reshape(1, length)

    genes = by_distance(segment_ids)
    places = by_distance(jnp.arange(length, dtype=jnp.int32))
    starts = [jnp.sum((segment_ids < gene).astype(jnp.int32)) for gene in range(1, GENES)]
    begin = jnp.zeros_like(genes)
    for gene in range(1, GENES):
        begin = jnp.where(genes == gene, starts[gene - 1], begin)
    half = HEAD_DIM // 2
    frequency = jnp.exp(
        jnp.arange(half, dtype=F32) * (-2.0 * math.log(10000.0) / HEAD_DIM)
    )
    angle = (places - begin).astype(F32) * frequency[:, None]
    cosine, sine = jnp.cos(angle), jnp.sin(angle)
    ln1 = jnp.stack([ln1_gain, ln1_bias], axis=1)

    row = lambda vector: vector.reshape(1, -1)
    (
        output,
        grad_middle,
        early,
        vectors,
        gw_out,
        first,
        q,
        q_t,
        k_t,
        v_t,
        ke,
        qe,
        lse,
        inner,
        d_out,
        d_out_t,
    ) = call(
        forward_kernel,
        "layer_forward",
        (
            shape(block, D, dtype=BF),
            shape(block, D),
            shape(8, 2 * SHARD_ROWS, SHARD_COLS, dtype=BF),
            shape(8, FF),
            shape(D, D),
            shape(D, length, dtype=BF),
            shape(block, DP, dtype=BF),
            shape(D, block, dtype=BF),
            shape(DP, length, dtype=BF),
            shape(DP, length, dtype=BF),
            shape(LANES, length, dtype=BF),
            shape(block, LANES, dtype=BF),
            shape(block, LANES),
            shape(block, LANES),
            shape(block, DP, dtype=BF),
            shape(D, block, dtype=BF),
        ),
        [pltpu.VMEM((block, DP), F32)],
        slot,
        x,
        x_t,
        *near,
        genes,
        cosine,
        sine,
        ln1,
        w_qkv.T,
        b_qkv.reshape(-1, 1),
        w_out,
        row(b_out),
        row(ln2_gain),
        row(ln2_bias),
        w_up,
        row(b_up),
        w_down,
        row(b_down),
        cotangent[0],
    )
    late, own, *far = call(
        backward_kernel,
        "layer_backward",
        (
            shape(8, SHARD_ROWS + VEC_ROWS, SHARD_COLS, dtype=BF),
            shape(D, block),
            shape(D, block, dtype=BF),
            shape(D, block, dtype=BF),
            shape(D, block, dtype=BF),
        ),
        [
            pltpu.VMEM((block, DP), F32),
            pltpu.VMEM((D, length), F32),
            pltpu.VMEM((D, length), F32),
            pltpu.VMEM((8, FF), F32),
        ],
        slot,
        x_t,
        *near,
        cosine,
        sine,
        w_qkv,
        first,
        q,
        q_t,
        k_t,
        v_t,
        ke,
        qe,
        lse,
        inner,
        d_out,
        d_out_t,
        vectors,
        gw_out,
    )
    back = [swap(far[bits - 1], 0, bits) for bits in (1, 2, 3)]
    input_grad = call(
        input_kernel, "input_gradient", shape(block, D), [], own, *back, x_t, ln1, grad_middle
    )

    def add(*terms):
        while len(terms) > 1:
            terms = [
                terms[i].astype(F32) + terms[i + 1].astype(F32) for i in range(0, len(terms), 2)
            ]
        return terms[0].astype(BF)

    part = jnp.concatenate([early, late], axis=1)
    part = add(part[:4], swap(part[4:], 0, 1))
    moves = [(0, 0), (1, 0), (0, 2), (1, 2)]
    part = add(part[0], *[swap(part[i], *moves[i]) for i in (1, 2, 3)])
    bit = 2
    while bit < dp_size:
        part = add(part, swap(part, bit, 0))
        bit *= 2
    part = jnp.stack([part] + [swap(part, *moves[i]) for i in (1, 2, 3)])
    part = jnp.concatenate([part, swap(part, 0, 1)])
    split = early.shape[1]
    g_qkv, g_out, g_up, g_down, lines = call(
        unpack_kernel,
        "unpack",
        (shape(D, 3 * D), shape(D, D), shape(D, FF), shape(FF, D), shape(8, FF)),
        [pltpu.VMEM((DP, FF), F32), pltpu.VMEM((D, FF), F32)],
        slot,
        part[:, :split],
        part[:, split:],
    )
    return (
        output[None],
        input_grad[None],
        lines[2, :D],
        lines[2, D : 2 * D],
        g_qkv,
        lines[1, : 3 * D],
        g_out,
        lines[1, 3 * D :],
        lines[2, 2 * D : 3 * D],
        lines[2, 3 * D :],
        g_up,
        lines[0],
        g_down,
        lines[3, :D],
    )


def solution(mesh):
    split = P("dp", "seq", None)
    whole = P()
    return jax.shard_map(
        functools.partial(per_device, (mesh.shape["dp"], mesh.shape["seq"])),
        mesh=mesh,
        in_specs=(split, P("dp", None)) + (whole,) * 12 + (split,),
        out_specs=(split, split) + (whole,) * 12,
        check_vma=False,
    )
```

```python
import functools
import math

import jax
import jax.numpy as jnp
from jax import lax
from jax.experimental import pallas as pl
from jax.experimental.pallas import tpu as pltpu
from jax.sharding import PartitionSpec as P

HEADS = 20
HEAD_DIM = 16
D = HEADS * HEAD_DIM
FF = 4 * D
GENES = 4
LANES = 128
TILE_HEADS = LANES // HEAD_DIM
DP = 384
BAR = -1e30
EPS = 1e-05
SHARD_ROWS, SHARD_COLS = D // 4, FF // 2
LATE_A, LATE_B, VEC_ROWS = 48, 32, 16
BLOCK_ROWS = SHARD_ROWS + LATE_A
VMEM_BYTES = 32 << 20
BF = jnp.bfloat16
F32 = jnp.float32
ERF_NUM = (
    -2.72614225801306e-10,
    2.77068142495902e-08,
    -2.10102402082508e-06,
    -5.69250639462346e-05,
    -7.34990630326855e-04,
    -2.95459980854025e-03,
    -1.60960333262415e-02,
)
ERF_DEN = (
    -1.45660718464996e-05,
    -2.13374055278905e-04,
    -1.68282697438203e-03,
    -7.37332916720468e-03,
    -1.42647390514189e-02,
)


def dot(a, b, contract=((1,), (0,))):
    return lax.dot_general(a, b, (contract, ((), ())), preferred_element_type=F32)


def dot_nt(a, b):
    return dot(a, b, ((1,), (1,)))


def dot_tn(a, b):
    return dot(a, b, ((0,), (0,)))


def poly(x, coefficients):
    total = jnp.full_like(x, coefficients[0])
    for entry in coefficients[1:]:
        total = total * x + entry
    return total


def erf(x):
    x = jnp.clip(x, -4.0, 4.0)
    square = x * x
    return x * poly(square, ERF_NUM) / poly(square, ERF_DEN)


def normed(values, axis):
    centered = values - jnp.mean(values, axis=axis, keepdims=True)
    spread = jnp.mean(centered * centered, axis=axis, keepdims=True)
    scale = lax.rsqrt(spread + EPS)
    return centered * scale, scale


def norm_back(grad, normal, scale, gain, axis):
    e = grad * gain
    return scale * (
        e
        - jnp.mean(e, axis=axis, keepdims=True)
        - normal * jnp.mean(e * normal, axis=axis, keepdims=True)
    )


def rotate_rows(values, cosine, sine):
    rows, cols = values.shape
    half = HEAD_DIM // 2
    parts = values.reshape(rows // HEAD_DIM, 2, half, cols)
    first, second = parts[:, 0], parts[:, 1]
    out = jnp.stack([first * cosine - second * sine, second * cosine + first * sine], axis=1)
    return out.reshape(rows, cols)


def pad_rows(values, rows):
    return jnp.concatenate(
        [values, jnp.zeros((rows - values.shape[0], values.shape[1]), values.dtype)], axis=0
    )


def pad_cols(values, cols):
    return jnp.concatenate(
        [values, jnp.zeros((values.shape[0], cols - values.shape[1]), values.dtype)], axis=1
    )


def prelude_kernel(
    place_ref,
    x0_ref,
    seg_ref,
    ln1_gain_ref,
    ln1_bias_ref,
    wqkv_ref,
    bqkv_ref,
    wqkv_t_ref,
    cols_ref,
    cos_ref,
    sin_ref,
    xn_ref,
    q_ref,
    qt_ref,
    kt_ref,
    vt_ref,
    ke_ref,
    qe_ref,
):
    block = x0_ref.shape[1]
    length = 4 * block
    seq = place_ref[0]
    genes = seg_ref[...]
    begins = [
        jnp.sum((genes < gene).astype(F32), axis=1, keepdims=True) for gene in range(1, GENES)
    ]
    index = lax.broadcasted_iota(jnp.int32, (1, block), 1).astype(F32)
    half = HEAD_DIM // 2
    step = lax.broadcasted_iota(jnp.int32, (half, block), 0).astype(F32)
    frequency = jnp.exp(step * (-2.0 * math.log(10000.0) / HEAD_DIM))
    row = lax.broadcasted_iota(jnp.int32, (LANES, block), 0)
    for distance in range(4):
        cols = slice(distance * block, (distance + 1) * block)
        chunk = seq ^ distance
        own = seg_ref[:, pl.ds(pl.multiple_of(chunk * block, block), block)]
        begin = jnp.zeros((1, block), F32)
        for gene in range(1, GENES):
            begin = jnp.where(own == gene, begins[gene - 1], begin)
        place = index + (chunk * block).astype(F32) - begin
        angle = place * frequency
        cos_ref[:, cols] = jnp.cos(angle)
        sin_ref[:, cols] = jnp.sin(angle)
        table = jnp.where(
            row < GENES, jnp.where(row == own, 0.0, BAR), jnp.where(row < GENES + 3, 1.0, 0.0)
        )
        ke_ref[:, cols] = table.astype(BF)
        if distance == 0:
            qe_ref[...] = jnp.where(row == own, 1.0, 0.0).T.astype(BF)

    def column(vector):
        return jnp.broadcast_to(vector.reshape(1, -1), (8, vector.shape[0])).T

    wqkv_t_ref[...] = wqkv_ref[...].T
    cols_ref[: 3 * D, :] = column(bqkv_ref[...])
    cols_ref[3 * D : 4 * D, :] = column(ln1_gain_ref[...])
    cols_ref[4 * D :, :] = column(ln1_bias_ref[...])
    normal, _ = normed(x0_ref[...].astype(F32), 0)
    first = (normal * cols_ref[3 * D : 4 * D, 0:1] + cols_ref[4 * D :, 0:1]).astype(BF)
    xn_ref[...] = first
    raw = dot(wqkv_t_ref[...], first) + cols_ref[: 3 * D, 0:1]
    cosine, sine = cos_ref[:, :block], sin_ref[:, :block]
    q_t = rotate_rows(raw[:D], cosine, sine).astype(BF)
    qt_ref[...] = q_t
    q_ref[...] = pad_rows(q_t.astype(F32) * (1.0 / math.sqrt(HEAD_DIM)), DP).T.astype(BF)
    kt_ref[...] = pad_rows(rotate_rows(raw[D : 2 * D], cosine, sine).astype(BF), DP)
    vt_ref[...] = pad_rows(raw[2 * D :].astype(BF), DP)


def forward_kernel(
    slot_ref,
    x0_ref,
    x1_ref,
    x2_ref,
    x3_ref,
    xn0_ref,
    k0_ref,
    v0_ref,
    q_ref,
    ke_ref,
    qe_ref,
    cos_ref,
    sin_ref,
    wqkv_t_ref,
    cols_ref,
    w_out_ref,
    b_out_ref,
    ln2_gain_ref,
    ln2_bias_ref,
    w_up_ref,
    b_up_ref,
    w_down_t_ref,
    b_down_ref,
    ct_t_ref,
    out_ref,
    gmid_ref,
    up_ref,
    down_ref,
    vec_ref,
    gw_out_ref,
    xn_ref,
    kt_ref,
    vt_ref,
    lse_ref,
    inner_ref,
    do_ref,
    dot_ref,
    att_acc,
):
    block = x0_ref.shape[1]
    gain, bias = cols_ref[3 * D : 4 * D, 0:1], cols_ref[4 * D :, 0:1]
    xn_ref[:, :block] = xn0_ref[...]
    for index, chunk in enumerate((x1_ref, x2_ref, x3_ref)):
        normal, _ = normed(chunk[...].astype(F32), 0)
        xn_ref[:, (index + 1) * block : (index + 2) * block] = (normal * gain + bias).astype(BF)
    first = xn_ref[:, block:]
    kt_ref[:, :block] = k0_ref[...]
    vt_ref[:, :block] = v0_ref[...]
    raw = dot(wqkv_t_ref[D:, :], first) + cols_ref[D : 3 * D, 0:1]
    keys = rotate_rows(raw[:D], cos_ref[:, block:], sin_ref[:, block:])
    kt_ref[:, block:] = pad_rows(keys.astype(BF), DP)
    vt_ref[:, block:] = pad_rows(raw[D:].astype(BF), DP)

    lane = lax.broadcasted_iota(jnp.int32, (block, LANES), 1)
    att_acc[...] = jnp.zeros_like(att_acc)
    lse_ref[...] = jnp.zeros_like(lse_ref)
    zero = jnp.zeros((), BF)

    def attend(head, carry):
        start = pl.multiple_of(head // TILE_HEADS * LANES, LANES)
        mask = lane // HEAD_DIM == head % TILE_HEADS
        left = jnp.concatenate(
            [jnp.where(mask, q_ref[:, pl.ds(start, LANES)], zero), qe_ref[...]], axis=1
        )
        right = jnp.concatenate([kt_ref[pl.ds(start, LANES), :], ke_ref[...]], axis=0)
        scores = dot(left, right)
        top = jnp.max(scores, axis=1, keepdims=True)
        weights = jnp.exp(scores - top)
        mass = jnp.sum(weights, axis=1, keepdims=True)
        mixed = dot_nt(weights.astype(BF), vt_ref[pl.ds(start, LANES), :])
        att_acc[:, pl.ds(start, LANES)] += jnp.where(mask, mixed / mass, 0.0)
        lse_ref[...] = jnp.where(lane == head, top + jnp.log(mass), lse_ref[...])
        return carry

    lax.fori_loop(0, HEADS, attend, 0, unroll=4)

    def line(ref):
        return ref[...].reshape(1, -1)

    attended_wide = att_acc[:, :D]
    attended = attended_wide.astype(BF)
    middle = x0_ref[...].T.astype(F32) + (dot(attended, w_out_ref[...]) + line(b_out_ref))
    normal2, scale2 = normed(middle, 1)
    gain2 = line(ln2_gain_ref)
    second = (normal2 * gain2 + line(ln2_bias_ref)).astype(BF)
    pre = dot(second, w_up_ref[...]) + line(b_up_ref)
    share = 0.5 + 0.5 * erf(pre * (1.0 / math.sqrt(2.0)))
    active = (pre * share).astype(BF)
    slope = share + pre * (jnp.exp(-0.5 * pre * pre) * (1.0 / math.sqrt(2.0 * math.pi)))
    output = middle + dot_nt(active, w_down_t_ref[...]) + line(b_down_ref)
    out_ref[...] = output.T.astype(BF)
    ct_t = ct_t_ref[...]
    ct = ct_t.T
    ct_wide = ct.astype(F32)
    grad_pre = (dot(ct, w_down_t_ref[...]) * slope).astype(BF)
    grad_second = dot_nt(grad_pre, w_up_ref[...])
    grad_middle = ct_wide + norm_back(grad_second, normal2, scale2, gain2, 1)
    gmid_ref[...] = grad_middle.T
    branch = grad_middle.astype(BF)
    grad_att = dot_nt(branch, w_out_ref[...]).astype(BF)
    grad_att_wide = pad_cols(grad_att.astype(F32), DP)
    do_ref[...] = grad_att_wide.astype(BF)
    dot_ref[...] = grad_att_wide.T[:D, :].astype(BF)
    att_acc[...] = grad_att_wide * att_acc[...]

    inner_ref[...] = jnp.zeros_like(inner_ref)

    def inner_sums(head, carry):
        start = pl.multiple_of(head // TILE_HEADS * LANES, LANES)
        mask = lane // HEAD_DIM == head % TILE_HEADS
        total = jnp.sum(
            jnp.where(mask, att_acc[:, pl.ds(start, LANES)], 0.0), axis=1, keepdims=True
        )
        inner_ref[...] = jnp.where(lane == head, total, inner_ref[...])
        return carry

    lax.fori_loop(0, HEADS, inner_sums, 0, unroll=4)

    grad_up = dot_tn(second, grad_pre).astype(BF)
    grad_down = dot(ct_t, active).astype(BF)
    for index in range(8):
        rows, cols = shard(index)
        up_ref[index ^ slot_ref[0]] = grad_up[rows, cols]
        down_ref[index ^ slot_ref[1]] = grad_down[rows, cols]
    gw_out_ref[...] = dot_tn(attended, branch)

    def column_sum(values):
        return jnp.sum(values, axis=0, keepdims=True)

    vec_ref[0:1, :] = column_sum(grad_pre.astype(F32))
    vec_ref[1:2, :D] = column_sum(branch.astype(F32))
    vec_ref[2:3, :D] = column_sum(grad_second * normal2)
    vec_ref[3:4, :D] = column_sum(grad_second)
    vec_ref[4:5, :D] = column_sum(ct_wide)


def shard(index):
    row, col = index % 4 * SHARD_ROWS, index // 4 * SHARD_COLS
    return slice(row, row + SHARD_ROWS), slice(col, col + SHARD_COLS)


def backward_kernel(
    slot_ref,
    x0_ref,
    x1_ref,
    x2_ref,
    x3_ref,
    cos_ref,
    sin_ref,
    wqkv_ref,
    xn_ref,
    q_ref,
    qt_ref,
    kt_ref,
    vt_ref,
    ke_ref,
    qe_ref,
    lse_ref,
    inner_ref,
    do_ref,
    dot_ref,
    vec_ref,
    gw_out_ref,
    up_ref,
    down_ref,
    keep_a_ref,
    send_a_ref,
    keep_b_ref,
    send_b_ref,
    own_ref,
    far1_ref,
    far2_ref,
    far3_ref,
    dq_acc,
    dk_acc,
    dv_acc,
    rows_ref,
):
    block = q_ref.shape[0]
    length = 4 * block
    lane = lax.broadcasted_iota(jnp.int32, (block, LANES), 1)
    zero = jnp.zeros((), BF)
    dq_acc[...] = jnp.zeros_like(dq_acc)

    def minus(ref, head):
        value = -jnp.sum(jnp.where(lane == head, ref[...], 0.0), axis=1, keepdims=True)
        value = jnp.broadcast_to(value, (block, LANES))
        high = value.astype(BF)
        rest = value - high.astype(F32)
        mid = rest.astype(BF)
        low = (rest - mid.astype(F32)).astype(BF)
        return jnp.where(
            lane == GENES,
            high,
            jnp.where(lane == GENES + 1, mid, jnp.where(lane == GENES + 2, low, zero)),
        )

    def attend(head, carry):
        start = pl.multiple_of(head // TILE_HEADS * LANES, LANES)
        row = pl.multiple_of(head * HEAD_DIM, HEAD_DIM)
        mask = lane // HEAD_DIM == head % TILE_HEADS
        keys = kt_ref[pl.ds(start, LANES), :]
        extra = ke_ref[...]
        left = jnp.concatenate(
            [
                jnp.where(mask, q_ref[:, pl.ds(start, LANES)], zero),
                qe_ref[...] + minus(lse_ref, head),
            ],
            axis=1,
        )
        probs = jnp.exp(dot(left, jnp.concatenate([keys, extra], axis=0)))
        left = jnp.concatenate(
            [jnp.where(mask, do_ref[:, pl.ds(start, LANES)], zero), minus(inner_ref, head)], axis=1
        )
        shifted = dot(left, jnp.concatenate([vt_ref[pl.ds(start, LANES), :], extra], axis=0))
        grad_scores = (probs * shifted).astype(BF)
        dv_acc[pl.ds(row, HEAD_DIM), :] = dot(dot_ref[pl.ds(row, HEAD_DIM), :], probs.astype(BF))
        dk_acc[pl.ds(row, HEAD_DIM), :] = dot(qt_ref[pl.ds(row, HEAD_DIM), :], grad_scores)
        dq_acc[:, pl.ds(start, LANES)] += jnp.where(mask, dot_nt(grad_scores, keys), 0.0)
        return carry

    lax.fori_loop(0, HEADS, attend, 0, unroll=4)

    cosine, sine = cos_ref[...], sin_ref[...]
    scale = 1.0 / math.sqrt(HEAD_DIM)
    dq_t = (dq_acc[...].T[:D, :] * scale).astype(BF).astype(F32)
    grad_q = rotate_rows(dq_t, cosine[:, :block], -sine[:, :block]).astype(BF)
    grad_kv = jnp.concatenate(
        [
            rotate_rows(dk_acc[...] * scale, cosine, -sine).astype(BF),
            dv_acc[...].astype(BF),
        ],
        axis=0,
    )
    grad_first = dot(wqkv_ref[:, D:], grad_kv)
    own = grad_first[:, :block] + dot(wqkv_ref[:, :D], grad_q)
    own_ref[...] = own
    far1_ref[...] = grad_first[:, block : 2 * block].astype(BF)
    far2_ref[...] = grad_first[:, 2 * block : 3 * block].astype(BF)
    far3_ref[...] = grad_first[:, 3 * block :].astype(BF)
    grad_first = jnp.concatenate([own, grad_first[:, block:]], axis=1)
    normal = jnp.concatenate(
        [normed(chunk[...].astype(F32), 0)[0] for chunk in (x0_ref, x1_ref, x2_ref, x3_ref)], axis=1
    )
    ones = jnp.ones((VEC_ROWS, length), BF)
    first = xn_ref[...]
    gw_q = dot_nt(first[:, :block], grad_q)
    gw_kv = dot_nt(first, grad_kv)
    matrix = jnp.concatenate([gw_q, gw_kv, gw_out_ref[...]], axis=1).astype(BF)
    rows_ref[0:1, :] = vec_ref[0:1, :]
    rows_ref[1:2, :] = jnp.concatenate(
        [
            dot_nt(ones[:, :block], grad_q)[0:1],
            dot_nt(ones, grad_kv)[0:1],
            vec_ref[1:2, :D],
        ],
        axis=1,
    )
    rows_ref[2:3, :] = jnp.concatenate(
        [
            dot_nt(ones, (grad_first * normal).astype(BF))[0:1],
            dot_nt(ones, grad_first.astype(BF))[0:1],
            vec_ref[2:3, :D],
            vec_ref[3:4, :D],
        ],
        axis=1,
    )
    rows_ref[3:4, :] = pad_cols(vec_ref[4:5, :D], FF)
    slot_a, slot_b = slot_ref[0], slot_ref[1]
    for index in range(8):
        rows, cols = shard(index)
        piece = matrix[rows, cols]
        line = rows_ref[index % 4 : index % 4 + 1, cols]
        lines = jnp.broadcast_to(line, (VEC_ROWS, SHARD_COLS)).astype(BF)

        def store_a(ref, place):
            ref[place, :SHARD_ROWS] = up_ref[index ^ slot_a]
            ref[place, SHARD_ROWS:] = piece[:LATE_A]

        def store_b(ref, place):
            ref[place, :SHARD_ROWS] = down_ref[index ^ slot_b]
            ref[place, SHARD_ROWS : SHARD_ROWS + LATE_B] = piece[LATE_A:]
            ref[place, SHARD_ROWS + LATE_B :] = lines

        place_a, place_b = index ^ slot_a, index ^ slot_b
        stays = index // 4 == slot_a // 4

        @pl.when(stays)
        def _():
            store_a(keep_a_ref, place_a)
            store_b(keep_b_ref, place_b)

        @pl.when(jnp.logical_not(stays))
        def _():
            store_a(send_a_ref, place_a - 4)
            store_b(send_b_ref, place_b - 4)


def input_kernel(own_ref, near1_ref, near2_ref, near3_ref, x0_ref, cols_ref, gmid_ref, out_ref):
    grad = (own_ref[...] + near1_ref[...].astype(F32)) + (
        near2_ref[...].astype(F32) + near3_ref[...].astype(F32)
    )
    normal, scale = normed(x0_ref[...].astype(F32), 0)
    out_ref[...] = gmid_ref[...] + norm_back(grad, normal, scale, cols_ref[3 * D : 4 * D, 0:1], 0)


def unpack_kernel(slot_ref, *refs):
    blocks_a, blocks_b = refs[:8], refs[8:16]
    g_up_ref, g_down_t_ref, g_qkv_ref, g_out_ref, *vector_refs = refs[16:-2]
    matrix, lines = refs[-2:]
    slot_a, slot_b = slot_ref[0], slot_ref[1]

    def spot(index):
        rows = pl.multiple_of(index % 4 * SHARD_ROWS, 16)
        return rows, pl.ds(pl.multiple_of(index // 4 * SHARD_COLS, LANES), SHARD_COLS)

    for place in range(8):
        rows, cols = spot(place ^ slot_a)
        values = blocks_a[place][...].astype(F32)
        g_up_ref[pl.ds(rows, SHARD_ROWS), cols] = values[:SHARD_ROWS]
        matrix[pl.ds(rows, LATE_A), cols] = values[SHARD_ROWS:]
        index = place ^ slot_b
        rows, cols = spot(index)
        values = blocks_b[place][...].astype(F32)
        g_down_t_ref[pl.ds(rows, SHARD_ROWS), cols] = values[:SHARD_ROWS]
        late = SHARD_ROWS + LATE_B
        matrix[pl.ds(rows + LATE_A, LATE_B), cols] = values[SHARD_ROWS:late]
        lines[pl.ds(index % 4, 1), cols] = values[late : late + 1]
    g_qkv_ref[...] = matrix[:, : 3 * D]
    g_out_ref[...] = matrix[:, 3 * D :]
    places = [
        (2, 0, D),
        (2, D, D),
        (1, 0, 3 * D),
        (1, 3 * D, D),
        (2, 2 * D, D),
        (2, 3 * D, D),
        (0, 0, FF),
        (3, 0, D),
    ]
    for ref, (row, start, size) in zip(vector_refs, places):
        ref[...] = lines[row : row + 1, start : start + size].reshape(size)


def call(kernel, name, out_shape, scratch, *operands):
    smem = pl.BlockSpec(memory_space=pltpu.SMEM)
    vmem = pl.BlockSpec(memory_space=pltpu.VMEM)
    return pl.pallas_call(
        kernel,
        name=name,
        out_shape=out_shape,
        in_specs=[smem if entry.shape == (2,) else vmem for entry in operands],
        out_specs=jax.tree.map(lambda _: vmem, out_shape),
        scratch_shapes=scratch,
        compiler_params=pltpu.CompilerParams(vmem_limit_bytes=VMEM_BYTES),
    )(*operands)


def shape(*dims, dtype=F32):
    return jax.ShapeDtypeStruct(dims, dtype)


def per_device(
    sizes,
    tokens,
    segment_ids,
    ln1_gain,
    ln1_bias,
    w_qkv,
    b_qkv,
    w_out,
    b_out,
    ln2_gain,
    ln2_bias,
    w_up,
    b_up,
    w_down,
    b_down,
    cotangent,
):
    dp_size, seq_size = sizes
    block = tokens.shape[1]
    length = segment_ids.shape[1]
    dp, seq = lax.axis_index("dp"), lax.axis_index("seq")

    def swap(value, dp_bits, seq_bits):
        pairs = [
            (a * seq_size + b, (a ^ dp_bits) * seq_size + (b ^ seq_bits))
            for a in range(dp_size)
            for b in range(seq_size)
        ]
        return lax.ppermute(value, ("dp", "seq"), pairs)

    core, chip_y, chip_x = seq & 1, seq >> 1, dp & 1
    slots = jnp.stack([core * 4 + chip_x * 2 + chip_y, core * 4 + chip_y * 2 + chip_x])
    slots = slots.astype(jnp.int32)
    places = jnp.stack([seq, dp]).astype(jnp.int32)

    x_t = tokens[0].T
    near = [swap(x_t, 0, bits) for bits in (2, 3, 1)]
    near = [near[2], near[0], near[1]]

    wqkv_t, cols, cosine, sine, first, q, q_t, k_t, v_t, ke, qe = call(
        prelude_kernel,
        "prelude",
        (
            shape(3 * D, D, dtype=BF),
            shape(5 * D, 8),
            shape(HEAD_DIM // 2, length),
            shape(HEAD_DIM // 2, length),
            shape(D, block, dtype=BF),
            shape(block, DP, dtype=BF),
            shape(D, block, dtype=BF),
            shape(DP, block, dtype=BF),
            shape(DP, block, dtype=BF),
            shape(LANES, length, dtype=BF),
            shape(block, LANES, dtype=BF),
        ),
        [],
        places,
        x_t,
        segment_ids,
        ln1_gain,
        ln1_bias,
        w_qkv,
        b_qkv,
    )
    (
        output,
        grad_middle,
        early_up,
        early_down,
        vectors,
        gw_out,
        first,
        k_t,
        v_t,
        lse,
        inner,
        d_out,
        d_out_t,
    ) = call(
        forward_kernel,
        "layer_forward",
        (
            shape(D, block, dtype=BF),
            shape(D, block),
            shape(8, SHARD_ROWS, SHARD_COLS, dtype=BF),
            shape(8, SHARD_ROWS, SHARD_COLS, dtype=BF),
            shape(8, FF),
            shape(D, D),
            shape(D, length, dtype=BF),
            shape(DP, length, dtype=BF),
            shape(DP, length, dtype=BF),
            shape(block, LANES),
            shape(block, LANES),
            shape(block, DP, dtype=BF),
            shape(D, block, dtype=BF),
        ),
        [pltpu.VMEM((block, DP), F32)],
        slots,
        x_t,
        *near,
        first,
        k_t,
        v_t,
        q,
        ke,
        qe,
        cosine,
        sine,
        wqkv_t,
        cols,
        w_out,
        b_out,
        ln2_gain,
        ln2_bias,
        w_up,
        b_up,
        w_down.T,
        b_down,
        cotangent[0].T,
    )
    blocks = shape(4, BLOCK_ROWS, SHARD_COLS, dtype=BF)
    keep_a, send_a, keep_b, send_b, own, *far = call(
        backward_kernel,
        "layer_backward",
        (
            blocks,
            blocks,
            blocks,
            blocks,
            shape(D, block),
            shape(D, block, dtype=BF),
            shape(D, block, dtype=BF),
            shape(D, block, dtype=BF),
        ),
        [
            pltpu.VMEM((block, DP), F32),
            pltpu.VMEM((D, length), F32),
            pltpu.VMEM((D, length), F32),
            pltpu.VMEM((8, FF), F32),
        ],
        slots,
        x_t,
        *near,
        cosine,
        sine,
        w_qkv,
        first,
        q,
        q_t,
        k_t,
        v_t,
        ke,
        qe,
        lse,
        inner,
        d_out,
        d_out_t,
        vectors,
        gw_out,
        early_up,
        early_down,
    )

    def add(first_term, second_term):
        return (first_term.astype(F32) + second_term.astype(F32)).astype(BF)

    move_core, move_x, move_y = (0, 1), (1, 0), (0, 2)
    got_a, got_b = swap(send_a, *move_core), swap(send_b, *move_core)
    keep_a, send_a = add(keep_a[:2], got_a[:2]), add(keep_a[2:], got_a[2:])
    keep_b, send_b = add(keep_b[:2], got_b[:2]), add(keep_b[2:], got_b[2:])
    got_a, got_b = swap(send_a, *move_x), swap(send_b, *move_y)
    keep_a, send_a = add(keep_a[0], got_a[0]), add(keep_a[1], got_a[1])
    keep_b, send_b = add(keep_b[0], got_b[0]), add(keep_b[1], got_b[1])
    got_a, got_b = swap(send_a, *move_y), swap(send_b, *move_x)
    part_a, part_b = add(keep_a, got_a), add(keep_b, got_b)
    if dp_size > 2:
        odd = (dp >> 1) & 1 == 1
        kept = jnp.where(odd, part_b, part_a)
        kept = add(kept, swap(jnp.where(odd, part_a, part_b), 2, 0))
        bit = 4
        while bit < dp_size:
            kept = add(kept, swap(kept, bit, 0))
            bit *= 2
        other = swap(kept, 2, 0)
        part_a, part_b = jnp.where(odd, other, kept), jnp.where(odd, kept, other)

    def spread(part, inner_move, outer_move):
        inner_block = swap(part, *inner_move)
        blocks = [part, inner_block, swap(part, *outer_move), swap(inner_block, *outer_move)]
        return blocks + [swap(entry, *move_core) for entry in blocks]

    blocks_a = spread(part_a, move_y, move_x)
    blocks_b = spread(part_b, move_x, move_y)
    back = [swap(far[bits - 1], 0, bits) for bits in (1, 2, 3)]
    input_grad = call(
        input_kernel, "input_gradient", shape(D, block), [], own, *back, x_t, cols, grad_middle
    )
    g_up, g_down_t, g_qkv, g_out, *vectors = call(
        unpack_kernel,
        "unpack",
        (
            shape(D, FF),
            shape(D, FF),
            shape(D, 3 * D),
            shape(D, D),
            shape(D),
            shape(D),
            shape(3 * D),
            shape(D),
            shape(D),
            shape(D),
            shape(FF),
            shape(D),
        ),
        [pltpu.VMEM((D, FF), F32), pltpu.VMEM((8, FF), F32)],
        slots,
        *blocks_a,
        *blocks_b,
    )
    g_ln1_gain, g_ln1_bias, g_bqkv, g_bout, g_ln2_gain, g_ln2_bias, g_bup, g_bdown = vectors
    return (
        output.T[None],
        input_grad.T[None],
        g_ln1_gain,
        g_ln1_bias,
        g_qkv,
        g_bqkv,
        g_out,
        g_bout,
        g_ln2_gain,
        g_ln2_bias,
        g_up,
        g_bup,
        g_down_t.T,
        g_bdown,
    )


def solution(mesh):
    split = P("dp", "seq", None)
    whole = P()
    return jax.shard_map(
        functools.partial(per_device, (mesh.shape["dp"], mesh.shape["seq"])),
        mesh=mesh,
        in_specs=(split, P("dp", None)) + (whole,) * 12 + (split,),
        out_specs=(split, split) + (whole,) * 12,
        check_vma=False,
    )
```

```python
import functools
import math

import jax
import jax.numpy as jnp
from jax import lax
from jax.experimental import pallas as pl
from jax.experimental.pallas import tpu as pltpu
from jax.sharding import PartitionSpec as P

HEADS = 20
HEAD_DIM = 16
D = HEADS * HEAD_DIM
FF = 4 * D
GENES = 4
LANES = 128
TILE_HEADS = LANES // HEAD_DIM
DP = 384
BAR = -1e30
EPS = 1e-05
SHARD_ROWS, SHARD_COLS, EXTRA_ROWS = D // 4, FF // 2, 16
EARLY_ROWS = SHARD_ROWS + EXTRA_ROWS
LATE_ROWS, LATE_COLS = D // 8, 8 * LANES
SPARE = LATE_COLS - 3 * D
OUT_BLOCKS = D // (2 * EXTRA_ROWS)
PIECE_HEADS = 4
PIECE_ROWS = PIECE_HEADS * HEAD_DIM
MIB = 1 << 20
BF = jnp.bfloat16
F32 = jnp.float32
ERF_NUM = (
    -2.72614225801306e-10,
    2.77068142495902e-08,
    -2.10102402082508e-06,
    -5.69250639462346e-05,
    -7.34990630326855e-04,
    -2.95459980854025e-03,
    -1.60960333262415e-02,
)
ERF_DEN = (
    -1.45660718464996e-05,
    -2.13374055278905e-04,
    -1.68282697438203e-03,
    -7.37332916720468e-03,
    -1.42647390514189e-02,
)


def dot(a, b, contract=((1,), (0,))):
    return lax.dot_general(a, b, (contract, ((), ())), preferred_element_type=F32)


def dot_nt(a, b):
    return dot(a, b, ((1,), (1,)))


def dot_tn(a, b):
    return dot(a, b, ((0,), (0,)))


def poly(x, coefficients):
    total = jnp.full_like(x, coefficients[0])
    for entry in coefficients[1:]:
        total = total * x + entry
    return total


def erf(x):
    x = jnp.clip(x, -4.0, 4.0)
    square = x * x
    return x * poly(square, ERF_NUM) / poly(square, ERF_DEN)


def normed(values, axis):
    centered = values - jnp.mean(values, axis=axis, keepdims=True)
    spread = jnp.mean(centered * centered, axis=axis, keepdims=True)
    scale = lax.rsqrt(spread + EPS)
    return centered * scale, scale


def norm_back(grad, normal, scale, gain, axis):
    e = grad * gain
    return scale * (
        e
        - jnp.mean(e, axis=axis, keepdims=True)
        - normal * jnp.mean(e * normal, axis=axis, keepdims=True)
    )


def rotate_rows(values, cosine, sine):
    rows, cols = values.shape
    half = HEAD_DIM // 2
    parts = values.reshape(rows // HEAD_DIM, 2, half, cols)
    first, second = parts[:, 0], parts[:, 1]
    out = jnp.stack([first * cosine - second * sine, second * cosine + first * sine], axis=1)
    return out.reshape(rows, cols)


def pad_rows(values, rows):
    return jnp.concatenate(
        [values, jnp.zeros((rows - values.shape[0], values.shape[1]), values.dtype)], axis=0
    )


def pad_cols(values, cols):
    return jnp.concatenate(
        [values, jnp.zeros((values.shape[0], cols - values.shape[1]), values.dtype)], axis=1
    )


def slots():
    dp, seq = lax.axis_index("dp"), lax.axis_index("seq")
    core, chip_y, chip_x = seq & 1, seq >> 1, dp & 1
    return core * 4 + chip_x * 2 + chip_y, core * 4 + chip_y * 2 + chip_x, (dp >> 1) & 1, seq


def load_all(sources, targets, sems):
    copies = [
        pltpu.make_async_copy(source, target, sems.at[i])
        for i, (source, target) in enumerate(zip(sources, targets))
    ]
    for copy in copies:
        copy.start()
    return copies


def column(vector):
    return jnp.broadcast_to(vector.reshape(1, -1), (8, vector.shape[0])).T


def prelude_kernel(*refs):
    sources, outs, (local, sems) = refs[:15], refs[15:-6], (refs[-6:-1], refs[-1])
    kept, made = outs[:10], outs[10:]
    copies = load_all(sources, (kept[0], *local, *kept[1:]), sems)
    for copy in copies[:6]:
        copy.wait()
    prelude_body(kept[0], *local, *made)
    for copy in copies[6:]:
        copy.wait()


def prelude_body(
    x0_ref,
    seg_ref,
    ln1_gain_ref,
    ln1_bias_ref,
    wqkv_ref,
    bqkv_ref,
    wqkv_t_ref,
    cols_ref,
    cos_ref,
    sin_ref,
    q_ref,
    qt_ref,
    kt_ref,
    vt_ref,
    ke_ref,
    qe_ref,
):
    block = x0_ref.shape[1]
    length = 4 * block
    seq = slots()[3]
    genes = seg_ref[...]
    begins = [
        jnp.sum((genes < gene).astype(F32), axis=1, keepdims=True) for gene in range(1, GENES)
    ]
    index = lax.broadcasted_iota(jnp.int32, (1, block), 1).astype(F32)
    half = HEAD_DIM // 2
    step = lax.broadcasted_iota(jnp.int32, (half, block), 0).astype(F32)
    frequency = jnp.exp(step * (-2.0 * math.log(10000.0) / HEAD_DIM))
    row = lax.broadcasted_iota(jnp.int32, (LANES, block), 0)
    for distance in range(4):
        cols = slice(distance * block, (distance + 1) * block)
        chunk = seq ^ distance
        own = seg_ref[:, pl.ds(pl.multiple_of(chunk * block, block), block)]
        begin = jnp.zeros((1, block), F32)
        for gene in range(1, GENES):
            begin = jnp.where(own == gene, begins[gene - 1], begin)
        place = index + (chunk * block).astype(F32) - begin
        angle = place * frequency
        cos_ref[:, cols] = jnp.cos(angle)
        sin_ref[:, cols] = jnp.sin(angle)
        table = jnp.where(
            row < GENES, jnp.where(row == own, 0.0, BAR), jnp.where(row < GENES + 3, 1.0, 0.0)
        )
        ke_ref[:, cols] = table.astype(BF)
        if distance == 0:
            qe_ref[...] = jnp.where(row == own, 1.0, 0.0).T.astype(BF)

    wqkv_t_ref[...] = wqkv_ref[...].T
    cols_ref[: 3 * D, :] = column(bqkv_ref[...])
    cols_ref[3 * D : 4 * D, :] = column(ln1_gain_ref[...])
    cols_ref[4 * D :, :] = column(ln1_bias_ref[...])
    normal, _ = normed(x0_ref[...].astype(F32), 0)
    first = (normal * cols_ref[3 * D : 4 * D, 0:1] + cols_ref[4 * D :, 0:1]).astype(BF)
    raw = dot(wqkv_t_ref[...], first) + cols_ref[: 3 * D, 0:1]
    cosine, sine = cos_ref[:, :block], sin_ref[:, :block]
    q_t = rotate_rows(raw[:D], cosine, sine).astype(BF)
    qt_ref[...] = q_t
    q_ref[...] = pad_rows(q_t.astype(F32) * (1.0 / math.sqrt(HEAD_DIM)), DP).T.astype(BF)
    kt_ref[...] = pad_rows(rotate_rows(raw[D : 2 * D], cosine, sine).astype(BF), DP)
    vt_ref[...] = pad_rows(raw[2 * D :].astype(BF), DP)


def forward_kernel(
    x0_ref,
    x1_ref,
    x2_ref,
    x3_ref,
    k0_ref,
    v0_ref,
    q_ref,
    ke_ref,
    qe_ref,
    cos_ref,
    sin_ref,
    wqkv_t_ref,
    cols_ref,
    w_out_ref,
    b_out_ref,
    ln2_gain_ref,
    ln2_bias_ref,
    w_up_ref,
    b_up_ref,
    w_down_t_ref,
    b_down_ref,
    ct_t_ref,
    out_ref,
    gmid_ref,
    keep_ref,
    send_ref,
    kt_ref,
    vt_ref,
    lse_ref,
    inner_ref,
    do_ref,
    dot_ref,
    x_all_hbm,
    att_acc,
    xn_ref,
    sems,
):
    block = x0_ref.shape[1]
    chunks = (x0_ref, x1_ref, x2_ref, x3_ref)
    copies = load_all(chunks, [x_all_hbm.at[i] for i in range(4)], sems)
    gain, bias = cols_ref[3 * D : 4 * D, 0:1], cols_ref[4 * D :, 0:1]
    for index, chunk in enumerate((x1_ref, x2_ref, x3_ref)):
        normal, _ = normed(chunk[...].astype(F32), 0)
        xn_ref[:, index * block : (index + 1) * block] = (normal * gain + bias).astype(BF)
    first = xn_ref[...]
    kt_ref[:, :block] = k0_ref[...]
    vt_ref[:, :block] = v0_ref[...]
    raw = dot(wqkv_t_ref[D:, :], first) + cols_ref[D : 3 * D, 0:1]
    keys = rotate_rows(raw[:D], cos_ref[:, block:], sin_ref[:, block:])
    kt_ref[:, block:] = pad_rows(keys.astype(BF), DP)
    vt_ref[:, block:] = pad_rows(raw[D:].astype(BF), DP)

    lane = lax.broadcasted_iota(jnp.int32, (block, LANES), 1)
    att_acc[...] = jnp.zeros_like(att_acc)
    lse_ref[...] = jnp.zeros_like(lse_ref)
    zero = jnp.zeros((), BF)

    def attend(head, carry):
        start = pl.multiple_of(head // TILE_HEADS * LANES, LANES)
        mask = lane // HEAD_DIM == head % TILE_HEADS
        left = jnp.concatenate(
            [jnp.where(mask, q_ref[:, pl.ds(start, LANES)], zero), qe_ref[...]], axis=1
        )
        right = jnp.concatenate([kt_ref[pl.ds(start, LANES), :], ke_ref[...]], axis=0)
        scores = dot(left, right)
        top = jnp.max(scores, axis=1, keepdims=True)
        weights = jnp.exp(scores - top)
        mass = jnp.sum(weights, axis=1, keepdims=True)
        mixed = dot_nt(weights.astype(BF), vt_ref[pl.ds(start, LANES), :])
        att_acc[:, pl.ds(start, LANES)] += jnp.where(mask, mixed / mass, 0.0)
        lse_ref[...] = jnp.where(lane == head, top + jnp.log(mass), lse_ref[...])
        return carry

    lax.fori_loop(0, HEADS, attend, 0, unroll=4)

    def line(ref):
        return ref[...].reshape(1, -1)

    attended_wide = att_acc[:, :D]
    attended = attended_wide.astype(BF)
    middle = x0_ref[...].T.astype(F32) + (dot(attended, w_out_ref[...]) + line(b_out_ref))
    normal2, scale2 = normed(middle, 1)
    gain2 = line(ln2_gain_ref)
    second = (normal2 * gain2 + line(ln2_bias_ref)).astype(BF)
    pre = dot(second, w_up_ref[...]) + line(b_up_ref)
    share = 0.5 + 0.5 * erf(pre * (1.0 / math.sqrt(2.0)))
    active = (pre * share).astype(BF)
    slope = share + pre * (jnp.exp(-0.5 * pre * pre) * (1.0 / math.sqrt(2.0 * math.pi)))
    output = middle + dot_nt(active, w_down_t_ref[...]) + line(b_down_ref)
    out_ref[...] = output.T.astype(BF)
    ct_t = ct_t_ref[...]
    ct = ct_t.T
    ct_wide = ct.astype(F32)
    grad_pre = (dot(ct, w_down_t_ref[...]) * slope).astype(BF)
    grad_second = dot_nt(grad_pre, w_up_ref[...])
    grad_middle = ct_wide + norm_back(grad_second, normal2, scale2, gain2, 1)
    gmid_ref[...] = grad_middle.T
    branch = grad_middle.astype(BF)
    grad_att = dot_nt(branch, w_out_ref[...]).astype(BF)
    grad_att_wide = pad_cols(grad_att.astype(F32), DP)
    do_ref[...] = grad_att_wide.astype(BF)
    dot_ref[...] = grad_att_wide.T[:D, :].astype(BF)
    att_acc[...] = grad_att_wide * att_acc[...]

    inner_ref[...] = jnp.zeros_like(inner_ref)

    def inner_sums(head, carry):
        start = pl.multiple_of(head // TILE_HEADS * LANES, LANES)
        mask = lane // HEAD_DIM == head % TILE_HEADS
        total = jnp.sum(
            jnp.where(mask, att_acc[:, pl.ds(start, LANES)], 0.0), axis=1, keepdims=True
        )
        inner_ref[...] = jnp.where(lane == head, total, inner_ref[...])
        return carry

    lax.fori_loop(0, HEADS, inner_sums, 0, unroll=4)

    grad_up = dot_tn(second, grad_pre).astype(BF)
    grad_down = dot(ct_t, active).astype(BF)
    grad_out = dot_tn(attended, branch)

    def column_sum(values):
        return jnp.sum(values, axis=0, keepdims=True)

    lines = column_sum(grad_pre.astype(F32))
    lines = [
        lines[:, :SHARD_COLS],
        lines[:, SHARD_COLS:],
        jnp.concatenate([column_sum(branch.astype(F32)), column_sum(grad_second * normal2)], axis=1),
        jnp.concatenate([column_sum(grad_second), column_sum(ct_wide)], axis=1),
    ]

    def extra(index):
        if index < OUT_BLOCKS:
            row = 2 * EXTRA_ROWS * index
            upper = grad_out[row : row + EXTRA_ROWS]
            lower = grad_out[row + EXTRA_ROWS : row + 2 * EXTRA_ROWS]
            return jnp.concatenate([upper, lower], axis=1).astype(BF)
        if index < OUT_BLOCKS + len(lines):
            line = lines[index - OUT_BLOCKS]
            return jnp.broadcast_to(line, (EXTRA_ROWS, SHARD_COLS)).astype(BF)
        return jnp.zeros((EXTRA_ROWS, SHARD_COLS), BF)

    own_slots = slots()
    for index in range(8):
        rows, cols = shard(index)
        stays = index // 4 == own_slots[0] // 4
        for array, values in enumerate((grad_up, grad_down)):
            block_values = jnp.concatenate([values[rows, cols], extra(8 * array + index)], axis=0)
            place = (index ^ own_slots[array]) % 4
            store_block(keep_ref, send_ref, stays, (array, place), block_values)
    for copy in copies:
        copy.wait()


def store_block(keep_ref, send_ref, stays, place, values):
    @pl.when(stays)
    def _():
        keep_ref[place] = values

    @pl.when(jnp.logical_not(stays))
    def _():
        send_ref[place] = values


def shard(index):
    row, col = index % 4 * SHARD_ROWS, index // 4 * SHARD_COLS
    return slice(row, row + SHARD_ROWS), slice(col, col + SHARD_COLS)


def piece_kernel(
    piece,
    after_ref,
    cos_ref,
    sin_ref,
    q_ref,
    qt_ref,
    kt_ref,
    vt_ref,
    ke_ref,
    qe_ref,
    lse_ref,
    inner_ref,
    do_ref,
    dot_ref,
    *refs,
):
    gq_ref, gk_ref, gv_ref, dk_acc, dv_acc = refs[-5:]
    block = q_ref.shape[0]
    lane = lax.broadcasted_iota(jnp.int32, (block, LANES), 1)
    zero = jnp.zeros((), BF)
    heads = range(piece * PIECE_HEADS, (piece + 1) * PIECE_HEADS)
    start = heads[0] // TILE_HEADS * LANES
    tile = slice(start, start + LANES)
    keys, extra = kt_ref[tile, :], ke_ref[...]
    key_side = jnp.concatenate([keys, extra], axis=0)
    value_side = jnp.concatenate([vt_ref[tile, :], extra], axis=0)

    def minus(ref, head):
        value = jnp.broadcast_to(-ref[:, head : head + 1], (block, LANES))
        high = value.astype(BF)
        rest = value - high.astype(F32)
        mid = rest.astype(BF)
        low = (rest - mid.astype(F32)).astype(BF)
        return jnp.where(
            lane == GENES,
            high,
            jnp.where(lane == GENES + 1, mid, jnp.where(lane == GENES + 2, low, zero)),
        )

    grad_queries = jnp.zeros((block, LANES), F32)
    for index, head in enumerate(heads):
        rows = slice(head * HEAD_DIM, (head + 1) * HEAD_DIM)
        here = slice(index * HEAD_DIM, (index + 1) * HEAD_DIM)
        mask = lane // HEAD_DIM == head % TILE_HEADS
        left = jnp.concatenate(
            [jnp.where(mask, q_ref[:, tile], zero), qe_ref[...] + minus(lse_ref, head)], axis=1
        )
        probs = jnp.exp(dot(left, key_side))
        left = jnp.concatenate(
            [jnp.where(mask, do_ref[:, tile], zero), minus(inner_ref, head)], axis=1
        )
        grad_scores = (probs * dot(left, value_side)).astype(BF)
        dv_acc[here, :] = dot(dot_ref[rows, :], probs.astype(BF))
        dk_acc[here, :] = dot(qt_ref[rows, :], grad_scores)
        grad_queries += jnp.where(mask, dot_nt(grad_scores, keys), 0.0)

    cosine, sine = cos_ref[...], sin_ref[...]
    scale = 1.0 / math.sqrt(HEAD_DIM)
    first = heads[0] % TILE_HEADS * HEAD_DIM
    dq_t = (grad_queries.T[first : first + PIECE_ROWS, :] * scale).astype(BF).astype(F32)
    rows = slice(piece * PIECE_ROWS, (piece + 1) * PIECE_ROWS)
    gq_ref[rows, :] = rotate_rows(dq_t, cosine[:, :block], -sine[:, :block]).astype(BF)
    gk_ref[rows, :] = rotate_rows(dk_acc[...] * scale, cosine, -sine).astype(BF)
    gv_ref[rows, :] = dv_acc[...].astype(BF)


def projection_kernel(
    gq_ref,
    gk_ref,
    gv_ref,
    x_hbm,
    wqkv_hbm,
    ln1_gain_hbm,
    ln1_bias_hbm,
    keep_ref,
    send_ref,
    own_ref,
    far_ref,
    x_ref,
    wqkv_ref,
    ln1_gain_ref,
    ln1_bias_ref,
    matrix,
    sems,
):
    copies = load_all(
        (wqkv_hbm, x_hbm, ln1_gain_hbm, ln1_bias_hbm),
        (wqkv_ref, x_ref, ln1_gain_ref, ln1_bias_ref),
        sems,
    )
    block = x_ref.shape[2]
    length = 4 * block
    ones = jnp.ones((16, length), BF)
    grad_q, grad_k, grad_v = gq_ref[...], gk_ref[...], gv_ref[...]
    sums = [
        dot_nt(ones[:, :block], grad_q)[0:1],
        dot_nt(ones, grad_k)[0:1],
        dot_nt(ones, grad_v)[0:1],
    ]
    for copy in copies:
        copy.wait()
    gain, bias = column(ln1_gain_ref[...])[:, 0:1], column(ln1_bias_ref[...])[:, 0:1]
    normal = jnp.concatenate([normed(x_ref[i].astype(F32), 0)[0] for i in range(4)], axis=1)
    first = (normal * gain + bias).astype(BF)
    grad_first = dot(wqkv_ref[:, D : 2 * D], grad_k) + dot(wqkv_ref[:, 2 * D :], grad_v)
    own = grad_first[:, :block] + dot(wqkv_ref[:, :D], grad_q)
    own_ref[0] = own
    own_ref[1] = grad_first[:, 2 * block : 3 * block]
    far_ref[0] = grad_first[:, block : 2 * block].astype(BF)
    far_ref[1] = grad_first[:, 3 * block :].astype(BF)
    grad_first = jnp.concatenate([own, grad_first[:, block:]], axis=1)
    matrix[:, :D] = dot_nt(first[:, :block], grad_q)
    matrix[:, D : 2 * D] = dot_nt(first, grad_k)
    matrix[:, 2 * D : 3 * D] = dot_nt(first, grad_v)
    matrix[:, 3 * D :] = jnp.zeros((D, SPARE), F32)
    vectors = jnp.concatenate(
        [
            *sums,
            dot_nt(ones, (grad_first * normal).astype(BF))[0:1],
            dot_nt(ones, grad_first.astype(BF))[0:1],
        ],
        axis=1,
    )
    for index in range(5 * D // SPARE):
        row = index // 4 * LATE_ROWS + index % 4
        matrix[row : row + 1, 3 * D :] = vectors[:, index * SPARE : (index + 1) * SPARE]
    slot = slots()[0]
    for index in range(8):
        values = matrix[index * LATE_ROWS : (index + 1) * LATE_ROWS, :].astype(BF)
        stays = index // 4 == slot // 4
        store_block(keep_ref, send_ref, stays, (index ^ slot) % 4, values)


def input_kernel(own_ref, core_ref, chip_ref, x_ref, ln1_gain_ref, gmid_ref, out_ref):
    grad = own_ref[0] + core_ref[0].astype(F32) + chip_ref[...].astype(F32)
    normal, scale = normed(x_ref[...].astype(F32), 0)
    gain = column(ln1_gain_ref[...])[:, 0:1]
    out_ref[...] = gmid_ref[...] + norm_back(grad, normal, scale, gain, 0)


def plus(first, second):
    return (first.astype(F32) + second.astype(F32)).astype(BF)


def halve_kernel(keep_ref, got_ref, *refs):
    kept_ref, send_ref = refs[-2:]
    half = kept_ref.shape[0]
    kept_ref[...] = plus(keep_ref[:half], got_ref[:half])
    send_ref[...] = plus(keep_ref[half:], got_ref[half:])


def halve_pair_kernel(keep_ref, got_ref, *refs):
    kept_ref, send_a_ref, send_b_ref = refs[-3:]
    half = kept_ref.shape[1]
    kept_ref[...] = plus(keep_ref[:, :half], got_ref[:, :half])
    send_a_ref[...] = plus(keep_ref[0, half:], got_ref[0, half:])
    send_b_ref[...] = plus(keep_ref[1, half:], got_ref[1, half:])


def halve_two_kernel(keep_ref, got_a_ref, got_b_ref, *refs):
    kept_ref, send_a_ref, send_b_ref = refs[-3:]
    for index, (got_ref, send_ref) in enumerate(((got_a_ref, send_a_ref), (got_b_ref, send_b_ref))):
        kept_ref[index] = plus(keep_ref[index, 0], got_ref[0])
        send_ref[...] = plus(keep_ref[index, 1], got_ref[1])


def choose_kernel(keep_ref, got_a_ref, got_b_ref, *refs):
    kept_ref, send_ref = refs[-2:]
    odd = slots()[2]
    part_a, part_b = plus(keep_ref[0], got_a_ref[...]), plus(keep_ref[1], got_b_ref[...])

    @pl.when(odd == 0)
    def _():
        kept_ref[...] = part_a
        send_ref[...] = part_b

    @pl.when(odd == 1)
    def _():
        kept_ref[...] = part_b
        send_ref[...] = part_a


def plus_kernel(first_ref, second_ref, *refs):
    refs[-1][...] = plus(first_ref[...], second_ref[...])


def unpack_kernel(
    early_ref,
    early_far_ref,
    late_ref,
    late_far_ref,
    g_up_ref,
    g_down_t_ref,
    g_qkv_ref,
    g_out_ref,
    *refs,
):
    vector_refs, (matrix, extras, line) = refs[:-3], refs[-3:]
    slot_a, slot_b = slots()[:2]

    def spot(index):
        row = pl.multiple_of(index % 4 * SHARD_ROWS, 16)
        col = pl.multiple_of(index // 4 * SHARD_COLS, LANES)
        return pl.ds(row, SHARD_ROWS), pl.ds(col, SHARD_COLS)

    for place in range(8):
        early = early_ref if place < 4 else early_far_ref
        late = late_ref if place < 4 else late_far_ref
        index = place ^ slot_a
        rows, cols = spot(index)
        values = early[place % 4, 0].astype(F32)
        g_up_ref[rows, cols] = values[:SHARD_ROWS]
        extras[index] = values[SHARD_ROWS:]
        row = pl.multiple_of(index * LATE_ROWS, 8)
        matrix[pl.ds(row, LATE_ROWS), :] = late[place % 4].astype(F32)
        core, chip_x, chip_y = place // 4, place // 2 % 2, place % 2
        index = (core * 4 + chip_y * 2 + chip_x) ^ slot_b
        rows, cols = spot(index)
        values = early[place % 4, 1].astype(F32)
        g_down_t_ref[rows, cols] = values[:SHARD_ROWS]
        extras[8 + index] = values[SHARD_ROWS:]
    g_qkv_ref[...] = matrix[:, : 3 * D]
    for index in range(OUT_BLOCKS):
        row = 2 * EXTRA_ROWS * index
        g_out_ref[row : row + EXTRA_ROWS, :] = extras[index, :, :D]
        g_out_ref[row + EXTRA_ROWS : row + 2 * EXTRA_ROWS, :] = extras[index, :, D:]
    for index in range(2):
        cols = slice(index * SHARD_COLS, (index + 1) * SHARD_COLS)
        line[0:1, cols] = extras[OUT_BLOCKS + index, 0:1, :]
    g_ln1_gain, g_ln1_bias, g_bqkv, g_bout, g_ln2_gain, g_ln2_bias, g_bup, g_bdown = vector_refs
    g_bup[...] = line[0:1, :FF].reshape(FF)
    g_bout[...] = extras[OUT_BLOCKS + 2, 0:1, :D].reshape(D)
    g_ln2_gain[...] = extras[OUT_BLOCKS + 2, 0:1, D:].reshape(D)
    g_ln2_bias[...] = extras[OUT_BLOCKS + 3, 0:1, :D].reshape(D)
    g_bdown[...] = extras[OUT_BLOCKS + 3, 0:1, D:].reshape(D)
    for index in range(5 * D // SPARE):
        row = index // 4 * LATE_ROWS + index % 4
        line[1:2, index * SPARE : (index + 1) * SPARE] = matrix[row : row + 1, 3 * D :]
    g_bqkv[...] = line[1:2, : 3 * D].reshape(3 * D)
    g_ln1_gain[...] = line[1:2, 3 * D : 4 * D].reshape(D)
    g_ln1_bias[...] = line[1:2, 4 * D : 5 * D].reshape(D)


def call(kernel, name, out_shape, scratch, *operands, vmem=16, loads=(), aliases=None):
    operands = list(operands)
    specs = [pl.BlockSpec(memory_space=pltpu.VMEM) for entry in operands]
    operands += [pltpu.with_memory_space_constraint(entry, pltpu.HBM) for entry in loads]
    specs += [pl.BlockSpec(memory_space=pltpu.HBM) for entry in loads]
    return pl.pallas_call(
        kernel,
        name=name,
        out_shape=out_shape,
        in_specs=specs,
        out_specs=jax.tree.map(
            lambda entry: pl.BlockSpec(
                memory_space=pltpu.VMEM if isinstance(entry, jax.ShapeDtypeStruct) else pltpu.HBM
            ),
            out_shape,
        ),
        scratch_shapes=scratch,
        input_output_aliases=aliases or {},
        compiler_params=pltpu.CompilerParams(vmem_limit_bytes=vmem * MIB),
    )(*operands)


def shape(*dims, dtype=F32):
    return jax.ShapeDtypeStruct(dims, dtype)


def per_device(
    sizes,
    tokens,
    segment_ids,
    ln1_gain,
    ln1_bias,
    w_qkv,
    b_qkv,
    w_out,
    b_out,
    ln2_gain,
    ln2_bias,
    w_up,
    b_up,
    w_down,
    b_down,
    cotangent,
):
    dp_size, seq_size = sizes
    block = tokens.shape[1]
    length = segment_ids.shape[1]
    dp = lax.axis_index("dp")

    def swap(value, dp_bits, seq_bits):
        pairs = [
            (a * seq_size + b, (a ^ dp_bits) * seq_size + (b ^ seq_bits))
            for a in range(dp_size)
            for b in range(seq_size)
        ]
        return lax.ppermute(value, ("dp", "seq"), pairs)

    odd = (dp >> 1) & 1
    tie = lax.optimization_barrier

    x_t = tokens[0].T
    near = {bits: swap(x_t, 0, bits) for bits in (2, 3, 1)}
    loads = (
        x_t,
        segment_ids,
        ln1_gain,
        ln1_bias,
        w_qkv,
        b_qkv,
        cotangent[0].T,
        w_up,
        w_down.T,
        w_out,
        b_out,
        ln2_gain,
        ln2_bias,
        b_up,
        b_down,
    )
    like = lambda entry: jax.ShapeDtypeStruct(entry.shape, entry.dtype)
    buffer = lambda entry: pltpu.VMEM(entry.shape, entry.dtype)
    out = call(
        prelude_kernel,
        "prelude",
        (like(x_t), *[like(entry) for entry in loads[6:]])
        + (
            shape(3 * D, D, dtype=BF),
            shape(5 * D, 8),
            shape(HEAD_DIM // 2, length),
            shape(HEAD_DIM // 2, length),
            shape(block, DP, dtype=BF),
            shape(D, block, dtype=BF),
            shape(DP, block, dtype=BF),
            shape(DP, block, dtype=BF),
            shape(LANES, length, dtype=BF),
            shape(block, LANES, dtype=BF),
        ),
        [buffer(entry) for entry in loads[1:6]] + [pltpu.SemaphoreType.DMA((len(loads),))],
        loads=loads,
    )
    x0, ct_t, w_up, w_down_t, w_out, b_out, ln2_gain, ln2_bias, b_up, b_down = out[:10]
    wqkv_t, cols, cosine, sine, q, q_t, k_t, v_t, ke, qe = out[10:]
    blocks = shape(2, 4, EARLY_ROWS, SHARD_COLS, dtype=BF)
    (output, grad_middle, keep, send, k_t, v_t, lse, inner, d_out, d_out_t, x_all) = call(
        forward_kernel,
        "layer_forward",
        (
            shape(D, block, dtype=BF),
            shape(D, block),
            blocks,
            blocks,
            shape(DP, length, dtype=BF),
            shape(DP, length, dtype=BF),
            shape(block, LANES),
            shape(block, LANES),
            shape(block, DP, dtype=BF),
            shape(D, block, dtype=BF),
            pltpu.HBM((4, D, block), BF),
        ),
        [
            pltpu.VMEM((block, DP), F32),
            pltpu.VMEM((D, 3 * block), BF),
            pltpu.SemaphoreType.DMA((4,)),
        ],
        x0,
        near[1],
        near[2],
        near[3],
        k_t,
        v_t,
        q,
        ke,
        qe,
        cosine,
        sine,
        wqkv_t,
        cols,
        w_out,
        b_out,
        ln2_gain,
        ln2_bias,
        w_up,
        b_up,
        w_down_t,
        b_down,
        ct_t,
    )

    move_core, move_x, move_y, move_z = (0, 1), (1, 0), (0, 2), (2, 0)

    def add(first_term, second_term, *after):
        return call(plus_kernel, "add", like(first_term), [], first_term, second_term, *after)

    def far_sum(part):
        bit = 4
        while bit < dp_size:
            part = add(part, swap(part, bit, 0))
            bit *= 2
        return part

    def step(piece, after, grads):
        operands = (cosine, sine, q, q_t, k_t, v_t, ke, qe, lse, inner, d_out, d_out_t)
        first = 1 + len(operands)
        return call(
            functools.partial(piece_kernel, piece),
            f"attention_backward_{piece}",
            (
                shape(D, block, dtype=BF),
                shape(D, length, dtype=BF),
                shape(D, length, dtype=BF),
            ),
            [pltpu.VMEM((PIECE_ROWS, length), F32), pltpu.VMEM((PIECE_ROWS, length), F32)],
            after,
            *operands,
            *grads,
            aliases={first + i: i for i in range(len(grads))},
        )

    block_shape = (EARLY_ROWS, SHARD_COLS)
    got = swap(send, *move_core)
    got, *grads = tie((got, *step(0, send, ())))
    keep, send_a, send_b = call(
        halve_pair_kernel,
        "add_core",
        (
            shape(2, 2, *block_shape, dtype=BF),
            shape(2, *block_shape, dtype=BF),
            shape(2, *block_shape, dtype=BF),
        ),
        [],
        keep,
        got,
    )
    got_a, got_b = swap(send_a, *move_x), swap(send_b, *move_y)
    grads = step(1, send_a, grads)
    got_a, got_b, *grads = tie((got_a, got_b, *step(2, send_b, grads)))
    keep, send_a, send_b = call(
        halve_two_kernel,
        "add_chips",
        (
            shape(2, *block_shape, dtype=BF),
            shape(*block_shape, dtype=BF),
            shape(*block_shape, dtype=BF),
        ),
        [],
        keep,
        got_a,
        got_b,
    )
    got_a, got_b = swap(send_a, *move_y), swap(send_b, *move_x)
    got_a, got_b, *grads = tie((got_a, got_b, *step(3, send_a, grads)))
    kept, sent = call(
        choose_kernel,
        "add_square",
        (shape(*block_shape, dtype=BF), shape(*block_shape, dtype=BF)),
        [],
        keep,
        got_a,
        got_b,
    )
    if dp_size > 2:
        got = swap(sent, *move_z)
        got, *grads = tie((got, *step(4, sent, grads)))
        kept = add(kept, got)
    else:
        grads = step(4, sent, grads)
    late_blocks = shape(4, LATE_ROWS, LATE_COLS, dtype=BF)
    late_keep, late_send, own, far = call(
        projection_kernel,
        "projection",
        (late_blocks, late_blocks, shape(2, D, block), shape(2, D, block, dtype=BF)),
        [
            pltpu.VMEM((4, D, block), BF),
            buffer(w_qkv),
            buffer(ln1_gain),
            buffer(ln1_bias),
            pltpu.VMEM((D, LATE_COLS), F32),
            pltpu.SemaphoreType.DMA((4,)),
        ],
        *grads,
        loads=(x_all, w_qkv, ln1_gain, ln1_bias),
    )
    def halve(keep, got, half):
        return call(
            halve_kernel,
            "add_half",
            (shape(half, *keep.shape[1:], dtype=BF),) * 2,
            [],
            keep,
            got,
        )

    core_far = swap(far, *move_core)
    late, late_send = halve(late_keep, swap(late_send, *move_core), 2)
    late_send, kept = tie((late_send, kept))
    got = swap(late_send, *move_x)
    kept = far_sum(kept)
    late, late_send = halve(late, got, 1)
    late_send, kept = tie((late_send, kept))
    got = swap(late_send[0], *move_y)
    chip_far = swap(plus(own[1], core_far[1]), *move_y)
    other = swap(kept, *move_z) if dp_size > 2 else sent
    late = add(late[0], got)
    early = jnp.stack([jnp.where(odd == 1, other, kept), jnp.where(odd == 1, kept, other)])
    late, early, chip_far = tie((late, early, chip_far))
    input_grad = call(
        input_kernel,
        "input_gradient",
        shape(D, block),
        [],
        own,
        core_far,
        chip_far,
        x0,
        ln1_gain,
        grad_middle,
        vmem=8,
    )

    def spread(part, move):
        return jnp.concatenate([part, swap(part, *move)])

    early = spread(early[None], move_y)
    if dp_size > 2:
        late = add(late, swap(late, *move_z))
        late, early, input_grad = tie((late, early, input_grad))
    early = spread(early, move_x)
    late = far_sum(late)
    late = spread(late[None], move_y)
    late, early = tie((late, early))
    early_far = swap(early, *move_core)
    late = spread(late, move_x)
    late_far = swap(late, *move_core)
    g_up, g_down_t, g_qkv, g_out, *vectors = call(
        unpack_kernel,
        "unpack",
        (
            shape(D, FF),
            shape(D, FF),
            shape(D, 3 * D),
            shape(D, D),
            shape(D),
            shape(D),
            shape(3 * D),
            shape(D),
            shape(D),
            shape(D),
            shape(FF),
            shape(D),
        ),
        [
            pltpu.VMEM((D, LATE_COLS), F32),
            pltpu.VMEM((16, EXTRA_ROWS, SHARD_COLS), F32),
            pltpu.VMEM((8, 5 * D), F32),
        ],
        early,
        early_far,
        late,
        late_far,
    )
    g_ln1_gain, g_ln1_bias, g_bqkv, g_bout, g_ln2_gain, g_ln2_bias, g_bup, g_bdown = vectors
    return (
        output.T[None],
        input_grad.T[None],
        g_ln1_gain,
        g_ln1_bias,
        g_qkv,
        g_bqkv,
        g_out,
        g_bout,
        g_ln2_gain,
        g_ln2_bias,
        g_up,
        g_bup,
        g_down_t.T,
        g_bdown,
    )


def solution(mesh):
    split = P("dp", "seq", None)
    whole = P()
    return jax.shard_map(
        functools.partial(per_device, (mesh.shape["dp"], mesh.shape["seq"])),
        mesh=mesh,
        in_specs=(split, P("dp", None)) + (whole,) * 12 + (split,),
        out_specs=(split, split) + (whole,) * 12,
        check_vma=False,
    )
```

```python
import functools
import math

import jax
import jax.numpy as jnp
from jax import lax
from jax.experimental import pallas as pl
from jax.experimental.pallas import tpu as pltpu
from jax.sharding import PartitionSpec as P

HEADS = 20
HEAD_DIM = 16
D = HEADS * HEAD_DIM
FF = 4 * D
GENES = 4
LANES = 128
TILE_HEADS = LANES // HEAD_DIM
DP = 384
BAR = -1e30
EPS = 1e-05
SHARD_ROWS, SHARD_COLS, EXTRA_ROWS = D // 4, FF // 2, 16
EARLY_ROWS = SHARD_ROWS + EXTRA_ROWS
LATE_ROWS, LATE_COLS = D // 8, 8 * LANES
SPARE = LATE_COLS - 3 * D
OUT_BLOCKS = D // (2 * EXTRA_ROWS)
PIECES = (range(0, 4), range(4, HEADS))
MIB = 1 << 20
BF = jnp.bfloat16
F32 = jnp.float32
ERF_NUM = (
    -2.72614225801306e-10,
    2.77068142495902e-08,
    -2.10102402082508e-06,
    -5.69250639462346e-05,
    -7.34990630326855e-04,
    -2.95459980854025e-03,
    -1.60960333262415e-02,
)
ERF_DEN = (
    -1.45660718464996e-05,
    -2.13374055278905e-04,
    -1.68282697438203e-03,
    -7.37332916720468e-03,
    -1.42647390514189e-02,
)


def dot(a, b, contract=((1,), (0,))):
    return lax.dot_general(a, b, (contract, ((), ())), preferred_element_type=F32)


def dot_nt(a, b):
    return dot(a, b, ((1,), (1,)))


def dot_tn(a, b):
    return dot(a, b, ((0,), (0,)))


def poly(x, coefficients):
    total = jnp.full_like(x, coefficients[0])
    for entry in coefficients[1:]:
        total = total * x + entry
    return total


def erf(x):
    x = jnp.clip(x, -4.0, 4.0)
    square = x * x
    return x * poly(square, ERF_NUM) / poly(square, ERF_DEN)


def normed(values, axis):
    centered = values - jnp.mean(values, axis=axis, keepdims=True)
    spread = jnp.mean(centered * centered, axis=axis, keepdims=True)
    scale = lax.rsqrt(spread + EPS)
    return centered * scale, scale


def norm_back(grad, normal, scale, gain, axis):
    e = grad * gain
    return scale * (
        e
        - jnp.mean(e, axis=axis, keepdims=True)
        - normal * jnp.mean(e * normal, axis=axis, keepdims=True)
    )


def rotate_rows(values, cosine, sine):
    rows, cols = values.shape
    half = HEAD_DIM // 2
    parts = values.reshape(rows // HEAD_DIM, 2, half, cols)
    first, second = parts[:, 0], parts[:, 1]
    out = jnp.stack([first * cosine - second * sine, second * cosine + first * sine], axis=1)
    return out.reshape(rows, cols)


def pad_rows(values, rows):
    return jnp.concatenate(
        [values, jnp.zeros((rows - values.shape[0], values.shape[1]), values.dtype)], axis=0
    )


def pad_cols(values, cols):
    return jnp.concatenate(
        [values, jnp.zeros((values.shape[0], cols - values.shape[1]), values.dtype)], axis=1
    )


def slots():
    dp, seq = lax.axis_index("dp"), lax.axis_index("seq")
    core, chip_y, chip_x = seq & 1, seq >> 1, dp & 1
    return core * 4 + chip_x * 2 + chip_y, (dp >> 1) & 1, seq


def load_all(sources, targets, sems):
    copies = [
        pltpu.make_async_copy(source, target, sems.at[i])
        for i, (source, target) in enumerate(zip(sources, targets))
    ]
    for copy in copies:
        copy.start()
    return copies


def column(vector):
    return jnp.broadcast_to(vector.reshape(1, -1), (8, vector.shape[0])).T


def prelude_kernel(*refs):
    sources, outs, (local, sems) = refs[:15], refs[15:-6], (refs[-6:-1], refs[-1])
    kept, made = outs[:10], outs[10:]
    copies = load_all(sources, (kept[0], *local, *kept[1:]), sems)
    for copy in copies[:6]:
        copy.wait()
    prelude_body(kept[0], *local, *made)
    for copy in copies[6:]:
        copy.wait()


def prelude_body(
    x0_ref,
    seg_ref,
    ln1_gain_ref,
    ln1_bias_ref,
    wqkv_ref,
    bqkv_ref,
    wqkv_t_ref,
    cols_ref,
    cos_ref,
    sin_ref,
    q_ref,
    qt_ref,
    kt_ref,
    vt_ref,
    ke_ref,
    qe_ref,
):
    block = x0_ref.shape[1]
    length = 4 * block
    seq = slots()[2]
    genes = seg_ref[...]
    begins = [
        jnp.sum((genes < gene).astype(F32), axis=1, keepdims=True) for gene in range(1, GENES)
    ]
    index = lax.broadcasted_iota(jnp.int32, (1, block), 1).astype(F32)
    half = HEAD_DIM // 2
    step = lax.broadcasted_iota(jnp.int32, (half, block), 0).astype(F32)
    frequency = jnp.exp(step * (-2.0 * math.log(10000.0) / HEAD_DIM))
    row = lax.broadcasted_iota(jnp.int32, (LANES, block), 0)
    for distance in range(4):
        cols = slice(distance * block, (distance + 1) * block)
        chunk = seq ^ distance
        own = seg_ref[:, pl.ds(pl.multiple_of(chunk * block, block), block)]
        begin = jnp.zeros((1, block), F32)
        for gene in range(1, GENES):
            begin = jnp.where(own == gene, begins[gene - 1], begin)
        place = index + (chunk * block).astype(F32) - begin
        angle = place * frequency
        cos_ref[:, cols] = jnp.cos(angle)
        sin_ref[:, cols] = jnp.sin(angle)
        table = jnp.where(
            row < GENES, jnp.where(row == own, 0.0, BAR), jnp.where(row < GENES + 3, 1.0, 0.0)
        )
        ke_ref[:, cols] = table.astype(BF)
        if distance == 0:
            qe_ref[...] = jnp.where(row == own, 1.0, 0.0).T.astype(BF)

    wqkv_t_ref[...] = wqkv_ref[...].T
    cols_ref[: 3 * D, :] = column(bqkv_ref[...])
    cols_ref[3 * D : 4 * D, :] = column(ln1_gain_ref[...])
    cols_ref[4 * D :, :] = column(ln1_bias_ref[...])
    normal, _ = normed(x0_ref[...].astype(F32), 0)
    first = (normal * cols_ref[3 * D : 4 * D, 0:1] + cols_ref[4 * D :, 0:1]).astype(BF)
    raw = dot(wqkv_t_ref[...], first) + cols_ref[: 3 * D, 0:1]
    cosine, sine = cos_ref[:, :block], sin_ref[:, :block]
    q_t = rotate_rows(raw[:D], cosine, sine).astype(BF)
    qt_ref[...] = q_t
    q_ref[...] = pad_rows(q_t.astype(F32) * (1.0 / math.sqrt(HEAD_DIM)), DP).T.astype(BF)
    kt_ref[...] = pad_rows(rotate_rows(raw[D : 2 * D], cosine, sine).astype(BF), DP)
    vt_ref[...] = pad_rows(raw[2 * D :].astype(BF), DP)


def forward_kernel(
    x0_ref,
    x1_ref,
    x2_ref,
    x3_ref,
    k0_ref,
    v0_ref,
    q_ref,
    ke_ref,
    qe_ref,
    cos_ref,
    sin_ref,
    wqkv_t_ref,
    cols_ref,
    w_out_ref,
    b_out_ref,
    ln2_gain_ref,
    ln2_bias_ref,
    w_up_ref,
    b_up_ref,
    w_down_t_ref,
    b_down_ref,
    ct_t_ref,
    out_ref,
    gmid_ref,
    keep_ref,
    send_ref,
    kt_ref,
    vt_ref,
    lse_ref,
    inner_ref,
    do_ref,
    dot_ref,
    x_all_hbm,
    att_acc,
    xn_ref,
    sems,
):
    block = x0_ref.shape[1]
    chunks = (x0_ref, x1_ref, x2_ref, x3_ref)
    copies = load_all(chunks, [x_all_hbm.at[i] for i in range(4)], sems)
    gain, bias = cols_ref[3 * D : 4 * D, 0:1], cols_ref[4 * D :, 0:1]
    for index, chunk in enumerate((x1_ref, x2_ref, x3_ref)):
        normal, _ = normed(chunk[...].astype(F32), 0)
        xn_ref[:, index * block : (index + 1) * block] = (normal * gain + bias).astype(BF)
    first = xn_ref[...]
    kt_ref[:, :block] = k0_ref[...]
    vt_ref[:, :block] = v0_ref[...]
    raw = dot(wqkv_t_ref[D:, :], first) + cols_ref[D : 3 * D, 0:1]
    keys = rotate_rows(raw[:D], cos_ref[:, block:], sin_ref[:, block:])
    kt_ref[:, block:] = pad_rows(keys.astype(BF), DP)
    vt_ref[:, block:] = pad_rows(raw[D:].astype(BF), DP)

    lane = lax.broadcasted_iota(jnp.int32, (block, LANES), 1)
    att_acc[...] = jnp.zeros_like(att_acc)
    lse_ref[...] = jnp.zeros_like(lse_ref)
    zero = jnp.zeros((), BF)

    def score(head):
        start = head // TILE_HEADS * LANES
        mask = lane // HEAD_DIM == head % TILE_HEADS
        left = jnp.concatenate(
            [jnp.where(mask, q_ref[:, start : start + LANES], zero), qe_ref[...]], axis=1
        )
        right = jnp.concatenate([kt_ref[start : start + LANES, :], ke_ref[...]], axis=0)
        return head, mask, slice(start, start + LANES), dot(left, right)

    def mix(head, mask, tile, scores):
        top = jnp.max(scores, axis=1, keepdims=True)
        weights = jnp.exp(scores - top)
        mass = jnp.sum(weights, axis=1, keepdims=True)
        mixed = dot_nt(weights.astype(BF), vt_ref[tile, :])
        att_acc[:, tile] += jnp.where(mask, mixed / mass, 0.0)
        lse_ref[...] = jnp.where(lane == head, top + jnp.log(mass), lse_ref[...])

    scored = score(0)
    for head in range(1, HEADS):
        ahead = score(head)
        mix(*scored)
        scored = ahead
    mix(*scored)

    def line(ref):
        return ref[...].reshape(1, -1)

    attended_wide = att_acc[:, :D]
    attended = attended_wide.astype(BF)
    middle = x0_ref[...].T.astype(F32) + (dot(attended, w_out_ref[...]) + line(b_out_ref))
    normal2, scale2 = normed(middle, 1)
    gain2 = line(ln2_gain_ref)
    second = (normal2 * gain2 + line(ln2_bias_ref)).astype(BF)
    pre = dot(second, w_up_ref[...]) + line(b_up_ref)
    share = 0.5 + 0.5 * erf(pre * (1.0 / math.sqrt(2.0)))
    active = (pre * share).astype(BF)
    slope = share + pre * (jnp.exp(-0.5 * pre * pre) * (1.0 / math.sqrt(2.0 * math.pi)))
    output = middle + dot_nt(active, w_down_t_ref[...]) + line(b_down_ref)
    out_ref[...] = output.T.astype(BF)
    ct_t = ct_t_ref[...]
    ct = ct_t.T
    ct_wide = ct.astype(F32)
    grad_pre = (dot(ct, w_down_t_ref[...]) * slope).astype(BF)
    grad_second = dot_nt(grad_pre, w_up_ref[...])
    grad_middle = ct_wide + norm_back(grad_second, normal2, scale2, gain2, 1)
    gmid_ref[...] = grad_middle.T
    branch = grad_middle.astype(BF)
    grad_att = dot_nt(branch, w_out_ref[...]).astype(BF)
    grad_att_wide = pad_cols(grad_att.astype(F32), DP)
    do_ref[...] = grad_att_wide.astype(BF)
    dot_ref[...] = grad_att_wide.T[:D, :].astype(BF)
    att_acc[...] = grad_att_wide * att_acc[...]

    inner_ref[...] = jnp.zeros_like(inner_ref)

    for head in range(HEADS):
        tile = slice(head // TILE_HEADS * LANES, (head // TILE_HEADS + 1) * LANES)
        mask = lane // HEAD_DIM == head % TILE_HEADS
        total = jnp.sum(jnp.where(mask, att_acc[:, tile], 0.0), axis=1, keepdims=True)
        inner_ref[...] = jnp.where(lane == head, total, inner_ref[...])

    grad_up = dot_tn(second, grad_pre).astype(BF)
    grad_down = dot(ct_t, active).astype(BF)
    grad_out = dot_tn(attended, branch)

    def column_sum(values):
        return jnp.sum(values, axis=0, keepdims=True)

    lines = column_sum(grad_pre.astype(F32))
    lines = [
        lines[:, :SHARD_COLS],
        lines[:, SHARD_COLS:],
        jnp.concatenate([column_sum(branch.astype(F32)), column_sum(grad_second * normal2)], axis=1),
        jnp.concatenate([column_sum(grad_second), column_sum(ct_wide)], axis=1),
    ]

    def extra(index):
        if index < OUT_BLOCKS:
            row = 2 * EXTRA_ROWS * index
            upper = grad_out[row : row + EXTRA_ROWS]
            lower = grad_out[row + EXTRA_ROWS : row + 2 * EXTRA_ROWS]
            return jnp.concatenate([upper, lower], axis=1).astype(BF)
        if index < OUT_BLOCKS + len(lines):
            line = lines[index - OUT_BLOCKS]
            return jnp.broadcast_to(line, (EXTRA_ROWS, SHARD_COLS)).astype(BF)
        return jnp.zeros((EXTRA_ROWS, SHARD_COLS), BF)

    slot = slots()[0]
    for index in range(8):
        rows, cols = shard(index)
        stays = index // 4 == slot // 4
        for array, values in enumerate((grad_up, grad_down)):
            block_values = jnp.concatenate([values[rows, cols], extra(8 * array + index)], axis=0)
            store_block(keep_ref, send_ref, stays, ((index ^ slot) % 4, array), block_values)
    for copy in copies:
        copy.wait()


def store_block(keep_ref, send_ref, stays, place, values):
    @pl.when(stays)
    def _():
        keep_ref[place] = values

    @pl.when(jnp.logical_not(stays))
    def _():
        send_ref[place] = values


def shard(index):
    row, col = index % 4 * SHARD_ROWS, index // 4 * SHARD_COLS
    return slice(row, row + SHARD_ROWS), slice(col, col + SHARD_COLS)


def piece_kernel(
    heads,
    loads,
    after_ref,
    cos_ref,
    sin_ref,
    q_ref,
    qt_ref,
    kt_ref,
    vt_ref,
    ke_ref,
    qe_ref,
    lse_ref,
    inner_ref,
    do_ref,
    dot_ref,
    *refs,
):
    dq_acc, dk_acc, dv_acc, sems = refs[-4:]
    outs = refs[-4 - 3 - loads : -4]
    gq_ref, gk_ref, gv_ref = outs[:3]
    copies = load_all(refs[len(refs) - 4 - 3 - 2 * loads : len(refs) - 4 - 3 - loads], outs[3:], sems)
    block = q_ref.shape[0]
    lane = lax.broadcasted_iota(jnp.int32, (block, LANES), 1)
    zero = jnp.zeros((), BF)
    extra = ke_ref[...]

    def minus(ref, head):
        value = jnp.broadcast_to(-ref[:, head : head + 1], (block, LANES))
        high = value.astype(BF)
        rest = value - high.astype(F32)
        mid = rest.astype(BF)
        low = (rest - mid.astype(F32)).astype(BF)
        return jnp.where(
            lane == GENES,
            high,
            jnp.where(lane == GENES + 1, mid, jnp.where(lane == GENES + 2, low, zero)),
        )

    first_tile, last_tile = heads[0] // TILE_HEADS, heads[-1] // TILE_HEADS
    for tile_index in range(first_tile, last_tile + 1):
        tile = slice(tile_index * LANES, (tile_index + 1) * LANES)
        keys = kt_ref[tile, :]
        key_side = jnp.concatenate([keys, extra], axis=0)
        value_side = jnp.concatenate([vt_ref[tile, :], extra], axis=0)
        grad_queries = jnp.zeros((block, LANES), F32)
        for head in heads:
            if head // TILE_HEADS != tile_index:
                continue
            rows = slice(head * HEAD_DIM, (head + 1) * HEAD_DIM)
            here = slice((head - heads[0]) * HEAD_DIM, (head - heads[0] + 1) * HEAD_DIM)
            mask = lane // HEAD_DIM == head % TILE_HEADS
            left = jnp.concatenate(
                [jnp.where(mask, q_ref[:, tile], zero), qe_ref[...] + minus(lse_ref, head)], axis=1
            )
            probs = jnp.exp(dot(left, key_side))
            left = jnp.concatenate(
                [jnp.where(mask, do_ref[:, tile], zero), minus(inner_ref, head)], axis=1
            )
            grad_scores = (probs * dot(left, value_side)).astype(BF)
            dv_acc[here, :] = dot(dot_ref[rows, :], probs.astype(BF))
            dk_acc[here, :] = dot(qt_ref[rows, :], grad_scores)
            grad_queries += jnp.where(mask, dot_nt(grad_scores, keys), 0.0)
        dq_acc[(tile_index - first_tile) * LANES : (tile_index - first_tile + 1) * LANES, :] = (
            grad_queries.T
        )

    cosine, sine = cos_ref[...], sin_ref[...]
    scale = 1.0 / math.sqrt(HEAD_DIM)
    rows = slice(heads[0] * HEAD_DIM, (heads[-1] + 1) * HEAD_DIM)
    skip = first_tile * LANES
    dq_t = (dq_acc[rows.start - skip : rows.stop - skip, :] * scale).astype(BF).astype(F32)
    gq_ref[rows, :] = rotate_rows(dq_t, cosine[:, :block], -sine[:, :block]).astype(BF)
    gk_ref[rows, :] = rotate_rows(dk_acc[...] * scale, cosine, -sine).astype(BF)
    gv_ref[rows, :] = dv_acc[...].astype(BF)
    for copy in copies:
        copy.wait()


def projection_kernel(
    after_ref,
    gq_ref,
    gk_ref,
    gv_ref,
    x_ref,
    wqkv_ref,
    ln1_gain_ref,
    ln1_bias_ref,
    keep_ref,
    send_ref,
    own_ref,
    far_ref,
    matrix,
):
    block = x_ref.shape[2]
    length = 4 * block
    ones = jnp.ones((16, length), BF)
    grad_q, grad_k, grad_v = gq_ref[...], gk_ref[...], gv_ref[...]
    sums = [
        dot_nt(ones[:, :block], grad_q)[0:1],
        dot_nt(ones, grad_k)[0:1],
        dot_nt(ones, grad_v)[0:1],
    ]
    gain, bias = column(ln1_gain_ref[...])[:, 0:1], column(ln1_bias_ref[...])[:, 0:1]
    normal = jnp.concatenate([normed(x_ref[i].astype(F32), 0)[0] for i in range(4)], axis=1)
    first = (normal * gain + bias).astype(BF)
    grad_first = dot(wqkv_ref[:, D : 2 * D], grad_k) + dot(wqkv_ref[:, 2 * D :], grad_v)
    own = grad_first[:, :block] + dot(wqkv_ref[:, :D], grad_q)
    own_ref[0] = own
    own_ref[1] = grad_first[:, 2 * block : 3 * block]
    far_ref[0] = grad_first[:, block : 2 * block].astype(BF)
    far_ref[1] = grad_first[:, 3 * block :].astype(BF)
    grad_first = jnp.concatenate([own, grad_first[:, block:]], axis=1)
    matrix[:, :D] = dot_nt(first[:, :block], grad_q)
    matrix[:, D : 2 * D] = dot_nt(first, grad_k)
    matrix[:, 2 * D : 3 * D] = dot_nt(first, grad_v)
    matrix[:, 3 * D :] = jnp.zeros((D, SPARE), F32)
    vectors = jnp.concatenate(
        [
            *sums,
            dot_nt(ones, (grad_first * normal).astype(BF))[0:1],
            dot_nt(ones, grad_first.astype(BF))[0:1],
        ],
        axis=1,
    )
    for index in range(5 * D // SPARE):
        row = index // 4 * LATE_ROWS + index % 4
        matrix[row : row + 1, 3 * D :] = vectors[:, index * SPARE : (index + 1) * SPARE]
    slot = slots()[0]
    for index in range(8):
        values = matrix[index * LATE_ROWS : (index + 1) * LATE_ROWS, :].astype(BF)
        stays = index // 4 == slot // 4
        store_block(keep_ref, send_ref, stays, (index ^ slot) % 4, values)


def input_kernel(own_ref, core_ref, chip_ref, x_ref, ln1_gain_ref, gmid_ref, out_ref):
    grad = own_ref[0] + core_ref[0].astype(F32) + chip_ref[...].astype(F32)
    normal, scale = normed(x_ref[...].astype(F32), 0)
    gain = column(ln1_gain_ref[...])[:, 0:1]
    out_ref[...] = gmid_ref[...] + norm_back(grad, normal, scale, gain, 0)


def plus(first, second):
    return (first.astype(F32) + second.astype(F32)).astype(BF)


def split_kernel(keep_ref, got_ref, *out_refs):
    for index, out_ref in enumerate(out_refs):
        out_ref[...] = plus(keep_ref[index], got_ref[index])


def four(refs):
    first, second, third, fourth = [ref[...].astype(F32) for ref in refs]
    return ((first + second) + (third + fourth)).astype(BF)


def square_kernel(*refs):
    refs[-1][...] = four(refs[:4])


def choose_kernel(*refs):
    kept_ref, send_ref = refs[-2:]
    total = four(refs[:4])
    odd = slots()[1]

    @pl.when(odd == 0)
    def _():
        kept_ref[...] = total[0]
        send_ref[...] = total[1]

    @pl.when(odd == 1)
    def _():
        kept_ref[...] = total[1]
        send_ref[...] = total[0]


def both_kernel(kept_ref, other_ref, a_ref, b_ref):
    odd = slots()[1]

    @pl.when(odd == 0)
    def _():
        a_ref[...] = kept_ref[...]
        b_ref[...] = other_ref[...]

    @pl.when(odd == 1)
    def _():
        a_ref[...] = other_ref[...]
        b_ref[...] = kept_ref[...]


def plus_kernel(first_ref, second_ref, *refs):
    refs[-1][...] = plus(first_ref[...], second_ref[...])


def gather_kernel(*refs):
    early_ref, late_ref = refs[-2:]
    for index in range(4):
        early_ref[2 * index : 2 * index + 2] = refs[index][...]
        late_ref[index] = refs[4 + index][...]


def unpack_early_kernel(own_ref, far_ref, *refs):
    g_up_ref, g_down_t_ref, g_out_ref, g_bout, g_ln2_gain, g_ln2_bias, g_bup, g_bdown = refs[:-2]
    extras, line = refs[-2:]
    slot = slots()[0]
    for place in range(8):
        blocks_ref = far_ref if place // 4 else own_ref
        places = (place, place // 4 * 4 + place % 2 * 2 + place // 2 % 2)
        for array, out_ref in enumerate((g_up_ref, g_down_t_ref)):
            index = places[array] ^ slot
            row = pl.multiple_of(index % 4 * SHARD_ROWS, 16)
            col = pl.multiple_of(index // 4 * SHARD_COLS, LANES)
            values = blocks_ref[4 * array + place % 4].astype(F32)
            out_ref[pl.ds(row, SHARD_ROWS), pl.ds(col, SHARD_COLS)] = values[:SHARD_ROWS]
            extras[8 * array + index] = values[SHARD_ROWS:]
    for index in range(OUT_BLOCKS):
        row = 2 * EXTRA_ROWS * index
        g_out_ref[row : row + EXTRA_ROWS, :] = extras[index, :, :D]
        g_out_ref[row + EXTRA_ROWS : row + 2 * EXTRA_ROWS, :] = extras[index, :, D:]
    for index in range(2):
        cols = slice(index * SHARD_COLS, (index + 1) * SHARD_COLS)
        line[0:1, cols] = extras[OUT_BLOCKS + index, 0:1, :]
    g_bup[...] = line[0:1, :FF].reshape(FF)
    g_bout[...] = extras[OUT_BLOCKS + 2, 0:1, :D].reshape(D)
    g_ln2_gain[...] = extras[OUT_BLOCKS + 2, 0:1, D:].reshape(D)
    g_ln2_bias[...] = extras[OUT_BLOCKS + 3, 0:1, :D].reshape(D)
    g_bdown[...] = extras[OUT_BLOCKS + 3, 0:1, D:].reshape(D)


def unpack_late_kernel(own_ref, far_ref, g_qkv_ref, g_bqkv, g_ln1_gain, g_ln1_bias, matrix, line):
    slot = slots()[0]
    for place in range(8):
        blocks_ref = far_ref if place // 4 else own_ref
        row = pl.multiple_of((place ^ slot) * LATE_ROWS, 8)
        matrix[pl.ds(row, LATE_ROWS), :] = blocks_ref[place % 4].astype(F32)
    g_qkv_ref[...] = matrix[:, : 3 * D]
    for index in range(5 * D // SPARE):
        row = index // 4 * LATE_ROWS + index % 4
        line[0:1, index * SPARE : (index + 1) * SPARE] = matrix[row : row + 1, 3 * D :]
    g_bqkv[...] = line[0:1, : 3 * D].reshape(3 * D)
    g_ln1_gain[...] = line[0:1, 3 * D : 4 * D].reshape(D)
    g_ln1_bias[...] = line[0:1, 4 * D : 5 * D].reshape(D)


def call(kernel, name, out_shape, scratch, *operands, vmem=16, loads=(), aliases=None, micros=0):
    operands = list(operands)
    specs = [pl.BlockSpec(memory_space=pltpu.VMEM) for entry in operands]
    operands += [pltpu.with_memory_space_constraint(entry, pltpu.HBM) for entry in loads]
    specs += [pl.BlockSpec(memory_space=pltpu.HBM) for entry in loads]
    return pl.pallas_call(
        kernel,
        name=name,
        out_shape=out_shape,
        in_specs=specs,
        out_specs=jax.tree.map(
            lambda entry: pl.BlockSpec(
                memory_space=pltpu.VMEM if isinstance(entry, jax.ShapeDtypeStruct) else pltpu.HBM
            ),
            out_shape,
        ),
        scratch_shapes=scratch,
        input_output_aliases=aliases or {},
        cost_estimate=pl.CostEstimate(flops=micros * 10**9, bytes_accessed=0, transcendentals=0)
        if micros
        else None,
        compiler_params=pltpu.CompilerParams(vmem_limit_bytes=vmem * MIB),
    )(*operands)


def shape(*dims, dtype=F32):
    return jax.ShapeDtypeStruct(dims, dtype)


def per_device(
    sizes,
    tokens,
    segment_ids,
    ln1_gain,
    ln1_bias,
    w_qkv,
    b_qkv,
    w_out,
    b_out,
    ln2_gain,
    ln2_bias,
    w_up,
    b_up,
    w_down,
    b_down,
    cotangent,
):
    dp_size, seq_size = sizes
    block = tokens.shape[1]
    length = segment_ids.shape[1]
    def swap(value, dp_bits, seq_bits):
        pairs = [
            (a * seq_size + b, (a ^ dp_bits) * seq_size + (b ^ seq_bits))
            for a in range(dp_size)
            for b in range(seq_size)
        ]
        return lax.ppermute(value, ("dp", "seq"), pairs)

    tie = lax.optimization_barrier

    x_t = tokens[0].T
    near = {bits: swap(x_t, 0, bits) for bits in (2, 3, 1)}
    loads = (
        x_t,
        segment_ids,
        ln1_gain,
        ln1_bias,
        w_qkv,
        b_qkv,
        cotangent[0].T,
        w_up,
        w_down.T,
        w_out,
        b_out,
        ln2_gain,
        ln2_bias,
        b_up,
        b_down,
    )
    like = lambda entry: jax.ShapeDtypeStruct(entry.shape, entry.dtype)
    buffer = lambda entry: pltpu.VMEM(entry.shape, entry.dtype)
    out = call(
        prelude_kernel,
        "prelude",
        (like(x_t), *[like(entry) for entry in loads[6:]])
        + (
            shape(3 * D, D, dtype=BF),
            shape(5 * D, 8),
            shape(HEAD_DIM // 2, length),
            shape(HEAD_DIM // 2, length),
            shape(block, DP, dtype=BF),
            shape(D, block, dtype=BF),
            shape(DP, block, dtype=BF),
            shape(DP, block, dtype=BF),
            shape(LANES, length, dtype=BF),
            shape(block, LANES, dtype=BF),
        ),
        [buffer(entry) for entry in loads[1:6]] + [pltpu.SemaphoreType.DMA((len(loads),))],
        loads=loads,
    )
    x0, ct_t, w_up, w_down_t, w_out, b_out, ln2_gain, ln2_bias, b_up, b_down = out[:10]
    wqkv_t, cols, cosine, sine, q, q_t, k_t, v_t, ke, qe = out[10:]
    early_block = shape(2, EARLY_ROWS, SHARD_COLS, dtype=BF)
    blocks = shape(4, *early_block.shape, dtype=BF)
    (output, grad_middle, keep, send, k_t, v_t, lse, inner, d_out, d_out_t, x_all) = call(
        forward_kernel,
        "layer_forward",
        (
            shape(D, block, dtype=BF),
            shape(D, block),
            blocks,
            blocks,
            shape(DP, length, dtype=BF),
            shape(DP, length, dtype=BF),
            shape(block, LANES),
            shape(block, LANES),
            shape(block, DP, dtype=BF),
            shape(D, block, dtype=BF),
            pltpu.HBM((4, D, block), BF),
        ),
        [
            pltpu.VMEM((block, DP), F32),
            pltpu.VMEM((D, 3 * block), BF),
            pltpu.SemaphoreType.DMA((4,)),
        ],
        x0,
        near[1],
        near[2],
        near[3],
        k_t,
        v_t,
        q,
        ke,
        qe,
        cosine,
        sine,
        wqkv_t,
        cols,
        w_out,
        b_out,
        ln2_gain,
        ln2_bias,
        w_up,
        b_up,
        w_down_t,
        b_down,
        ct_t,
        vmem=28,
    )

    move_core, move_x, move_y, move_z, move_z2 = (0, 1), (1, 0), (0, 2), (2, 0), (4, 0)

    def add(first_term, second_term, *after):
        return call(plus_kernel, "add", like(first_term), [], first_term, second_term, *after)

    def far_sum(part):
        bit = 8
        while bit < dp_size:
            part = add(part, swap(part, bit, 0))
            bit *= 2
        return part

    def step(piece, after, grads, loads=()):
        operands = (cosine, sine, q, q_t, k_t, v_t, ke, qe, lse, inner, d_out, d_out_t)
        first = 1 + len(operands)
        heads = PIECES[piece]
        rows = len(heads) * HEAD_DIM
        tiles = heads[-1] // TILE_HEADS - heads[0] // TILE_HEADS + 1
        return call(
            functools.partial(piece_kernel, heads, len(loads)),
            f"attention_backward_{piece}",
            (
                shape(D, block, dtype=BF),
                shape(D, length, dtype=BF),
                shape(D, length, dtype=BF),
                *[like(entry) for entry in loads],
            ),
            [
                pltpu.VMEM((tiles * LANES, block), F32),
                pltpu.VMEM((rows, length), F32),
                pltpu.VMEM((rows, length), F32),
                pltpu.SemaphoreType.DMA((max(1, len(loads)),)),
            ],
            after,
            *operands,
            *grads,
            aliases={first + i: i for i in range(len(grads))},
            loads=loads,
            vmem=28,
        )

    def split(name, keep, got):
        return call(split_kernel, name, (like(keep[0]),) * 4, [], keep, got)

    moves = [move_y, move_x, (1, 2)]

    def square_swap(parts):
        return [swap(part, *move) for part, move in zip(parts, moves)]

    got = swap(send, *move_core)
    got, *grads = tie((got, *step(0, send, ())))
    kept, *sends = split("add_core", keep, got)
    gots = square_swap(sends)
    grads = step(1, sends[2], grads, (x_all, w_qkv, ln1_gain, ln1_bias))
    *gots, first_grad = tie((*gots, grads[0]))
    grads = (first_grad, *grads[1:])
    half = shape(EARLY_ROWS, SHARD_COLS, dtype=BF)
    kept, sent = call(choose_kernel, "add_square", (half, half), [], kept, *gots)
    if dp_size > 2:
        got = swap(sent, *move_z)
    late_blocks = shape(4, LATE_ROWS, LATE_COLS, dtype=BF)
    late_keep, late_send, own, far = call(
        projection_kernel,
        "projection",
        (late_blocks, late_blocks, shape(2, D, block), shape(2, D, block, dtype=BF)),
        [pltpu.VMEM((D, LATE_COLS), F32)],
        sent,
        *grads,
    )
    if dp_size > 2:
        got, late_send = tie((got, late_send))
        kept = add(kept, got)
    if dp_size > 4:
        got = swap(kept, *move_z2)
    core_far = swap(far, *move_core)
    late, *sends = split("add_late_core", late_keep, swap(late_send, *move_core))
    gots = square_swap(sends)
    late = call(square_kernel, "add_late_square", like(late), [], late, *gots)
    if dp_size > 4:
        got, late = tie((got, late))
        kept = far_sum(add(kept, got))
    other = swap(kept, *move_z) if dp_size > 2 else sent
    late, core_far = tie((late, core_far))
    chip_far = swap(plus(own[1], core_far[1]), *move_y)
    if dp_size > 2:
        got, chip_far = tie((swap(late, *move_z), chip_far))
        late = add(late, got)
    early_a, early_b = call(both_kernel, "early_both", (half, half), [], kept, other)
    input_grad = call(
        input_kernel,
        "input_gradient",
        shape(D, block),
        [],
        own,
        core_far,
        chip_far,
        x0,
        ln1_gain,
        grad_middle,
        vmem=8,
        micros=1,
    )
    got_a, got_b = swap(early_a, *move_y), swap(early_b, *move_x)
    if dp_size > 4:
        got, got_a, got_b, input_grad = tie((swap(late, *move_z2), got_a, got_b, input_grad))
        late = far_sum(add(late, got))
    pairs = [jnp.stack([early_a, got_a]), jnp.stack([early_b, got_b])]
    gots = square_swap([late] * 3)
    *gots, got_a, got_b = tie((*gots, swap(pairs[0], *move_x), swap(pairs[1], *move_y)))
    early, late = call(
        gather_kernel,
        "gather_blocks",
        (shape(8, EARLY_ROWS, SHARD_COLS, dtype=BF), late_blocks),
        [],
        pairs[0],
        got_a,
        pairs[1],
        got_b,
        late,
        *gots,
    )
    far_late, far_early = swap(late, *move_core), swap(early, *move_core)
    vector = shape(D)
    g_up, g_down_t, g_out, g_bout, g_ln2_gain, g_ln2_bias, g_bup, g_bdown = call(
        unpack_early_kernel,
        "unpack_early",
        (shape(D, FF), shape(D, FF), shape(D, D), vector, vector, vector, shape(FF), vector),
        [pltpu.VMEM((16, EARLY_ROWS - SHARD_ROWS, SHARD_COLS), F32), pltpu.VMEM((8, FF), F32)],
        early,
        far_early,
    )
    g_qkv, g_bqkv, g_ln1_gain, g_ln1_bias = call(
        unpack_late_kernel,
        "unpack_late",
        (shape(D, 3 * D), shape(3 * D), vector, vector),
        [pltpu.VMEM((D, LATE_COLS), F32), pltpu.VMEM((8, 5 * D), F32)],
        late,
        far_late,
    )
    return (
        output.T[None],
        input_grad.T[None],
        g_ln1_gain,
        g_ln1_bias,
        g_qkv,
        g_bqkv,
        g_out,
        g_bout,
        g_ln2_gain,
        g_ln2_bias,
        g_up,
        g_bup,
        g_down_t.T,
        g_bdown,
    )


def solution(mesh):
    split = P("dp", "seq", None)
    whole = P()
    return jax.shard_map(
        functools.partial(per_device, (mesh.shape["dp"], mesh.shape["seq"])),
        mesh=mesh,
        in_specs=(split, P("dp", None)) + (whole,) * 12 + (split,),
        out_specs=(split, split) + (whole,) * 12,
        check_vma=False,
    )
```

```python
import functools
import math

import jax
import jax.numpy as jnp
from jax import lax
from jax.experimental import pallas as pl
from jax.experimental.pallas import tpu as pltpu
from jax.sharding import PartitionSpec as P

HEADS = 20
HEAD_DIM = 16
D = HEADS * HEAD_DIM
FF = 4 * D
GENES = 4
LANES = 128
TILE_HEADS = LANES // HEAD_DIM
DP = 384
BAR = -1e30
EPS = 1e-05
SHARD_ROWS, SHARD_COLS, EXTRA_ROWS = D // 4, FF // 2, 16
EARLY_ROWS = SHARD_ROWS + EXTRA_ROWS
LATE_DEPTH, LATE_COLS = D // 8, 8 * LANES
LATE_ROWS = LATE_DEPTH * LATE_COLS // SHARD_COLS
SPARE = LATE_COLS - 3 * D
OUT_BLOCKS = D // (2 * EXTRA_ROWS)
PIECES = (range(0, 4), range(4, HEADS))
MIB = 1 << 20
BF = jnp.bfloat16
F32 = jnp.float32
ERF_NUM = (
    -2.72614225801306e-10,
    2.77068142495902e-08,
    -2.10102402082508e-06,
    -5.69250639462346e-05,
    -7.34990630326855e-04,
    -2.95459980854025e-03,
    -1.60960333262415e-02,
)
ERF_DEN = (
    -1.45660718464996e-05,
    -2.13374055278905e-04,
    -1.68282697438203e-03,
    -7.37332916720468e-03,
    -1.42647390514189e-02,
)


def dot(a, b, contract=((1,), (0,))):
    return lax.dot_general(a, b, (contract, ((), ())), preferred_element_type=F32)


def dot_nt(a, b):
    return dot(a, b, ((1,), (1,)))


def dot_tn(a, b):
    return dot(a, b, ((0,), (0,)))


def poly(x, coefficients):
    total = jnp.full_like(x, coefficients[0])
    for entry in coefficients[1:]:
        total = total * x + entry
    return total


def erf(x):
    x = jnp.clip(x, -4.0, 4.0)
    square = x * x
    return x * poly(square, ERF_NUM) / poly(square, ERF_DEN)


def normed(values, axis):
    centered = values - jnp.mean(values, axis=axis, keepdims=True)
    spread = jnp.mean(centered * centered, axis=axis, keepdims=True)
    scale = lax.rsqrt(spread + EPS)
    return centered * scale, scale


def norm_back(grad, normal, scale, gain, axis):
    e = grad * gain
    return scale * (
        e
        - jnp.mean(e, axis=axis, keepdims=True)
        - normal * jnp.mean(e * normal, axis=axis, keepdims=True)
    )


def rotate_rows(values, cosine, sine):
    rows, cols = values.shape
    half = HEAD_DIM // 2
    parts = values.reshape(rows // HEAD_DIM, 2, half, cols)
    first, second = parts[:, 0], parts[:, 1]
    out = jnp.stack([first * cosine - second * sine, second * cosine + first * sine], axis=1)
    return out.reshape(rows, cols)


def pad_rows(values, rows):
    return jnp.concatenate(
        [values, jnp.zeros((rows - values.shape[0], values.shape[1]), values.dtype)], axis=0
    )


def pad_cols(values, cols):
    return jnp.concatenate(
        [values, jnp.zeros((values.shape[0], cols - values.shape[1]), values.dtype)], axis=1
    )


def slots():
    dp, seq = lax.axis_index("dp"), lax.axis_index("seq")
    core, chip_y, chip_x = seq & 1, seq >> 1, dp & 1
    return core * 4 + chip_x * 2 + chip_y, (dp >> 1) & 1, seq


def load_all(sources, targets, sems):
    copies = [
        pltpu.make_async_copy(source, target, sems.at[i])
        for i, (source, target) in enumerate(zip(sources, targets))
    ]
    for copy in copies:
        copy.start()
    return copies


def column(vector):
    return jnp.broadcast_to(vector.reshape(1, -1), (8, vector.shape[0])).T


def prelude_kernel(*refs):
    sources, outs, (local, sems) = refs[:15], refs[15:-6], (refs[-6:-1], refs[-1])
    kept, made = outs[:10], outs[10:]
    copies = load_all(sources, (kept[0], *local, *kept[1:]), sems)
    for copy in copies[:6]:
        copy.wait()
    prelude_body(kept[0], *local, *made)
    for copy in copies[6:]:
        copy.wait()


def prelude_body(
    x0_ref,
    seg_ref,
    ln1_gain_ref,
    ln1_bias_ref,
    wqkv_ref,
    bqkv_ref,
    wqkv_t_ref,
    cols_ref,
    cos_ref,
    sin_ref,
    q_ref,
    qt_ref,
    kt_ref,
    vt_ref,
    ke_ref,
    qe_ref,
):
    block = x0_ref.shape[1]
    length = 4 * block
    seq = slots()[2]
    genes = seg_ref[...]
    begins = [
        jnp.sum((genes < gene).astype(F32), axis=1, keepdims=True) for gene in range(1, GENES)
    ]
    index = lax.broadcasted_iota(jnp.int32, (1, block), 1).astype(F32)
    half = HEAD_DIM // 2
    step = lax.broadcasted_iota(jnp.int32, (half, block), 0).astype(F32)
    frequency = jnp.exp(step * (-2.0 * math.log(10000.0) / HEAD_DIM))
    row = lax.broadcasted_iota(jnp.int32, (LANES, block), 0)
    for distance in range(4):
        cols = slice(distance * block, (distance + 1) * block)
        chunk = seq ^ distance
        own = seg_ref[:, pl.ds(pl.multiple_of(chunk * block, block), block)]
        begin = jnp.zeros((1, block), F32)
        for gene in range(1, GENES):
            begin = jnp.where(own == gene, begins[gene - 1], begin)
        place = index + (chunk * block).astype(F32) - begin
        angle = place * frequency
        cos_ref[:, cols] = jnp.cos(angle)
        sin_ref[:, cols] = jnp.sin(angle)
        table = jnp.where(
            row < GENES, jnp.where(row == own, 0.0, BAR), jnp.where(row < GENES + 3, 1.0, 0.0)
        )
        ke_ref[:, cols] = table.astype(BF)
        if distance == 0:
            qe_ref[...] = jnp.where(row == own, 1.0, 0.0).T.astype(BF)

    wqkv_t_ref[...] = wqkv_ref[...].T
    cols_ref[: 3 * D, :] = column(bqkv_ref[...])
    cols_ref[3 * D : 4 * D, :] = column(ln1_gain_ref[...])
    cols_ref[4 * D :, :] = column(ln1_bias_ref[...])
    normal, _ = normed(x0_ref[...].astype(F32), 0)
    first = (normal * cols_ref[3 * D : 4 * D, 0:1] + cols_ref[4 * D :, 0:1]).astype(BF)
    raw = dot(wqkv_t_ref[...], first) + cols_ref[: 3 * D, 0:1]
    cosine, sine = cos_ref[:, :block], sin_ref[:, :block]
    q_t = rotate_rows(raw[:D], cosine, sine).astype(BF)
    qt_ref[...] = q_t
    q_ref[...] = pad_rows(q_t.astype(F32) * (1.0 / math.sqrt(HEAD_DIM)), DP).T.astype(BF)
    kt_ref[...] = pad_rows(rotate_rows(raw[D : 2 * D], cosine, sine).astype(BF), DP)
    vt_ref[...] = pad_rows(raw[2 * D :].astype(BF), DP)


def forward_kernel(
    x0_ref,
    x1_ref,
    x2_ref,
    x3_ref,
    k0_ref,
    v0_ref,
    q_ref,
    ke_ref,
    qe_ref,
    cos_ref,
    sin_ref,
    wqkv_t_ref,
    cols_ref,
    w_out_ref,
    b_out_ref,
    ln2_gain_ref,
    ln2_bias_ref,
    w_up_ref,
    b_up_ref,
    w_down_t_ref,
    b_down_ref,
    ct_t_ref,
    out_hbm,
    gmid_ref,
    keep_ref,
    send_ref,
    kt_ref,
    vt_ref,
    probs0_ref,
    probs1_ref,
    inner_ref,
    do_ref,
    dot_ref,
    x_all_hbm,
    att_acc,
    xn_ref,
    out_ref,
    sems,
    out_sems,
):
    block = x0_ref.shape[1]
    probs_refs = (probs0_ref, probs1_ref)
    chunks = (x0_ref, x1_ref, x2_ref, x3_ref)
    copies = load_all(chunks, [x_all_hbm.at[i] for i in range(4)], sems)
    gain, bias = cols_ref[3 * D : 4 * D, 0:1], cols_ref[4 * D :, 0:1]
    for index, chunk in enumerate((x1_ref, x2_ref, x3_ref)):
        normal, _ = normed(chunk[...].astype(F32), 0)
        xn_ref[:, index * block : (index + 1) * block] = (normal * gain + bias).astype(BF)
    first = xn_ref[...]
    kt_ref[:, :block] = k0_ref[...]
    vt_ref[:, :block] = v0_ref[...]
    raw = dot(wqkv_t_ref[D:, :], first) + cols_ref[D : 3 * D, 0:1]
    keys = rotate_rows(raw[:D], cos_ref[:, block:], sin_ref[:, block:])
    kt_ref[:, block:] = pad_rows(keys.astype(BF), DP)
    vt_ref[:, block:] = pad_rows(raw[D:].astype(BF), DP)

    lane = lax.broadcasted_iota(jnp.int32, (block, LANES), 1)
    att_acc[...] = jnp.zeros_like(att_acc)
    zero = jnp.zeros((), BF)

    def score(head):
        start = head // TILE_HEADS * LANES
        mask = lane // HEAD_DIM == head % TILE_HEADS
        left = jnp.concatenate(
            [jnp.where(mask, q_ref[:, start : start + LANES], zero), qe_ref[...]], axis=1
        )
        right = jnp.concatenate([kt_ref[start : start + LANES, :], ke_ref[...]], axis=0)
        return head, mask, slice(start, start + LANES), dot(left, right)

    def mix(head, mask, tile, scores):
        weights = jnp.exp(scores - jnp.max(scores, axis=1, keepdims=True))
        share = 1.0 / jnp.sum(weights, axis=1, keepdims=True)
        probs = (weights * share).astype(BF)
        piece = 0 if head in PIECES[0] else 1
        probs_refs[piece][head - PIECES[piece][0]] = probs
        att_acc[:, tile] += jnp.where(mask, dot_nt(probs, vt_ref[tile, :]), 0.0)

    scored = score(0)
    for head in range(1, HEADS):
        ahead = score(head)
        mix(*scored)
        scored = ahead
    mix(*scored)

    def line(ref):
        return ref[...].reshape(1, -1)

    attended_wide = att_acc[:, :D]
    attended = attended_wide.astype(BF)
    middle = x0_ref[...].T.astype(F32) + (dot(attended, w_out_ref[...]) + line(b_out_ref))
    normal2, scale2 = normed(middle, 1)
    gain2 = line(ln2_gain_ref)
    second = (normal2 * gain2 + line(ln2_bias_ref)).astype(BF)
    pre = dot(second, w_up_ref[...]) + line(b_up_ref)
    share = 0.5 + 0.5 * erf(pre * (1.0 / math.sqrt(2.0)))
    active = (pre * share).astype(BF)
    slope = share + pre * (jnp.exp(-0.5 * pre * pre) * (1.0 / math.sqrt(2.0 * math.pi)))
    output = middle + dot_nt(active, w_down_t_ref[...]) + line(b_down_ref)
    out_ref[...] = output.T.astype(BF)
    copies += load_all((out_ref,), (out_hbm,), out_sems)
    ct_t = ct_t_ref[...]
    ct = ct_t.T
    ct_wide = ct.astype(F32)
    grad_pre = (dot(ct, w_down_t_ref[...]) * slope).astype(BF)
    grad_second = dot_nt(grad_pre, w_up_ref[...])
    grad_middle = ct_wide + norm_back(grad_second, normal2, scale2, gain2, 1)
    gmid_ref[...] = grad_middle
    branch = grad_middle.astype(BF)
    grad_att = dot_nt(branch, w_out_ref[...]).astype(BF)
    grad_att_wide = pad_cols(grad_att.astype(F32), DP)
    do_ref[...] = grad_att_wide.astype(BF)
    dot_ref[...] = grad_att_wide.T[:D, :].astype(BF)
    inner_ref[...] = grad_att_wide * att_acc[...]

    grad_up = dot_tn(second, grad_pre).astype(BF)
    grad_down = dot(ct_t, active).astype(BF)
    grad_out = dot_tn(attended, branch)

    def column_sum(values):
        return jnp.sum(values, axis=0, keepdims=True)

    lines = column_sum(grad_pre.astype(F32))
    lines = [
        lines[:, :SHARD_COLS],
        lines[:, SHARD_COLS:],
        jnp.concatenate([column_sum(branch.astype(F32)), column_sum(grad_second * normal2)], axis=1),
        jnp.concatenate([column_sum(grad_second), column_sum(ct_wide)], axis=1),
    ]

    def extra(index):
        if index < OUT_BLOCKS:
            row = 2 * EXTRA_ROWS * index
            upper = grad_out[row : row + EXTRA_ROWS]
            lower = grad_out[row + EXTRA_ROWS : row + 2 * EXTRA_ROWS]
            return jnp.concatenate([upper, lower], axis=1).astype(BF)
        if index < OUT_BLOCKS + len(lines):
            line = lines[index - OUT_BLOCKS]
            return jnp.broadcast_to(line, (EXTRA_ROWS, SHARD_COLS)).astype(BF)
        return jnp.zeros((EXTRA_ROWS, SHARD_COLS), BF)

    slot = slots()[0]
    for index in range(8):
        rows, cols = shard(index)
        stays = index // 4 == slot // 4
        for array, values in enumerate((grad_up, grad_down)):
            block_values = jnp.concatenate([values[rows, cols], extra(8 * array + index)], axis=0)
            store_block(keep_ref, send_ref, stays, ((index ^ slot) % 4, array), block_values)
    for copy in copies:
        copy.wait()


def store_block(keep_ref, send_ref, stays, place, values):
    @pl.when(stays)
    def _():
        keep_ref[place] = values

    @pl.when(jnp.logical_not(stays))
    def _():
        send_ref[place] = values


def shard(index):
    row, col = index % 4 * SHARD_ROWS, index // 4 * SHARD_COLS
    return slice(row, row + SHARD_ROWS), slice(col, col + SHARD_COLS)


def piece_kernel(
    heads,
    loads,
    after_ref,
    cos_ref,
    sin_ref,
    qt_ref,
    kt_ref,
    vt_ref,
    probs_ref,
    inner_ref,
    do_ref,
    dot_ref,
    *refs,
):
    dq_acc, dk_acc, dv_acc, sems = refs[-4:]
    outs = refs[-4 - 3 - loads : -4]
    gq_ref, gk_ref, gv_ref = outs[:3]
    copies = load_all(refs[len(refs) - 4 - 3 - 2 * loads : len(refs) - 4 - 3 - loads], outs[3:], sems)
    block = do_ref.shape[0]
    lane = lax.broadcasted_iota(jnp.int32, (block, LANES), 1)
    first_tile, last_tile = heads[0] // TILE_HEADS, heads[-1] // TILE_HEADS

    def shift(head):
        tile = slice(head // TILE_HEADS * LANES, (head // TILE_HEADS + 1) * LANES)
        mask = lane // HEAD_DIM == head % TILE_HEADS
        left = jnp.where(mask, do_ref[:, tile], jnp.zeros((), BF))
        return head, tile, mask, dot(left, vt_ref[tile, :])

    def finish(head, tile, mask, grad_probs):
        rows = slice(head * HEAD_DIM, (head + 1) * HEAD_DIM)
        here = slice((head - heads[0]) * HEAD_DIM, (head - heads[0] + 1) * HEAD_DIM)
        probs = probs_ref[head - heads[0]]
        inner = jnp.sum(jnp.where(mask, inner_ref[:, tile], 0.0), axis=1, keepdims=True)
        grad_scores = (probs.astype(F32) * (grad_probs - inner)).astype(BF)
        dv_acc[here, :] = dot(dot_ref[rows, :], probs)
        dk_acc[here, :] = dot(qt_ref[rows, :], grad_scores)
        return jnp.where(mask, dot_nt(grad_scores, kt_ref[tile, :]), 0.0)

    totals = {}
    shifted = shift(heads[0])
    for head in heads:
        ahead = shift(head + 1) if head + 1 in heads else None
        index = head // TILE_HEADS - first_tile
        grad_queries = finish(*shifted)
        totals[index] = totals[index] + grad_queries if index in totals else grad_queries
        shifted = ahead
        if ahead is None or ahead[0] // TILE_HEADS - first_tile != index:
            dq_acc[index * LANES : (index + 1) * LANES, :] = totals[index].T

    cosine, sine = cos_ref[...], sin_ref[...]
    scale = 1.0 / math.sqrt(HEAD_DIM)
    rows = slice(heads[0] * HEAD_DIM, (heads[-1] + 1) * HEAD_DIM)
    skip = first_tile * LANES
    dq_t = (dq_acc[rows.start - skip : rows.stop - skip, :] * scale).astype(BF).astype(F32)
    gq_ref[rows, :] = rotate_rows(dq_t, cosine[:, :block], -sine[:, :block]).astype(BF)
    gk_ref[rows, :] = rotate_rows(dk_acc[...] * scale, cosine, -sine).astype(BF)
    gv_ref[rows, :] = dv_acc[...].astype(BF)
    for copy in copies:
        copy.wait()


def projection_kernel(
    after_ref,
    gq_ref,
    gk_ref,
    gv_ref,
    x_ref,
    wqkv_ref,
    ln1_gain_ref,
    ln1_bias_ref,
    keep_ref,
    send_ref,
    own_ref,
    far_ref,
    matrix,
):
    block = x_ref.shape[2]
    length = 4 * block
    ones = jnp.ones((16, length), BF)
    grad_q, grad_k, grad_v = gq_ref[...], gk_ref[...], gv_ref[...]
    sums = [
        dot_nt(ones[:, :block], grad_q)[0:1],
        dot_nt(ones, grad_k)[0:1],
        dot_nt(ones, grad_v)[0:1],
    ]
    gain, bias = column(ln1_gain_ref[...])[:, 0:1], column(ln1_bias_ref[...])[:, 0:1]
    normal = jnp.concatenate([normed(x_ref[i].astype(F32), 0)[0] for i in range(4)], axis=1)
    first = (normal * gain + bias).astype(BF)
    grad_first = dot(wqkv_ref[:, D : 2 * D], grad_k) + dot(wqkv_ref[:, 2 * D :], grad_v)
    own = grad_first[:, :block] + dot(wqkv_ref[:, :D], grad_q)
    own_ref[0] = own
    own_ref[1] = grad_first[:, 2 * block : 3 * block]
    far_ref[0] = grad_first[:, block : 2 * block].astype(BF)
    far_ref[1] = grad_first[:, 3 * block :].astype(BF)
    grad_first = jnp.concatenate([own, grad_first[:, block:]], axis=1)
    matrix[:, :D] = dot_nt(first[:, :block], grad_q)
    matrix[:, D : 2 * D] = dot_nt(first, grad_k)
    matrix[:, 2 * D : 3 * D] = dot_nt(first, grad_v)
    matrix[:, 3 * D :] = jnp.zeros((D, SPARE), F32)
    vectors = jnp.concatenate(
        [
            *sums,
            dot_nt(ones, (grad_first * normal).astype(BF))[0:1],
            dot_nt(ones, grad_first.astype(BF))[0:1],
        ],
        axis=1,
    )
    for index in range(5 * D // SPARE):
        row = index // 4 * LATE_DEPTH + index % 4
        matrix[row : row + 1, 3 * D :] = vectors[:, index * SPARE : (index + 1) * SPARE]
    slot = slots()[0]
    for index in range(8):
        values = pack_late(matrix[index * LATE_DEPTH : (index + 1) * LATE_DEPTH, :]).astype(BF)
        stays = index // 4 == slot // 4
        store_block(keep_ref, send_ref, stays, (index ^ slot) % 4, values)


def pack_late(values):
    tiles = [values[:, i * LANES : (i + 1) * LANES] for i in range(LATE_COLS // LANES)]
    tiles = jnp.concatenate(tiles, axis=0)
    tiles = [tiles[i * LATE_ROWS : (i + 1) * LATE_ROWS] for i in range(SHARD_COLS // LANES)]
    return jnp.concatenate(tiles, axis=1)


def unpack_late(values):
    tiles = [values[:, i * LANES : (i + 1) * LANES] for i in range(SHARD_COLS // LANES)]
    tiles = jnp.concatenate(tiles, axis=0)
    tiles = [tiles[i * LATE_DEPTH : (i + 1) * LATE_DEPTH] for i in range(LATE_COLS // LANES)]
    return jnp.concatenate(tiles, axis=1)


def input_kernel(own_ref, core_ref, chip_ref, x_ref, ln1_gain_ref, gmid_ref, out_ref):
    grad = own_ref[0] + core_ref[0].astype(F32) + chip_ref[...].astype(F32)
    normal, scale = normed(x_ref[...].astype(F32), 0)
    gain = column(ln1_gain_ref[...])[:, 0:1]
    out_ref[...] = gmid_ref[...].T + norm_back(grad, normal, scale, gain, 0)


def plus(first, second):
    return (first.astype(F32) + second.astype(F32)).astype(BF)


def split_kernel(keep_ref, got_ref, *out_refs):
    for index, out_ref in enumerate(out_refs):
        out_ref[...] = plus(keep_ref[index], got_ref[index])


def four(refs):
    first, second, third, fourth = [ref[...].astype(F32) for ref in refs]
    return ((first + second) + (third + fourth)).astype(BF)


def square_kernel(*refs):
    refs[-1][...] = four(refs[:4])


def choose_kernel(*refs):
    kept_ref, send_ref = refs[-2:]
    total = four(refs[:4])
    odd = slots()[1]

    @pl.when(odd == 0)
    def _():
        kept_ref[...] = total[0]
        send_ref[...] = total[1]

    @pl.when(odd == 1)
    def _():
        kept_ref[...] = total[1]
        send_ref[...] = total[0]


def both_kernel(kept_ref, other_ref, a_ref, b_ref):
    odd = slots()[1]

    @pl.when(odd == 0)
    def _():
        a_ref[...] = kept_ref[...]
        b_ref[...] = other_ref[...]

    @pl.when(odd == 1)
    def _():
        a_ref[...] = other_ref[...]
        b_ref[...] = kept_ref[...]


def send_kernel(a_ref, got_a_ref, b_ref, got_b_ref, late_ref, x_ref, y_ref):
    rows = a_ref.shape[0]
    for out_ref, parts in ((x_ref, (a_ref, got_a_ref)), (y_ref, (b_ref, got_b_ref))):
        for index, part_ref in enumerate((*parts, late_ref)):
            out_ref[index * rows : index * rows + part_ref.shape[0], :] = part_ref[...]


def plus_kernel(first_ref, second_ref, *refs):
    refs[-1][...] = plus(first_ref[...], second_ref[...])


def early_rows(array, place):
    return slice((4 * array + place) * EARLY_ROWS, (4 * array + place + 1) * EARLY_ROWS)


def late_rows(place):
    start = 8 * EARLY_ROWS + place * LATE_ROWS
    return slice(start, start + LATE_ROWS)


GATHERED_ROWS = 8 * EARLY_ROWS + 4 * LATE_ROWS


def gather_kernel(own_x_ref, own_y_ref, got_x_ref, got_y_ref, got_xy_ref, out_ref):
    pair = 2 * EARLY_ROWS
    for array, (own_ref, got_ref) in enumerate(((own_x_ref, got_x_ref), (own_y_ref, got_y_ref))):
        start = array * 2 * pair
        out_ref[start : start + pair, :] = own_ref[:pair, :]
        out_ref[start + pair : start + 2 * pair, :] = got_ref[:pair, :]
    out_ref[late_rows(0), :] = own_x_ref[pair:, :]
    out_ref[late_rows(1), :] = got_y_ref[pair:, :]
    out_ref[late_rows(2), :] = got_x_ref[pair:, :]
    out_ref[late_rows(3), :] = got_xy_ref[...]


def place_blocks(core, blocks_ref, up_hbm, down_t_hbm, qkv, spare, extras, values, sems):
    slot = slots()[0]
    copies = []
    for place in range(4):
        row = pl.multiple_of(((core * 4 + place) ^ slot) * LATE_DEPTH, 8)
        block = unpack_late(blocks_ref[late_rows(place), :].astype(F32))
        qkv[pl.ds(row, LATE_DEPTH), :] = block[:, : 3 * D]
        spare[pl.ds(row, LATE_DEPTH), :] = block[:, LATE_COLS - LANES :]
    for array, out_hbm in enumerate((up_hbm, down_t_hbm)):
        for place in range(4):
            which = 4 * array + place
            index = (core * 4 + (place % 2 * 2 + place // 2 if array else place)) ^ slot
            row = pl.multiple_of(index % 4 * SHARD_ROWS, 16)
            col = pl.multiple_of(index // 4 * SHARD_COLS, LANES)
            block = blocks_ref[early_rows(array, place), :].astype(F32)
            values[which] = block[:SHARD_ROWS]
            extras[8 * array + index] = block[SHARD_ROWS:]
            target = out_hbm.at[pl.ds(row, SHARD_ROWS), pl.ds(col, SHARD_COLS)]
            copies.append(pltpu.make_async_copy(values.at[which], target, sems.at[which]))
            copies[-1].start()
    return copies


def unpack_own_kernel(blocks_ref, up_hbm, down_t_hbm, qkv, spare, extras, values, sems):
    for copy in place_blocks(0, blocks_ref, up_hbm, down_t_hbm, qkv, spare, extras, values, sems):
        copy.wait()


def unpack_far_kernel(blocks_ref, own_qkv, own_spare, own_extras, *refs):
    up_hbm, down_t_hbm, qkv, spare, extras, qkv_hbm, out_hbm = refs[2:9]
    vector_hbms, vector_refs = refs[9:17], refs[17:25]
    g_bqkv, g_ln1_gain, g_ln1_bias, g_bup, g_bout, g_ln2_gain, g_ln2_bias, g_bdown = vector_refs
    line, out, values, sems = refs[25:]
    copies = place_blocks(1, blocks_ref, up_hbm, down_t_hbm, qkv, spare, extras, values, sems)
    copies.append(pltpu.make_async_copy(qkv, qkv_hbm, sems.at[8]))
    copies[-1].start()
    for index in range(OUT_BLOCKS):
        row = 2 * EXTRA_ROWS * index
        out[row : row + EXTRA_ROWS, :] = extras[index, :, :D]
        out[row + EXTRA_ROWS : row + 2 * EXTRA_ROWS, :] = extras[index, :, D:]
    copies.append(pltpu.make_async_copy(out, out_hbm, sems.at[9]))
    copies[-1].start()
    for index in range(2):
        cols = slice(index * SHARD_COLS, (index + 1) * SHARD_COLS)
        line[0:1, cols] = extras[OUT_BLOCKS + index, 0:1, :]
    g_bup[...] = line[0:1, :FF].reshape(FF)
    g_bout[...] = extras[OUT_BLOCKS + 2, 0:1, :D].reshape(D)
    g_ln2_gain[...] = extras[OUT_BLOCKS + 2, 0:1, D:].reshape(D)
    g_ln2_bias[...] = extras[OUT_BLOCKS + 3, 0:1, :D].reshape(D)
    g_bdown[...] = extras[OUT_BLOCKS + 3, 0:1, D:].reshape(D)
    for index in range(5 * D // SPARE):
        row = index // 4 * LATE_DEPTH + index % 4
        line[1:2, index * SPARE : (index + 1) * SPARE] = spare[row : row + 1, LANES - SPARE :]
    g_bqkv[...] = line[1:2, : 3 * D].reshape(3 * D)
    g_ln1_gain[...] = line[1:2, 3 * D : 4 * D].reshape(D)
    g_ln1_bias[...] = line[1:2, 4 * D : 5 * D].reshape(D)
    copies += load_all(vector_refs, vector_hbms, sems.at[10:])
    for copy in copies:
        copy.wait()


def call(kernel, name, out_shape, scratch, *operands, vmem=16, loads=(), aliases=None, micros=0):
    operands = list(operands)
    specs = [pl.BlockSpec(memory_space=pltpu.VMEM) for entry in operands]
    operands += [pltpu.with_memory_space_constraint(entry, pltpu.HBM) for entry in loads]
    specs += [pl.BlockSpec(memory_space=pltpu.HBM) for entry in loads]
    return pl.pallas_call(
        kernel,
        name=name,
        out_shape=out_shape,
        in_specs=specs,
        out_specs=jax.tree.map(
            lambda entry: pl.BlockSpec(
                memory_space=pltpu.VMEM if isinstance(entry, jax.ShapeDtypeStruct) else pltpu.HBM
            ),
            out_shape,
        ),
        scratch_shapes=scratch,
        input_output_aliases=aliases or {},
        cost_estimate=pl.CostEstimate(flops=micros * 10**9, bytes_accessed=0, transcendentals=0)
        if micros
        else None,
        compiler_params=pltpu.CompilerParams(vmem_limit_bytes=vmem * MIB),
    )(*operands)


def shape(*dims, dtype=F32):
    return jax.ShapeDtypeStruct(dims, dtype)


def per_device(
    sizes,
    tokens,
    segment_ids,
    ln1_gain,
    ln1_bias,
    w_qkv,
    b_qkv,
    w_out,
    b_out,
    ln2_gain,
    ln2_bias,
    w_up,
    b_up,
    w_down,
    b_down,
    cotangent,
):
    dp_size, seq_size = sizes
    block = tokens.shape[1]
    length = segment_ids.shape[1]
    def swap(value, dp_bits, seq_bits):
        pairs = [
            (a * seq_size + b, (a ^ dp_bits) * seq_size + (b ^ seq_bits))
            for a in range(dp_size)
            for b in range(seq_size)
        ]
        return lax.ppermute(value, ("dp", "seq"), pairs)

    tie = lax.optimization_barrier

    x_t = tokens[0].T
    near = {bits: swap(x_t, 0, bits) for bits in (2, 1)}
    loads = (
        x_t,
        segment_ids,
        ln1_gain,
        ln1_bias,
        w_qkv,
        b_qkv,
        cotangent[0].T,
        w_up,
        w_down.T,
        w_out,
        b_out,
        ln2_gain,
        ln2_bias,
        b_up,
        b_down,
    )
    like = lambda entry: jax.ShapeDtypeStruct(entry.shape, entry.dtype)
    buffer = lambda entry: pltpu.VMEM(entry.shape, entry.dtype)
    out = call(
        prelude_kernel,
        "prelude",
        (like(x_t), *[like(entry) for entry in loads[6:]])
        + (
            shape(3 * D, D, dtype=BF),
            shape(5 * D, 8),
            shape(HEAD_DIM // 2, length),
            shape(HEAD_DIM // 2, length),
            shape(block, DP, dtype=BF),
            shape(D, block, dtype=BF),
            shape(DP, block, dtype=BF),
            shape(DP, block, dtype=BF),
            shape(LANES, length, dtype=BF),
            shape(block, LANES, dtype=BF),
        ),
        [buffer(entry) for entry in loads[1:6]] + [pltpu.SemaphoreType.DMA((len(loads),))],
        loads=loads,
    )
    near[2], *out = tie((near[2], *out))
    near[3] = swap(near[2], 0, 1)
    x0, ct_t, w_up, w_down_t, w_out, b_out, ln2_gain, ln2_bias, b_up, b_down = out[:10]
    wqkv_t, cols, cosine, sine, q, q_t, k_t, v_t, ke, qe = out[10:]
    early_block = shape(2, EARLY_ROWS, SHARD_COLS, dtype=BF)
    blocks = shape(4, *early_block.shape, dtype=BF)
    (output, grad_middle, keep, send, k_t, v_t, *probs, inner, d_out, d_out_t, x_all) = call(
        forward_kernel,
        "layer_forward",
        (
            pltpu.HBM((D, block), BF),
            shape(block, D),
            blocks,
            blocks,
            shape(DP, length, dtype=BF),
            shape(DP, length, dtype=BF),
            *[shape(len(heads), block, length, dtype=BF) for heads in PIECES],
            shape(block, DP),
            shape(block, DP, dtype=BF),
            shape(D, block, dtype=BF),
            pltpu.HBM((4, D, block), BF),
        ),
        [
            pltpu.VMEM((block, DP), F32),
            pltpu.VMEM((D, 3 * block), BF),
            pltpu.VMEM((D, block), BF),
            pltpu.SemaphoreType.DMA((4,)),
            pltpu.SemaphoreType.DMA((1,)),
        ],
        x0,
        near[1],
        near[2],
        near[3],
        k_t,
        v_t,
        q,
        ke,
        qe,
        cosine,
        sine,
        wqkv_t,
        cols,
        w_out,
        b_out,
        ln2_gain,
        ln2_bias,
        w_up,
        b_up,
        w_down_t,
        b_down,
        ct_t,
        vmem=28,
    )

    move_core, move_x, move_y, move_z, move_z2 = (0, 1), (1, 0), (0, 2), (2, 0), (4, 0)

    def add(first_term, second_term, *after):
        return call(plus_kernel, "add", like(first_term), [], first_term, second_term, *after)

    def far_sum(part):
        bit = 8
        while bit < dp_size:
            part = add(part, swap(part, bit, 0))
            bit *= 2
        return part

    def step(piece, after, grads, loads=()):
        operands = (cosine, sine, q_t, k_t, v_t, probs[piece], inner, d_out, d_out_t)
        first = 1 + len(operands)
        heads = PIECES[piece]
        rows = len(heads) * HEAD_DIM
        tiles = heads[-1] // TILE_HEADS - heads[0] // TILE_HEADS + 1
        return call(
            functools.partial(piece_kernel, heads, len(loads)),
            f"attention_backward_{piece}",
            (
                shape(D, block, dtype=BF),
                shape(D, length, dtype=BF),
                shape(D, length, dtype=BF),
                *[like(entry) for entry in loads],
            ),
            [
                pltpu.VMEM((tiles * LANES, block), F32),
                pltpu.VMEM((rows, length), F32),
                pltpu.VMEM((rows, length), F32),
                pltpu.SemaphoreType.DMA((max(1, len(loads)),)),
            ],
            after,
            *operands,
            *grads,
            aliases={first + i: i for i in range(len(grads))},
            loads=loads,
            vmem=28,
        )

    def split(name, keep, got):
        return call(split_kernel, name, (like(keep[0]),) * 4, [], keep, got)

    moves = [move_y, move_x, (1, 2)]

    def square_swap(parts):
        return [swap(part, *move) for part, move in zip(parts, moves)]

    got = swap(send, *move_core)
    got, *grads = tie((got, *step(0, send, ())))
    kept, *sends = split("add_core", keep, got)
    gots = square_swap(sends)
    grads = step(1, sends[2], grads, (x_all, w_qkv, ln1_gain, ln1_bias))
    *gots, first_grad = tie((*gots, grads[0]))
    grads = (first_grad, *grads[1:])
    half = shape(EARLY_ROWS, SHARD_COLS, dtype=BF)
    kept, sent = call(choose_kernel, "add_square", (half, half), [], kept, *gots)
    if dp_size > 2:
        got = swap(sent, *move_z)
    late_blocks = shape(4, LATE_ROWS, SHARD_COLS, dtype=BF)
    late_keep, late_send, own, far = call(
        projection_kernel,
        "projection",
        (late_blocks, late_blocks, shape(2, D, block), shape(2, D, block, dtype=BF)),
        [pltpu.VMEM((D, LATE_COLS), F32)],
        sent,
        *grads,
    )
    if dp_size > 2:
        got, late_send = tie((got, late_send))
        kept = add(kept, got)
    if dp_size > 4:
        got = swap(kept, *move_z2)
    core_far = swap(far, *move_core)
    late, *sends = split("add_late_core", late_keep, swap(late_send, *move_core))
    gots = square_swap(sends)
    late = call(square_kernel, "add_late_square", like(late), [], late, *gots)
    if dp_size > 4:
        got, late = tie((got, late))
        kept = far_sum(add(kept, got))
    other = swap(kept, *move_z) if dp_size > 2 else sent
    late, core_far = tie((late, core_far))
    chip_far = swap(plus(own[1], core_far[1]), *move_y)
    if dp_size > 2:
        got, chip_far = tie((swap(late, *move_z), chip_far))
        late = add(late, got)
    early_a, early_b = call(both_kernel, "early_both", (half, half), [], kept, other)
    input_grad = call(
        input_kernel,
        "input_gradient",
        shape(D, block),
        [],
        own,
        core_far,
        chip_far,
        x0,
        ln1_gain,
        grad_middle,
        vmem=8,
        micros=1,
    )
    got_a, got_b = swap(early_a, *move_y), swap(early_b, *move_x)
    if dp_size > 4:
        got, got_a, got_b, input_grad = tie((swap(late, *move_z2), got_a, got_b, input_grad))
        late = far_sum(add(late, got))
    both = shape(2 * EARLY_ROWS + LATE_ROWS, SHARD_COLS, dtype=BF)
    own_x, own_y = call(
        send_kernel, "send", (both, both), [], early_a, got_a, early_b, got_b, late
    )
    gots = tie((swap(own_x, *move_x), swap(own_y, *move_y), swap(late, 1, 2)))
    gathered = shape(GATHERED_ROWS, SHARD_COLS, dtype=BF)
    blocks = call(gather_kernel, "gather_blocks", gathered, [], own_x, own_y, *gots)
    far_blocks = swap(blocks, *move_core)
    in_hbm = (pltpu.HBM((D, FF), F32), pltpu.HBM((D, FF), F32))
    assembled = (shape(D, 3 * D), shape(D, LANES), shape(16, EXTRA_ROWS, SHARD_COLS))
    values = pltpu.VMEM((8, SHARD_ROWS, SHARD_COLS), F32)
    g_up, g_down_t, *own_parts = call(
        unpack_own_kernel,
        "unpack_own",
        (*in_hbm, *assembled),
        [values, pltpu.SemaphoreType.DMA((8,))],
        blocks,
    )
    sizes = (3 * D, D, D, FF, D, D, D, D)
    vectors = [pltpu.HBM((size,), F32) for size in sizes]
    g_up, g_down_t, _, _, _, g_qkv, g_out, *vectors = call(
        unpack_far_kernel,
        "unpack_far",
        (*in_hbm, *assembled, pltpu.HBM((D, 3 * D), F32), pltpu.HBM((D, D), F32), *vectors),
        [
            *[pltpu.VMEM((size,), F32) for size in sizes],
            pltpu.VMEM((8, 5 * D), F32),
            pltpu.VMEM((D, D), F32),
            values,
            pltpu.SemaphoreType.DMA((18,)),
        ],
        far_blocks,
        *own_parts,
        loads=(g_up, g_down_t),
        aliases={4: 0, 5: 1, 1: 2, 2: 3, 3: 4},
    )
    g_bqkv, g_ln1_gain, g_ln1_bias, g_bup, g_bout, g_ln2_gain, g_ln2_bias, g_bdown = vectors
    return (
        output.T[None],
        input_grad.T[None],
        g_ln1_gain,
        g_ln1_bias,
        g_qkv,
        g_bqkv,
        g_out,
        g_bout,
        g_ln2_gain,
        g_ln2_bias,
        g_up,
        g_bup,
        g_down_t.T,
        g_bdown,
    )


def solution(mesh):
    split = P("dp", "seq", None)
    whole = P()
    return jax.shard_map(
        functools.partial(per_device, (mesh.shape["dp"], mesh.shape["seq"])),
        mesh=mesh,
        in_specs=(split, P("dp", None)) + (whole,) * 12 + (split,),
        out_specs=(split, split) + (whole,) * 12,
        check_vma=False,
    )
```

```python
import functools
import math

import jax
import jax.numpy as jnp
from jax import lax
from jax.experimental import pallas as pl
from jax.experimental.pallas import tpu as pltpu
from jax.sharding import PartitionSpec as P

HEADS = 20
HEAD_DIM = 16
D = HEADS * HEAD_DIM
FF = 4 * D
GENES = 4
LANES = 128
TILE_HEADS = LANES // HEAD_DIM
DP = 384
BAR = -1e30
SAFE = 40.0
EPS = 1e-05
SHARD_ROWS, SHARD_COLS, EXTRA_ROWS = D // 4, FF // 2, 16
EARLY_ROWS = SHARD_ROWS + EXTRA_ROWS
LATE_DEPTH, LATE_COLS = D // 8, 8 * LANES
LATE_ROWS = LATE_DEPTH * LATE_COLS // SHARD_COLS
SPARE = LATE_COLS - 3 * D
OUT_BLOCKS = D // (2 * EXTRA_ROWS)
PIECES = (range(HEADS),)
MIB = 1 << 20
BF = jnp.bfloat16
F32 = jnp.float32
ERF_NUM = (
    -2.72614225801306e-10,
    2.77068142495902e-08,
    -2.10102402082508e-06,
    -5.69250639462346e-05,
    -7.34990630326855e-04,
    -2.95459980854025e-03,
    -1.60960333262415e-02,
)
ERF_DEN = (
    -1.45660718464996e-05,
    -2.13374055278905e-04,
    -1.68282697438203e-03,
    -7.37332916720468e-03,
    -1.42647390514189e-02,
)


def dot(a, b, contract=((1,), (0,))):
    return lax.dot_general(a, b, (contract, ((), ())), preferred_element_type=F32)


def dot_nt(a, b):
    return dot(a, b, ((1,), (1,)))


def dot_tn(a, b):
    return dot(a, b, ((0,), (0,)))


def poly(x, coefficients):
    total = jnp.full_like(x, coefficients[0])
    for entry in coefficients[1:]:
        total = total * x + entry
    return total


def erf(x):
    x = jnp.clip(x, -4.0, 4.0)
    square = x * x
    return x * poly(square, ERF_NUM) / poly(square, ERF_DEN)


def normed(values, axis):
    centered = values - jnp.mean(values, axis=axis, keepdims=True)
    spread = jnp.mean(centered * centered, axis=axis, keepdims=True)
    scale = lax.rsqrt(spread + EPS)
    return centered * scale, scale


def norm_back(grad, normal, scale, gain, axis):
    e = grad * gain
    return scale * (
        e
        - jnp.mean(e, axis=axis, keepdims=True)
        - normal * jnp.mean(e * normal, axis=axis, keepdims=True)
    )


def rotate_rows(values, cosine, sine):
    rows, cols = values.shape
    half = HEAD_DIM // 2
    parts = values.reshape(rows // HEAD_DIM, 2, half, cols)
    first, second = parts[:, 0], parts[:, 1]
    out = jnp.stack([first * cosine - second * sine, second * cosine + first * sine], axis=1)
    return out.reshape(rows, cols)


def pad_rows(values, rows):
    return jnp.concatenate(
        [values, jnp.zeros((rows - values.shape[0], values.shape[1]), values.dtype)], axis=0
    )


def pad_cols(values, cols):
    return jnp.concatenate(
        [values, jnp.zeros((values.shape[0], cols - values.shape[1]), values.dtype)], axis=1
    )


def slots():
    dp, seq = lax.axis_index("dp"), lax.axis_index("seq")
    core, chip_y, chip_x = seq & 1, seq >> 1, dp & 1
    return core * 4 + chip_x * 2 + chip_y, (dp >> 1) & 1, seq


def load_all(sources, targets, sems):
    copies = [
        pltpu.make_async_copy(source, target, sems.at[i])
        for i, (source, target) in enumerate(zip(sources, targets))
    ]
    for copy in copies:
        copy.start()
    return copies


def column(vector):
    return jnp.broadcast_to(vector.reshape(1, -1), (8, vector.shape[0])).T


def prelude_kernel(*refs):
    sources, outs, (local, sems) = refs[:15], refs[15:-6], (refs[-6:-1], refs[-1])
    kept, made = outs[:10], outs[10:]
    copies = load_all(sources, (kept[0], *local, *kept[1:]), sems)
    for copy in copies[:6]:
        copy.wait()
    prelude_body(kept[0], *local, *made)
    for copy in copies[6:]:
        copy.wait()


def prelude_body(
    x0_ref,
    seg_ref,
    ln1_gain_ref,
    ln1_bias_ref,
    wqkv_ref,
    bqkv_ref,
    wqkv_t_ref,
    cols_ref,
    cos_ref,
    sin_ref,
    q_ref,
    qt_ref,
    kt_ref,
    vt_ref,
    ke_ref,
    qe_ref,
):
    block = x0_ref.shape[1]
    length = 4 * block
    seq = slots()[2]
    genes = seg_ref[...]
    begins = [
        jnp.sum((genes < gene).astype(F32), axis=1, keepdims=True) for gene in range(1, GENES)
    ]
    index = lax.broadcasted_iota(jnp.int32, (1, block), 1).astype(F32)
    half = HEAD_DIM // 2
    step = lax.broadcasted_iota(jnp.int32, (half, block), 0).astype(F32)
    frequency = jnp.exp(step * (-2.0 * math.log(10000.0) / HEAD_DIM))
    row = lax.broadcasted_iota(jnp.int32, (LANES, block), 0)
    for distance in range(4):
        cols = slice(distance * block, (distance + 1) * block)
        chunk = seq ^ distance
        own = seg_ref[:, pl.ds(pl.multiple_of(chunk * block, block), block)]
        begin = jnp.zeros((1, block), F32)
        for gene in range(1, GENES):
            begin = jnp.where(own == gene, begins[gene - 1], begin)
        place = index + (chunk * block).astype(F32) - begin
        angle = place * frequency
        cos_ref[:, cols] = jnp.cos(angle)
        sin_ref[:, cols] = jnp.sin(angle)
        table = jnp.where(
            row < GENES, jnp.where(row == own, 0.0, BAR), jnp.where(row < GENES + 3, 1.0, 0.0)
        )
        ke_ref[:, cols] = table.astype(BF)
        if distance == 0:
            qe_ref[...] = jnp.where(row == own, 1.0, 0.0).T.astype(BF)

    wqkv_t_ref[...] = wqkv_ref[...].T
    cols_ref[: 3 * D, :] = column(bqkv_ref[...])
    cols_ref[3 * D : 4 * D, :] = column(ln1_gain_ref[...])
    cols_ref[4 * D :, :] = column(ln1_bias_ref[...])
    normal, _ = normed(x0_ref[...].astype(F32), 0)
    first = (normal * cols_ref[3 * D : 4 * D, 0:1] + cols_ref[4 * D :, 0:1]).astype(BF)
    raw = dot(wqkv_t_ref[...], first) + cols_ref[: 3 * D, 0:1]
    cosine, sine = cos_ref[:, :block], sin_ref[:, :block]
    q_t = rotate_rows(raw[:D], cosine, sine).astype(BF)
    qt_ref[...] = q_t
    q_ref[...] = pad_rows(q_t.astype(F32) * (1.0 / math.sqrt(HEAD_DIM)), DP).T.astype(BF)
    kt_ref[...] = pad_rows(rotate_rows(raw[D : 2 * D], cosine, sine).astype(BF), DP)
    vt_ref[...] = pad_rows(raw[2 * D :].astype(BF), DP)


def forward_kernel(
    x0_ref,
    x1_ref,
    x2_ref,
    x3_ref,
    k0_ref,
    v0_ref,
    q_ref,
    qt_ref,
    ke_ref,
    qe_ref,
    cos_ref,
    sin_ref,
    wqkv_t_ref,
    cols_ref,
    w_out_ref,
    b_out_ref,
    ln2_gain_ref,
    ln2_bias_ref,
    w_up_ref,
    b_up_ref,
    w_down_t_ref,
    ct_t_ref,
    gmid_ref,
    keep_ref,
    send_ref,
    kt_ref,
    vt_ref,
    probs_ref,
    branch_ref,
    middle_ref,
    active_ref,
    att_acc,
    share_ref,
    x_all_hbm,
    xn_ref,
    sems,
):
    block = x0_ref.shape[1]
    chunks = (x0_ref, x1_ref, x2_ref, x3_ref)
    copies = load_all(chunks, [x_all_hbm.at[i] for i in range(4)], sems)
    gain, bias = cols_ref[3 * D : 4 * D, 0:1], cols_ref[4 * D :, 0:1]
    for index, chunk in enumerate((x1_ref, x2_ref, x3_ref)):
        normal, _ = normed(chunk[...].astype(F32), 0)
        xn_ref[:, index * block : (index + 1) * block] = (normal * gain + bias).astype(BF)
    first = xn_ref[...]
    kt_ref[:, :block] = k0_ref[...]
    vt_ref[:, :block] = v0_ref[...]
    raw = dot(wqkv_t_ref[D:, :], first) + cols_ref[D : 3 * D, 0:1]
    keys = rotate_rows(raw[:D], cos_ref[:, block:], sin_ref[:, block:])
    kt_ref[:, block:] = pad_rows(keys.astype(BF), DP)
    vt_ref[:, block:] = pad_rows(raw[D:].astype(BF), DP)

    lane = lax.broadcasted_iota(jnp.int32, (block, LANES), 1)
    att_acc[...] = jnp.zeros_like(att_acc)
    share_ref[...] = jnp.ones_like(share_ref)
    zero = jnp.zeros((), BF)

    def largest(values):
        squares = jnp.square(values).reshape(HEADS, HEAD_DIM, values.shape[1])
        return jnp.max(jnp.sum(squares, axis=1), axis=1, keepdims=True)

    key_sizes = jnp.maximum(largest(keys), largest(k0_ref[:D, :].astype(F32)))
    bound = jnp.max(largest(qt_ref[...].astype(F32)) * key_sizes, axis=0, keepdims=True)
    safe = bound[0, 0] * (1.02 / HEAD_DIM) < SAFE * SAFE

    def score(head, start):
        mask = lane // HEAD_DIM == head % TILE_HEADS
        left = jnp.concatenate(
            [jnp.where(mask, q_ref[:, pl.ds(start, LANES)], zero), qe_ref[...]], axis=1
        )
        right = jnp.concatenate([kt_ref[pl.ds(start, LANES), :], ke_ref[...]], axis=0)
        return mask, dot(left, right)

    def mix(start, mask, scores, head):
        tile = pl.ds(start, LANES)
        weights = jnp.exp(scores)
        mass = jnp.sum(weights, axis=1, keepdims=True)
        probs_ref[head] = weights.astype(BF)
        att_acc[:, tile] += jnp.where(mask, dot_nt(weights.astype(BF), vt_ref[tile, :]), 0.0)
        share_ref[:, tile] = jnp.where(mask, mass, share_ref[:, tile])

    @pl.when(safe)
    def _():
        scored = score(0, 0)
        for head in range(HEADS):
            ahead = score(head + 1, (head + 1) // TILE_HEADS * LANES) if head + 1 < HEADS else None
            mix(head // TILE_HEADS * LANES, *scored, head)
            scored = ahead

    @pl.when(jnp.logical_not(safe))
    def _():
        def attend(head, carry):
            start = pl.multiple_of(head // TILE_HEADS * LANES, LANES)
            mask, scores = score(head, start)
            scores = scores - jnp.max(scores, axis=1, keepdims=True)
            mix(start, mask, scores, head)
            return carry

        lax.fori_loop(0, HEADS, attend, 0, unroll=4)

    def line(ref):
        return ref[...].reshape(1, -1)

    share_ref[...] = 1.0 / share_ref[...]
    att_acc[...] = att_acc[...] * share_ref[...]
    attended = att_acc[:, :D].astype(BF)
    middle = x0_ref[...].T.astype(F32) + (dot(attended, w_out_ref[...]) + line(b_out_ref))
    normal2, scale2 = normed(middle, 1)
    gain2 = line(ln2_gain_ref)
    second = (normal2 * gain2 + line(ln2_bias_ref)).astype(BF)
    pre = dot(second, w_up_ref[...]) + line(b_up_ref)
    share = 0.5 + 0.5 * erf(pre * (1.0 / math.sqrt(2.0)))
    active = (pre * share).astype(BF)
    slope = share + pre * (jnp.exp(-0.5 * pre * pre) * (1.0 / math.sqrt(2.0 * math.pi)))
    middle_ref[...] = middle
    active_ref[...] = active
    ct_t = ct_t_ref[...]
    ct = ct_t.T
    ct_wide = ct.astype(F32)
    grad_pre = (dot(ct, w_down_t_ref[...]) * slope).astype(BF)
    grad_second = dot_nt(grad_pre, w_up_ref[...])
    grad_middle = ct_wide + norm_back(grad_second, normal2, scale2, gain2, 1)
    gmid_ref[...] = grad_middle
    branch = grad_middle.astype(BF)
    branch_ref[...] = branch

    grad_up = dot_tn(second, grad_pre).astype(BF)
    grad_down = dot(ct_t, active).astype(BF)
    grad_out = dot_tn(attended, branch)

    def column_sum(values):
        return jnp.sum(values, axis=0, keepdims=True)

    lines = column_sum(grad_pre.astype(F32))
    lines = [
        lines[:, :SHARD_COLS],
        lines[:, SHARD_COLS:],
        jnp.concatenate([column_sum(branch.astype(F32)), column_sum(grad_second * normal2)], axis=1),
        jnp.concatenate([column_sum(grad_second), column_sum(ct_wide)], axis=1),
    ]

    def extra(index):
        if index < OUT_BLOCKS:
            row = 2 * EXTRA_ROWS * index
            upper = grad_out[row : row + EXTRA_ROWS]
            lower = grad_out[row + EXTRA_ROWS : row + 2 * EXTRA_ROWS]
            return jnp.concatenate([upper, lower], axis=1).astype(BF)
        if index < OUT_BLOCKS + len(lines):
            line = lines[index - OUT_BLOCKS]
            return jnp.broadcast_to(line, (EXTRA_ROWS, SHARD_COLS)).astype(BF)
        return jnp.zeros((EXTRA_ROWS, SHARD_COLS), BF)

    slot = slots()[0]
    for index in range(8):
        rows, cols = shard(index)
        stays = index // 4 == slot // 4
        for array, values in enumerate((grad_up, grad_down)):
            block_values = jnp.concatenate([values[rows, cols], extra(8 * array + index)], axis=0)
            store_block(keep_ref, send_ref, stays, ((index ^ slot) % 4, array), block_values)
    for copy in copies:
        copy.wait()


def finish_kernel(
    branch_ref,
    att_ref,
    share_ref,
    w_out_ref,
    middle_ref,
    active_ref,
    w_down_t_ref,
    b_down_ref,
    do_ref,
    dot_ref,
    inner_ref,
    out_hbm,
    out_ref,
    sems,
):
    output = middle_ref[...] + dot_nt(active_ref[...], w_down_t_ref[...])
    output = output + b_down_ref[...].reshape(1, -1)
    out_ref[...] = output.T.astype(BF)
    (copy,) = load_all((out_ref,), (out_hbm,), sems)
    grad_att = dot_nt(branch_ref[...], w_out_ref[...]).astype(BF)
    grad_att_wide = pad_cols(grad_att.astype(F32), DP)
    do_ref[...] = grad_att_wide.astype(BF)
    dot_ref[...] = (grad_att_wide * share_ref[...]).T[:D, :].astype(BF)
    inner_ref[...] = grad_att_wide * att_ref[...]
    copy.wait()


def store_block(keep_ref, send_ref, stays, place, values):
    @pl.when(stays)
    def _():
        keep_ref[place] = values

    @pl.when(jnp.logical_not(stays))
    def _():
        send_ref[place] = values


def shard(index):
    row, col = index % 4 * SHARD_ROWS, index // 4 * SHARD_COLS
    return slice(row, row + SHARD_ROWS), slice(col, col + SHARD_COLS)


def piece_kernel(
    heads,
    loads,
    after_ref,
    cos_ref,
    sin_ref,
    qt_ref,
    kt_ref,
    vt_ref,
    probs_ref,
    share_ref,
    inner_ref,
    do_ref,
    dot_ref,
    *refs,
):
    dq_acc, dk_acc, dv_acc, sems = refs[-4:]
    outs = refs[-4 - 3 - loads : -4]
    gq_ref, gk_ref, gv_ref = outs[:3]
    copies = load_all(refs[len(refs) - 4 - 3 - 2 * loads : len(refs) - 4 - 3 - loads], outs[3:], sems)
    block = do_ref.shape[0]
    lane = lax.broadcasted_iota(jnp.int32, (block, LANES), 1)
    first_tile, last_tile = heads[0] // TILE_HEADS, heads[-1] // TILE_HEADS

    def shift(head):
        tile = slice(head // TILE_HEADS * LANES, (head // TILE_HEADS + 1) * LANES)
        mask = lane // HEAD_DIM == head % TILE_HEADS
        left = jnp.where(mask, do_ref[:, tile], jnp.zeros((), BF))
        return head, tile, mask, dot(left, vt_ref[tile, :])

    def finish(head, tile, mask, grad_probs):
        rows = slice(head * HEAD_DIM, (head + 1) * HEAD_DIM)
        here = slice((head - heads[0]) * HEAD_DIM, (head - heads[0] + 1) * HEAD_DIM)
        probs = probs_ref[head - heads[0]]
        share = share_ref[:, rows.start : rows.start + 1]
        inner = jnp.sum(jnp.where(mask, inner_ref[:, tile], 0.0), axis=1, keepdims=True)
        grad_scores = (probs.astype(F32) * ((grad_probs - inner) * share)).astype(BF)
        dv_acc[here, :] = dot(dot_ref[rows, :], probs)
        dk_acc[here, :] = dot(qt_ref[rows, :], grad_scores)
        return jnp.where(mask, dot_nt(grad_scores, kt_ref[tile, :]), 0.0)

    totals = {}
    shifted = shift(heads[0])
    for head in heads:
        ahead = shift(head + 1) if head + 1 in heads else None
        index = head // TILE_HEADS - first_tile
        grad_queries = finish(*shifted)
        totals[index] = totals[index] + grad_queries if index in totals else grad_queries
        shifted = ahead
        if ahead is None or ahead[0] // TILE_HEADS - first_tile != index:
            dq_acc[index * LANES : (index + 1) * LANES, :] = totals[index].T

    cosine, sine = cos_ref[...], sin_ref[...]
    scale = 1.0 / math.sqrt(HEAD_DIM)
    rows = slice(heads[0] * HEAD_DIM, (heads[-1] + 1) * HEAD_DIM)
    skip = first_tile * LANES
    dq_t = (dq_acc[rows.start - skip : rows.stop - skip, :] * scale).astype(BF).astype(F32)
    gq_ref[rows, :] = rotate_rows(dq_t, cosine[:, :block], -sine[:, :block]).astype(BF)
    gk_ref[rows, :] = rotate_rows(dk_acc[...] * scale, cosine, -sine).astype(BF)
    gv_ref[rows, :] = dv_acc[...].astype(BF)
    for copy in copies:
        copy.wait()


def projection_kernel(
    after_ref,
    gq_ref,
    gk_ref,
    gv_ref,
    x_ref,
    wqkv_ref,
    ln1_gain_ref,
    ln1_bias_ref,
    keep_ref,
    send_ref,
    own_ref,
    far_ref,
    matrix,
):
    block = x_ref.shape[2]
    length = 4 * block
    ones = jnp.ones((16, length), BF)
    grad_q, grad_k, grad_v = gq_ref[...], gk_ref[...], gv_ref[...]
    sums = [
        dot_nt(ones[:, :block], grad_q)[0:1],
        dot_nt(ones, grad_k)[0:1],
        dot_nt(ones, grad_v)[0:1],
    ]
    gain, bias = column(ln1_gain_ref[...])[:, 0:1], column(ln1_bias_ref[...])[:, 0:1]
    normal = jnp.concatenate([normed(x_ref[i].astype(F32), 0)[0] for i in range(4)], axis=1)
    first = (normal * gain + bias).astype(BF)
    grad_first = dot(wqkv_ref[:, D : 2 * D], grad_k) + dot(wqkv_ref[:, 2 * D :], grad_v)
    own = grad_first[:, :block] + dot(wqkv_ref[:, :D], grad_q)
    own_ref[0] = own
    own_ref[1] = grad_first[:, 2 * block : 3 * block]
    far_ref[0] = grad_first[:, block : 2 * block].astype(BF)
    far_ref[1] = grad_first[:, 3 * block :].astype(BF)
    grad_first = jnp.concatenate([own, grad_first[:, block:]], axis=1)
    matrix[:, :D] = dot_nt(first[:, :block], grad_q)
    matrix[:, D : 2 * D] = dot_nt(first, grad_k)
    matrix[:, 2 * D : 3 * D] = dot_nt(first, grad_v)
    matrix[:, 3 * D :] = jnp.zeros((D, SPARE), F32)
    vectors = jnp.concatenate(
        [
            *sums,
            dot_nt(ones, (grad_first * normal).astype(BF))[0:1],
            dot_nt(ones, grad_first.astype(BF))[0:1],
        ],
        axis=1,
    )
    for index in range(5 * D // SPARE):
        row = index // 4 * LATE_DEPTH + index % 4
        matrix[row : row + 1, 3 * D :] = vectors[:, index * SPARE : (index + 1) * SPARE]
    slot = slots()[0]
    for index in range(8):
        values = pack_late(matrix[index * LATE_DEPTH : (index + 1) * LATE_DEPTH, :]).astype(BF)
        stays = index // 4 == slot // 4
        store_block(keep_ref, send_ref, stays, (index ^ slot) % 4, values)


def pack_late(values):
    tiles = [values[:, i * LANES : (i + 1) * LANES] for i in range(LATE_COLS // LANES)]
    tiles = jnp.concatenate(tiles, axis=0)
    tiles = [tiles[i * LATE_ROWS : (i + 1) * LATE_ROWS] for i in range(SHARD_COLS // LANES)]
    return jnp.concatenate(tiles, axis=1)


def unpack_late(values):
    tiles = [values[:, i * LANES : (i + 1) * LANES] for i in range(SHARD_COLS // LANES)]
    tiles = jnp.concatenate(tiles, axis=0)
    tiles = [tiles[i * LATE_DEPTH : (i + 1) * LATE_DEPTH] for i in range(LATE_COLS // LANES)]
    return jnp.concatenate(tiles, axis=1)


def input_kernel(own_ref, core_ref, chip_ref, x_ref, ln1_gain_ref, gmid_ref, out_ref):
    grad = own_ref[0] + core_ref[0].astype(F32) + chip_ref[...].astype(F32)
    normal, scale = normed(x_ref[...].astype(F32), 0)
    gain = column(ln1_gain_ref[...])[:, 0:1]
    out_ref[...] = gmid_ref[...].T + norm_back(grad, normal, scale, gain, 0)


def plus(first, second):
    return (first.astype(F32) + second.astype(F32)).astype(BF)


def split_kernel(keep_ref, got_ref, *out_refs):
    for index, out_ref in enumerate(out_refs):
        out_ref[...] = plus(keep_ref[index], got_ref[index])


def four(refs):
    first, second, third, fourth = [ref[...].astype(F32) for ref in refs]
    return ((first + second) + (third + fourth)).astype(BF)


def square_kernel(*refs):
    refs[-1][...] = four(refs[:4])


def choose_kernel(*refs):
    kept_ref, send_ref = refs[-2:]
    total = four(refs[:4])
    odd = slots()[1]

    @pl.when(odd == 0)
    def _():
        kept_ref[...] = total[0]
        send_ref[...] = total[1]

    @pl.when(odd == 1)
    def _():
        kept_ref[...] = total[1]
        send_ref[...] = total[0]


def both_kernel(kept_ref, other_ref, a_ref, b_ref):
    odd = slots()[1]

    @pl.when(odd == 0)
    def _():
        a_ref[...] = kept_ref[...]
        b_ref[...] = other_ref[...]

    @pl.when(odd == 1)
    def _():
        a_ref[...] = other_ref[...]
        b_ref[...] = kept_ref[...]


def send_kernel(a_ref, got_a_ref, b_ref, got_b_ref, late_ref, x_ref, y_ref):
    rows = a_ref.shape[0]
    for out_ref, parts in ((x_ref, (a_ref, got_a_ref)), (y_ref, (b_ref, got_b_ref))):
        for index, part_ref in enumerate((*parts, late_ref)):
            out_ref[index * rows : index * rows + part_ref.shape[0], :] = part_ref[...]


def plus_kernel(first_ref, second_ref, *refs):
    refs[-1][...] = plus(first_ref[...], second_ref[...])


def early_rows(array, place):
    return slice((4 * array + place) * EARLY_ROWS, (4 * array + place + 1) * EARLY_ROWS)


def late_rows(place):
    start = 8 * EARLY_ROWS + place * LATE_ROWS
    return slice(start, start + LATE_ROWS)


GATHERED_ROWS = 8 * EARLY_ROWS + 4 * LATE_ROWS


def gather_kernel(own_x_ref, own_y_ref, got_x_ref, got_y_ref, got_xy_ref, out_ref):
    pair = 2 * EARLY_ROWS
    for array, (own_ref, got_ref) in enumerate(((own_x_ref, got_x_ref), (own_y_ref, got_y_ref))):
        start = array * 2 * pair
        out_ref[start : start + pair, :] = own_ref[:pair, :]
        out_ref[start + pair : start + 2 * pair, :] = got_ref[:pair, :]
    out_ref[late_rows(0), :] = own_x_ref[pair:, :]
    out_ref[late_rows(1), :] = got_y_ref[pair:, :]
    out_ref[late_rows(2), :] = got_x_ref[pair:, :]
    out_ref[late_rows(3), :] = got_xy_ref[...]


def place_blocks(core, blocks_ref, up_hbm, down_t_hbm, qkv, spare, extras, values, sems):
    slot = slots()[0]
    copies = []
    for place in range(4):
        row = pl.multiple_of(((core * 4 + place) ^ slot) * LATE_DEPTH, 8)
        block = unpack_late(blocks_ref[late_rows(place), :].astype(F32))
        qkv[pl.ds(row, LATE_DEPTH), :] = block[:, : 3 * D]
        spare[pl.ds(row, LATE_DEPTH), :] = block[:, LATE_COLS - LANES :]
    for array, out_hbm in enumerate((up_hbm, down_t_hbm)):
        for place in range(4):
            which = 4 * array + place
            index = (core * 4 + (place % 2 * 2 + place // 2 if array else place)) ^ slot
            row = pl.multiple_of(index % 4 * SHARD_ROWS, 16)
            col = pl.multiple_of(index // 4 * SHARD_COLS, LANES)
            block = blocks_ref[early_rows(array, place), :].astype(F32)
            values[which] = block[:SHARD_ROWS]
            extras[8 * array + index] = block[SHARD_ROWS:]
            target = out_hbm.at[pl.ds(row, SHARD_ROWS), pl.ds(col, SHARD_COLS)]
            copies.append(pltpu.make_async_copy(values.at[which], target, sems.at[which]))
            copies[-1].start()
    return copies


def unpack_own_kernel(blocks_ref, up_hbm, down_t_hbm, qkv, spare, extras, values, sems):
    for copy in place_blocks(0, blocks_ref, up_hbm, down_t_hbm, qkv, spare, extras, values, sems):
        copy.wait()


def unpack_far_kernel(blocks_ref, own_qkv, own_spare, own_extras, *refs):
    up_hbm, down_t_hbm, qkv, spare, extras, qkv_hbm, out_hbm = refs[2:9]
    vector_hbms, vector_refs = refs[9:17], refs[17:25]
    g_bqkv, g_ln1_gain, g_ln1_bias, g_bup, g_bout, g_ln2_gain, g_ln2_bias, g_bdown = vector_refs
    line, out, values, sems = refs[25:]
    copies = place_blocks(1, blocks_ref, up_hbm, down_t_hbm, qkv, spare, extras, values, sems)
    copies.append(pltpu.make_async_copy(qkv, qkv_hbm, sems.at[8]))
    copies[-1].start()
    for index in range(OUT_BLOCKS):
        row = 2 * EXTRA_ROWS * index
        out[row : row + EXTRA_ROWS, :] = extras[index, :, :D]
        out[row + EXTRA_ROWS : row + 2 * EXTRA_ROWS, :] = extras[index, :, D:]
    copies.append(pltpu.make_async_copy(out, out_hbm, sems.at[9]))
    copies[-1].start()
    for index in range(2):
        cols = slice(index * SHARD_COLS, (index + 1) * SHARD_COLS)
        line[0:1, cols] = extras[OUT_BLOCKS + index, 0:1, :]
    g_bup[...] = line[0:1, :FF].reshape(FF)
    g_bout[...] = extras[OUT_BLOCKS + 2, 0:1, :D].reshape(D)
    g_ln2_gain[...] = extras[OUT_BLOCKS + 2, 0:1, D:].reshape(D)
    g_ln2_bias[...] = extras[OUT_BLOCKS + 3, 0:1, :D].reshape(D)
    g_bdown[...] = extras[OUT_BLOCKS + 3, 0:1, D:].reshape(D)
    for index in range(5 * D // SPARE):
        row = index // 4 * LATE_DEPTH + index % 4
        line[1:2, index * SPARE : (index + 1) * SPARE] = spare[row : row + 1, LANES - SPARE :]
    g_bqkv[...] = line[1:2, : 3 * D].reshape(3 * D)
    g_ln1_gain[...] = line[1:2, 3 * D : 4 * D].reshape(D)
    g_ln1_bias[...] = line[1:2, 4 * D : 5 * D].reshape(D)
    copies += load_all(vector_refs, vector_hbms, sems.at[10:])
    for copy in copies:
        copy.wait()


def call(kernel, name, out_shape, scratch, *operands, vmem=16, loads=(), aliases=None, micros=0):
    operands = list(operands)
    specs = [pl.BlockSpec(memory_space=pltpu.VMEM) for entry in operands]
    operands += [pltpu.with_memory_space_constraint(entry, pltpu.HBM) for entry in loads]
    specs += [pl.BlockSpec(memory_space=pltpu.HBM) for entry in loads]
    return pl.pallas_call(
        kernel,
        name=name,
        out_shape=out_shape,
        in_specs=specs,
        out_specs=jax.tree.map(
            lambda entry: pl.BlockSpec(
                memory_space=pltpu.VMEM if isinstance(entry, jax.ShapeDtypeStruct) else pltpu.HBM
            ),
            out_shape,
        ),
        scratch_shapes=scratch,
        input_output_aliases=aliases or {},
        cost_estimate=pl.CostEstimate(flops=micros * 10**9, bytes_accessed=0, transcendentals=0)
        if micros
        else None,
        compiler_params=pltpu.CompilerParams(vmem_limit_bytes=vmem * MIB),
    )(*operands)


def shape(*dims, dtype=F32):
    return jax.ShapeDtypeStruct(dims, dtype)


def per_device(
    sizes,
    tokens,
    segment_ids,
    ln1_gain,
    ln1_bias,
    w_qkv,
    b_qkv,
    w_out,
    b_out,
    ln2_gain,
    ln2_bias,
    w_up,
    b_up,
    w_down,
    b_down,
    cotangent,
):
    dp_size, seq_size = sizes
    block = tokens.shape[1]
    length = segment_ids.shape[1]
    def swap(value, dp_bits, seq_bits):
        pairs = [
            (a * seq_size + b, (a ^ dp_bits) * seq_size + (b ^ seq_bits))
            for a in range(dp_size)
            for b in range(seq_size)
        ]
        return lax.ppermute(value, ("dp", "seq"), pairs)

    tie = lax.optimization_barrier

    x_t = tokens[0].T
    near = {bits: swap(x_t, 0, bits) for bits in (2, 1)}
    loads = (
        x_t,
        segment_ids,
        ln1_gain,
        ln1_bias,
        w_qkv,
        b_qkv,
        cotangent[0].T,
        w_up,
        w_down.T,
        w_out,
        b_out,
        ln2_gain,
        ln2_bias,
        b_up,
        b_down,
    )
    like = lambda entry: jax.ShapeDtypeStruct(entry.shape, entry.dtype)
    buffer = lambda entry: pltpu.VMEM(entry.shape, entry.dtype)
    out = call(
        prelude_kernel,
        "prelude",
        (like(x_t), *[like(entry) for entry in loads[6:]])
        + (
            shape(3 * D, D, dtype=BF),
            shape(5 * D, 8),
            shape(HEAD_DIM // 2, length),
            shape(HEAD_DIM // 2, length),
            shape(block, DP, dtype=BF),
            shape(D, block, dtype=BF),
            shape(DP, block, dtype=BF),
            shape(DP, block, dtype=BF),
            shape(LANES, length, dtype=BF),
            shape(block, LANES, dtype=BF),
        ),
        [buffer(entry) for entry in loads[1:6]] + [pltpu.SemaphoreType.DMA((len(loads),))],
        loads=loads,
    )
    near[2], *out = tie((near[2], *out))
    near[3] = swap(near[2], 0, 1)
    x0, ct_t, w_up, w_down_t, w_out, b_out, ln2_gain, ln2_bias, b_up, b_down = out[:10]
    wqkv_t, cols, cosine, sine, q, q_t, k_t, v_t, ke, qe = out[10:]
    early_block = shape(2, EARLY_ROWS, SHARD_COLS, dtype=BF)
    blocks = shape(4, *early_block.shape, dtype=BF)
    grad_middle, keep, send, k_t, v_t, probs, branch, middle, active, attended, share, x_all = call(
        forward_kernel,
        "layer_forward",
        (
            shape(block, D),
            blocks,
            blocks,
            shape(DP, length, dtype=BF),
            shape(DP, length, dtype=BF),
            shape(HEADS, block, length, dtype=BF),
            shape(block, D, dtype=BF),
            shape(block, D),
            shape(block, FF, dtype=BF),
            shape(block, DP),
            shape(block, DP),
            pltpu.HBM((4, D, block), BF),
        ),
        [pltpu.VMEM((D, 3 * block), BF), pltpu.SemaphoreType.DMA((4,))],
        x0,
        near[1],
        near[2],
        near[3],
        k_t,
        v_t,
        q,
        q_t,
        ke,
        qe,
        cosine,
        sine,
        wqkv_t,
        cols,
        w_out,
        b_out,
        ln2_gain,
        ln2_bias,
        w_up,
        b_up,
        w_down_t,
        ct_t,
        vmem=28,
    )

    move_core, move_x, move_y, move_z, move_z2 = (0, 1), (1, 0), (0, 2), (2, 0), (4, 0)

    def add(first_term, second_term, *after):
        return call(plus_kernel, "add", like(first_term), [], first_term, second_term, *after)

    def far_sum(part):
        bit = 8
        while bit < dp_size:
            part = add(part, swap(part, bit, 0))
            bit *= 2
        return part

    def step(piece, after, grads, loads=()):
        operands = (cosine, sine, q_t, k_t, v_t, probs, share, inner, d_out, d_out_t)
        first = 1 + len(operands)
        heads = PIECES[piece]
        rows = len(heads) * HEAD_DIM
        tiles = heads[-1] // TILE_HEADS - heads[0] // TILE_HEADS + 1
        return call(
            functools.partial(piece_kernel, heads, len(loads)),
            f"attention_backward_{piece}",
            (
                shape(D, block, dtype=BF),
                shape(D, length, dtype=BF),
                shape(D, length, dtype=BF),
                *[like(entry) for entry in loads],
            ),
            [
                pltpu.VMEM((tiles * LANES, block), F32),
                pltpu.VMEM((rows, length), F32),
                pltpu.VMEM((rows, length), F32),
                pltpu.SemaphoreType.DMA((max(1, len(loads)),)),
            ],
            after,
            *operands,
            *grads,
            aliases={first + i: i for i in range(len(grads))},
            loads=loads,
            vmem=28,
        )

    def split(name, keep, got):
        return call(split_kernel, name, (like(keep[0]),) * 4, [], keep, got)

    moves = [move_y, move_x, (1, 2)]

    def square_swap(parts):
        return [swap(part, *move) for part, move in zip(parts, moves)]

    got = swap(send, *move_core)
    d_out, d_out_t, inner, output = call(
        finish_kernel,
        "layer_finish",
        (
            shape(block, DP, dtype=BF),
            shape(D, block, dtype=BF),
            shape(block, DP),
            pltpu.HBM((D, block), BF),
        ),
        [pltpu.VMEM((D, block), BF), pltpu.SemaphoreType.DMA((1,))],
        branch,
        attended,
        share,
        w_out,
        middle,
        active,
        w_down_t,
        b_down,
    )
    got, d_out = tie((got, d_out))
    kept, *sends = split("add_core", keep, got)
    gots = square_swap(sends)
    grads = step(0, sends[2], (), (x_all, w_qkv, ln1_gain, ln1_bias))
    *gots, first_grad = tie((*gots, grads[0]))
    grads = (first_grad, *grads[1:])
    half = shape(EARLY_ROWS, SHARD_COLS, dtype=BF)
    kept, sent = call(choose_kernel, "add_square", (half, half), [], kept, *gots)
    if dp_size > 2:
        got = swap(sent, *move_z)
    late_blocks = shape(4, LATE_ROWS, SHARD_COLS, dtype=BF)
    late_keep, late_send, own, far = call(
        projection_kernel,
        "projection",
        (late_blocks, late_blocks, shape(2, D, block), shape(2, D, block, dtype=BF)),
        [pltpu.VMEM((D, LATE_COLS), F32)],
        sent,
        *grads,
    )
    if dp_size > 2:
        got, late_send = tie((got, late_send))
        kept = add(kept, got)
    if dp_size > 4:
        got = swap(kept, *move_z2)
    core_far = swap(far, *move_core)
    late, *sends = split("add_late_core", late_keep, swap(late_send, *move_core))
    gots = square_swap(sends)
    if dp_size > 4:
        got, gots[0], gots[2] = tie((got, gots[0], gots[2]))
        kept = far_sum(add(kept, got))
    late = call(square_kernel, "add_late_square", like(late), [], late, *gots)
    other = swap(kept, *move_z) if dp_size > 2 else sent
    late, core_far = tie((late, core_far))
    chip_far = swap(plus(own[1], core_far[1]), *move_y)
    if dp_size > 2:
        got, chip_far = tie((swap(late, *move_z), chip_far))
        late = add(late, got)
    early_a, early_b = call(both_kernel, "early_both", (half, half), [], kept, other)
    input_grad = call(
        input_kernel,
        "input_gradient",
        shape(D, block),
        [],
        own,
        core_far,
        chip_far,
        x0,
        ln1_gain,
        grad_middle,
        vmem=8,
        micros=1,
    )
    got_a, got_b = swap(early_a, *move_y), swap(early_b, *move_x)
    if dp_size > 4:
        got, got_a, got_b, input_grad = tie((swap(late, *move_z2), got_a, got_b, input_grad))
        late = far_sum(add(late, got))
    both = shape(2 * EARLY_ROWS + LATE_ROWS, SHARD_COLS, dtype=BF)
    own_x, own_y = call(
        send_kernel, "send", (both, both), [], early_a, got_a, early_b, got_b, late
    )
    gots = tie((swap(own_x, *move_x), swap(own_y, *move_y), swap(late, 1, 2)))
    gathered = shape(GATHERED_ROWS, SHARD_COLS, dtype=BF)
    blocks = call(gather_kernel, "gather_blocks", gathered, [], own_x, own_y, *gots)
    far_blocks = swap(blocks, *move_core)
    in_hbm = (pltpu.HBM((D, FF), F32), pltpu.HBM((D, FF), F32))
    assembled = (shape(D, 3 * D), shape(D, LANES), shape(16, EXTRA_ROWS, SHARD_COLS))
    values = pltpu.VMEM((8, SHARD_ROWS, SHARD_COLS), F32)
    g_up, g_down_t, *own_parts = call(
        unpack_own_kernel,
        "unpack_own",
        (*in_hbm, *assembled),
        [values, pltpu.SemaphoreType.DMA((8,))],
        blocks,
    )
    sizes = (3 * D, D, D, FF, D, D, D, D)
    vectors = [pltpu.HBM((size,), F32) for size in sizes]
    g_up, g_down_t, _, _, _, g_qkv, g_out, *vectors = call(
        unpack_far_kernel,
        "unpack_far",
        (*in_hbm, *assembled, pltpu.HBM((D, 3 * D), F32), pltpu.HBM((D, D), F32), *vectors),
        [
            *[pltpu.VMEM((size,), F32) for size in sizes],
            pltpu.VMEM((8, 5 * D), F32),
            pltpu.VMEM((D, D), F32),
            values,
            pltpu.SemaphoreType.DMA((18,)),
        ],
        far_blocks,
        *own_parts,
        loads=(g_up, g_down_t),
        aliases={4: 0, 5: 1, 1: 2, 2: 3, 3: 4},
    )
    g_bqkv, g_ln1_gain, g_ln1_bias, g_bup, g_bout, g_ln2_gain, g_ln2_bias, g_bdown = vectors
    return (
        output.T[None],
        input_grad.T[None],
        g_ln1_gain,
        g_ln1_bias,
        g_qkv,
        g_bqkv,
        g_out,
        g_bout,
        g_ln2_gain,
        g_ln2_bias,
        g_up,
        g_bup,
        g_down_t.T,
        g_bdown,
    )


def solution(mesh):
    split = P("dp", "seq", None)
    whole = P()
    return jax.shard_map(
        functools.partial(per_device, (mesh.shape["dp"], mesh.shape["seq"])),
        mesh=mesh,
        in_specs=(split, P("dp", None)) + (whole,) * 12 + (split,),
        out_specs=(split, split) + (whole,) * 12,
        check_vma=False,
    )
```

```python
import functools
import math

import jax
import jax.numpy as jnp
from jax import lax
from jax.experimental import pallas as pl
from jax.experimental.pallas import tpu as pltpu
from jax.sharding import PartitionSpec as P

HEADS = 20
HEAD_DIM = 16
D = HEADS * HEAD_DIM
FF = 4 * D
GENES = 4
LANES = 128
TILE_HEADS = LANES // HEAD_DIM
DP = 384
BAR = -1e30
SAFE = 40.0
EPS = 1e-05
SHARD_ROWS, SHARD_COLS, EXTRA_ROWS = D // 4, FF // 2, 16
EARLY_ROWS = SHARD_ROWS + EXTRA_ROWS
LATE_DEPTH, LATE_COLS = D // 8, 8 * LANES
LATE_ROWS = LATE_DEPTH * LATE_COLS // SHARD_COLS
SPARE = LATE_COLS - 3 * D
OUT_BLOCKS = D // (2 * EXTRA_ROWS)
PIECES = (range(HEADS),)
MIB = 1 << 20
BF = jnp.bfloat16
F32 = jnp.float32
ERFC_P = 0.3275911
ERFC = (1.061405429, -1.453152027, 1.421413741, -0.284496736, 0.254829592)


def dot(a, b, contract=((1,), (0,))):
    return lax.dot_general(a, b, (contract, ((), ())), preferred_element_type=F32)


def dot_nt(a, b):
    return dot(a, b, ((1,), (1,)))


def dot_tn(a, b):
    return dot(a, b, ((0,), (0,)))


def normal_cdf(x):
    bell = jnp.exp(-0.5 * x * x)
    t = 1.0 / (1.0 + (ERFC_P / math.sqrt(2.0)) * jnp.abs(x))
    tail = jnp.full_like(x, 0.5 * ERFC[0])
    for entry in ERFC[1:]:
        tail = tail * t + 0.5 * entry
    tail = tail * t * bell
    return jnp.where(x < 0.0, tail, 1.0 - tail), bell


def normed(values, axis):
    centered = values - jnp.mean(values, axis=axis, keepdims=True)
    spread = jnp.mean(centered * centered, axis=axis, keepdims=True)
    scale = lax.rsqrt(spread + EPS)
    return centered * scale, scale


def norm_back(grad, normal, scale, gain, axis):
    e = grad * gain
    return scale * (
        e
        - jnp.mean(e, axis=axis, keepdims=True)
        - normal * jnp.mean(e * normal, axis=axis, keepdims=True)
    )


def rotate_rows(values, cosine, sine):
    rows, cols = values.shape
    half = HEAD_DIM // 2
    parts = values.reshape(rows // HEAD_DIM, 2, half, cols)
    first, second = parts[:, 0], parts[:, 1]
    out = jnp.stack([first * cosine - second * sine, second * cosine + first * sine], axis=1)
    return out.reshape(rows, cols)


def pad_rows(values, rows):
    return jnp.concatenate(
        [values, jnp.zeros((rows - values.shape[0], values.shape[1]), values.dtype)], axis=0
    )


def pad_cols(values, cols):
    return jnp.concatenate(
        [values, jnp.zeros((values.shape[0], cols - values.shape[1]), values.dtype)], axis=1
    )


def slots():
    dp, seq = lax.axis_index("dp"), lax.axis_index("seq")
    core, chip_y, chip_x = seq & 1, seq >> 1, dp & 1
    return core * 4 + chip_x * 2 + chip_y, (dp >> 1) & 1, seq


def load_all(sources, targets, sems):
    copies = [
        pltpu.make_async_copy(source, target, sems.at[i])
        for i, (source, target) in enumerate(zip(sources, targets))
    ]
    for copy in copies:
        copy.start()
    return copies


def column(vector):
    return jnp.broadcast_to(vector.reshape(1, -1), (8, vector.shape[0])).T


def prelude_kernel(*refs):
    sources, outs, (local, sems) = refs[:14], refs[14:-6], (refs[-6:-1], refs[-1])
    kept, made = outs[:9], outs[9:]
    copies = load_all(sources, (kept[0], *local, *kept[1:]), sems)
    for copy in copies[:6]:
        copy.wait()
    prelude_body(kept[0], *local, *made)
    for copy in copies[6:]:
        copy.wait()


def prelude_body(
    x0_ref,
    seg_ref,
    ln1_gain_ref,
    ln1_bias_ref,
    wqkv_ref,
    bqkv_ref,
    wqkv_t_ref,
    cols_ref,
    cos_ref,
    sin_ref,
    q_ref,
    qt_ref,
    kt_ref,
    vt_ref,
    ke_ref,
    qe_ref,
):
    block = x0_ref.shape[1]
    length = 4 * block
    seq = slots()[2]
    genes = seg_ref[...]
    begins = [
        jnp.sum((genes < gene).astype(F32), axis=1, keepdims=True) for gene in range(1, GENES)
    ]
    index = lax.broadcasted_iota(jnp.int32, (1, block), 1).astype(F32)
    half = HEAD_DIM // 2
    step = lax.broadcasted_iota(jnp.int32, (half, block), 0).astype(F32)
    frequency = jnp.exp(step * (-2.0 * math.log(10000.0) / HEAD_DIM))
    row = lax.broadcasted_iota(jnp.int32, (LANES, block), 0)
    for distance in range(4):
        cols = slice(distance * block, (distance + 1) * block)
        chunk = seq ^ distance
        own = seg_ref[:, pl.ds(pl.multiple_of(chunk * block, block), block)]
        begin = jnp.zeros((1, block), F32)
        for gene in range(1, GENES):
            begin = jnp.where(own == gene, begins[gene - 1], begin)
        place = index + (chunk * block).astype(F32) - begin
        angle = place * frequency
        cos_ref[:, cols] = jnp.cos(angle)
        sin_ref[:, cols] = jnp.sin(angle)
        table = jnp.where(
            row < GENES, jnp.where(row == own, 0.0, BAR), jnp.where(row < GENES + 3, 1.0, 0.0)
        )
        ke_ref[:, cols] = table.astype(BF)
        if distance == 0:
            qe_ref[...] = jnp.where(row == own, 1.0, 0.0).T.astype(BF)

    wqkv_t_ref[...] = wqkv_ref[...].T
    cols_ref[: 3 * D, :] = column(bqkv_ref[...])
    cols_ref[3 * D : 4 * D, :] = column(ln1_gain_ref[...])
    cols_ref[4 * D :, :] = column(ln1_bias_ref[...])
    normal, _ = normed(x0_ref[...].astype(F32), 0)
    first = (normal * cols_ref[3 * D : 4 * D, 0:1] + cols_ref[4 * D :, 0:1]).astype(BF)
    raw = dot(wqkv_t_ref[...], first) + cols_ref[: 3 * D, 0:1]
    cosine, sine = cos_ref[:, :block], sin_ref[:, :block]
    q_t = rotate_rows(raw[:D], cosine, sine).astype(BF)
    qt_ref[...] = q_t
    q_ref[...] = pad_rows(q_t.astype(F32) * (1.0 / math.sqrt(HEAD_DIM)), DP).T.astype(BF)
    kt_ref[...] = pad_rows(rotate_rows(raw[D : 2 * D], cosine, sine).astype(BF), DP)
    vt_ref[...] = pad_rows(raw[2 * D :].astype(BF), DP)


def forward_kernel(
    x0_ref,
    x1_ref,
    x2_ref,
    x3_ref,
    k0_ref,
    v0_ref,
    q_ref,
    qt_ref,
    ke_ref,
    qe_ref,
    cos_ref,
    sin_ref,
    wqkv_t_ref,
    cols_ref,
    w_out_ref,
    b_out_ref,
    ln2_gain_ref,
    ln2_bias_ref,
    w_up_ref,
    b_up_ref,
    w_down_t_ref,
    ct_t_ref,
    gmid_ref,
    keep_ref,
    send0_ref,
    send1_ref,
    send2_ref,
    send3_ref,
    kt_ref,
    vt_ref,
    probs_ref,
    branch_ref,
    att_acc,
    share_ref,
    x_all_hbm,
    middle_hbm,
    active_hbm,
    xn_ref,
    middle_ref,
    active_ref,
    sems,
    out_sems,
):
    block = x0_ref.shape[1]
    send_refs = (send0_ref, send1_ref, send2_ref, send3_ref)
    chunks = (x0_ref, x1_ref, x2_ref, x3_ref)
    copies = load_all(chunks, [x_all_hbm.at[i] for i in range(4)], sems)
    gain, bias = cols_ref[3 * D : 4 * D, 0:1], cols_ref[4 * D :, 0:1]
    for index, chunk in enumerate((x1_ref, x2_ref, x3_ref)):
        normal, _ = normed(chunk[...].astype(F32), 0)
        xn_ref[:, index * block : (index + 1) * block] = (normal * gain + bias).astype(BF)
    first = xn_ref[...]
    kt_ref[:, :block] = k0_ref[...]
    vt_ref[:, :block] = v0_ref[...]
    raw = dot(wqkv_t_ref[D:, :], first) + cols_ref[D : 3 * D, 0:1]
    keys = rotate_rows(raw[:D], cos_ref[:, block:], sin_ref[:, block:])
    kt_ref[:, block:] = pad_rows(keys.astype(BF), DP)
    vt_ref[:, block:] = pad_rows(raw[D:].astype(BF), DP)

    lane = lax.broadcasted_iota(jnp.int32, (block, LANES), 1)
    att_acc[...] = jnp.zeros_like(att_acc)
    share_ref[...] = jnp.ones_like(share_ref)
    zero = jnp.zeros((), BF)

    def largest(values):
        squares = jnp.square(values).reshape(HEADS, HEAD_DIM, values.shape[1])
        return jnp.max(jnp.sum(squares, axis=1), axis=1, keepdims=True)

    key_sizes = jnp.maximum(largest(keys), largest(k0_ref[:D, :].astype(F32)))
    bound = jnp.max(largest(qt_ref[...].astype(F32)) * key_sizes, axis=0, keepdims=True)
    safe = bound[0, 0] * (1.02 / HEAD_DIM) < SAFE * SAFE

    def score(head, start):
        mask = lane // HEAD_DIM == head % TILE_HEADS
        left = jnp.concatenate(
            [jnp.where(mask, q_ref[:, pl.ds(start, LANES)], zero), qe_ref[...]], axis=1
        )
        right = jnp.concatenate([kt_ref[pl.ds(start, LANES), :], ke_ref[...]], axis=0)
        return mask, dot(left, right)

    def mix(start, mask, scores, head):
        tile = pl.ds(start, LANES)
        weights = jnp.exp(scores)
        mass = jnp.sum(weights, axis=1, keepdims=True)
        probs_ref[head] = weights.astype(BF)
        att_acc[:, tile] += jnp.where(mask, dot_nt(weights.astype(BF), vt_ref[tile, :]), 0.0)
        share_ref[:, tile] = jnp.where(mask, mass, share_ref[:, tile])

    @pl.when(safe)
    def _():
        scored = score(0, 0)
        for head in range(HEADS):
            ahead = score(head + 1, (head + 1) // TILE_HEADS * LANES) if head + 1 < HEADS else None
            mix(head // TILE_HEADS * LANES, *scored, head)
            scored = ahead

    @pl.when(jnp.logical_not(safe))
    def _():
        def attend(head, carry):
            start = pl.multiple_of(head // TILE_HEADS * LANES, LANES)
            mask, scores = score(head, start)
            scores = scores - jnp.max(scores, axis=1, keepdims=True)
            mix(start, mask, scores, head)
            return carry

        lax.fori_loop(0, HEADS, attend, 0, unroll=4)

    def line(ref):
        return ref[...].reshape(1, -1)

    share_ref[...] = 1.0 / share_ref[...]
    att_acc[...] = att_acc[...] * share_ref[...]
    attended = att_acc[:, :D].astype(BF)
    middle = x0_ref[...].T.astype(F32) + (dot(attended, w_out_ref[...]) + line(b_out_ref))
    normal2, scale2 = normed(middle, 1)
    gain2 = line(ln2_gain_ref)
    second = (normal2 * gain2 + line(ln2_bias_ref)).astype(BF)
    pre = dot(second, w_up_ref[...]) + line(b_up_ref)
    share, bell = normal_cdf(pre)
    active = (pre * share).astype(BF)
    slope = share + pre * (bell * (1.0 / math.sqrt(2.0 * math.pi)))
    middle_ref[...] = middle
    active_ref[...] = active
    copies += load_all((middle_ref, active_ref), (middle_hbm, active_hbm), out_sems)
    ct_t = ct_t_ref[...]
    ct = ct_t.T
    ct_wide = ct.astype(F32)
    grad_pre = (dot(ct, w_down_t_ref[...]) * slope).astype(BF)
    grad_second = dot_nt(grad_pre, w_up_ref[...])
    grad_middle = ct_wide + norm_back(grad_second, normal2, scale2, gain2, 1)
    gmid_ref[...] = grad_middle
    branch = grad_middle.astype(BF)
    branch_ref[...] = branch

    grad_up = dot_tn(second, grad_pre).astype(BF)
    grad_down = dot(ct_t, active).astype(BF)
    grad_out = dot_tn(attended, branch)

    def column_sum(values):
        return jnp.sum(values, axis=0, keepdims=True)

    lines = column_sum(grad_pre.astype(F32))
    lines = [
        lines[:, :SHARD_COLS],
        lines[:, SHARD_COLS:],
        jnp.concatenate([column_sum(branch.astype(F32)), column_sum(grad_second * normal2)], axis=1),
        jnp.concatenate([column_sum(grad_second), column_sum(ct_wide)], axis=1),
    ]

    def extra(index):
        if index < OUT_BLOCKS:
            row = 2 * EXTRA_ROWS * index
            upper = grad_out[row : row + EXTRA_ROWS]
            lower = grad_out[row + EXTRA_ROWS : row + 2 * EXTRA_ROWS]
            return jnp.concatenate([upper, lower], axis=1).astype(BF)
        if index < OUT_BLOCKS + len(lines):
            line = lines[index - OUT_BLOCKS]
            return jnp.broadcast_to(line, (EXTRA_ROWS, SHARD_COLS)).astype(BF)
        return jnp.zeros((EXTRA_ROWS, SHARD_COLS), BF)

    slot = slots()[0]
    for index in range(8):
        rows, cols = shard(index)
        stays = index // 4 == slot // 4
        for array, values in enumerate((grad_up, grad_down)):
            block_values = jnp.concatenate([values[rows, cols], extra(8 * array + index)], axis=0)
            place = (index ^ slot) % 4
            store_parts(keep_ref, send_refs, stays, place, array, block_values)
    for copy in copies:
        copy.wait()


def finish_kernel(branch_ref, att_ref, share_ref, w_out_ref, do_ref, dot_ref, inner_ref):
    grad_att = dot_nt(branch_ref[...], w_out_ref[...]).astype(BF)
    grad_att_wide = pad_cols(grad_att.astype(F32), DP)
    do_ref[...] = grad_att_wide.astype(BF)
    dot_ref[...] = (grad_att_wide * share_ref[...]).T[:D, :].astype(BF)
    inner_ref[...] = grad_att_wide * att_ref[...]


def store_parts(keep_ref, send_refs, stays, place, array, values):
    @pl.when(stays)
    def _():
        keep_ref[place, array] = values

    for index, send_ref in enumerate(send_refs):

        @pl.when(jnp.logical_and(jnp.logical_not(stays), place == index))
        def _():
            send_ref[array] = values


def store_block(keep_ref, send_ref, stays, place, values):
    @pl.when(stays)
    def _():
        keep_ref[place] = values

    @pl.when(jnp.logical_not(stays))
    def _():
        send_ref[place] = values


def shard(index):
    row, col = index % 4 * SHARD_ROWS, index // 4 * SHARD_COLS
    return slice(row, row + SHARD_ROWS), slice(col, col + SHARD_COLS)


def piece_kernel(
    heads,
    loads,
    after_ref,
    cos_ref,
    sin_ref,
    qt_ref,
    kt_ref,
    vt_ref,
    probs_ref,
    share_ref,
    inner_ref,
    do_ref,
    dot_ref,
    *refs,
):
    dq_acc, dk_acc, dv_acc, sems = refs[-4:]
    outs = refs[-4 - 3 - loads : -4]
    gq_ref, gk_ref, gv_ref = outs[:3]
    copies = load_all(refs[len(refs) - 4 - 3 - 2 * loads : len(refs) - 4 - 3 - loads], outs[3:], sems)
    block = do_ref.shape[0]
    lane = lax.broadcasted_iota(jnp.int32, (block, LANES), 1)
    first_tile, last_tile = heads[0] // TILE_HEADS, heads[-1] // TILE_HEADS

    def shift(head):
        tile = slice(head // TILE_HEADS * LANES, (head // TILE_HEADS + 1) * LANES)
        mask = lane // HEAD_DIM == head % TILE_HEADS
        left = jnp.where(mask, do_ref[:, tile], jnp.zeros((), BF))
        return head, tile, mask, dot(left, vt_ref[tile, :])

    def finish(head, tile, mask, grad_probs):
        rows = slice(head * HEAD_DIM, (head + 1) * HEAD_DIM)
        here = slice((head - heads[0]) * HEAD_DIM, (head - heads[0] + 1) * HEAD_DIM)
        probs = probs_ref[head - heads[0]]
        share = share_ref[:, rows.start : rows.start + 1]
        inner = jnp.sum(jnp.where(mask, inner_ref[:, tile], 0.0), axis=1, keepdims=True)
        grad_scores = (probs.astype(F32) * ((grad_probs - inner) * share)).astype(BF)
        dv_acc[here, :] = dot(dot_ref[rows, :], probs)
        dk_acc[here, :] = dot(qt_ref[rows, :], grad_scores)
        return jnp.where(mask, dot_nt(grad_scores, kt_ref[tile, :]), 0.0)

    totals = {}
    shifted = shift(heads[0])
    for head in heads:
        ahead = shift(head + 1) if head + 1 in heads else None
        index = head // TILE_HEADS - first_tile
        grad_queries = finish(*shifted)
        totals[index] = totals[index] + grad_queries if index in totals else grad_queries
        shifted = ahead
        if ahead is None or ahead[0] // TILE_HEADS - first_tile != index:
            dq_acc[index * LANES : (index + 1) * LANES, :] = totals[index].T

    cosine, sine = cos_ref[...], sin_ref[...]
    scale = 1.0 / math.sqrt(HEAD_DIM)
    rows = slice(heads[0] * HEAD_DIM, (heads[-1] + 1) * HEAD_DIM)
    skip = first_tile * LANES
    dq_t = (dq_acc[rows.start - skip : rows.stop - skip, :] * scale).astype(BF).astype(F32)
    gq_ref[rows, :] = rotate_rows(dq_t, cosine[:, :block], -sine[:, :block]).astype(BF)
    gk_ref[rows, :] = rotate_rows(dk_acc[...] * scale, cosine, -sine).astype(BF)
    gv_ref[rows, :] = dv_acc[...].astype(BF)
    for copy in copies:
        copy.wait()


def projection_kernel(
    after_ref,
    gq_ref,
    gk_ref,
    gv_ref,
    x_ref,
    wqkv_ref,
    ln1_gain_ref,
    ln1_bias_ref,
    keep_ref,
    send_ref,
    own_ref,
    far_ref,
    matrix,
):
    block = x_ref.shape[2]
    length = 4 * block
    ones = jnp.ones((16, length), BF)
    grad_q, grad_k, grad_v = gq_ref[...], gk_ref[...], gv_ref[...]
    sums = [
        dot_nt(ones[:, :block], grad_q)[0:1],
        dot_nt(ones, grad_k)[0:1],
        dot_nt(ones, grad_v)[0:1],
    ]
    gain, bias = column(ln1_gain_ref[...])[:, 0:1], column(ln1_bias_ref[...])[:, 0:1]
    normal = jnp.concatenate([normed(x_ref[i].astype(F32), 0)[0] for i in range(4)], axis=1)
    first = (normal * gain + bias).astype(BF)
    grad_first = dot(wqkv_ref[:, D : 2 * D], grad_k) + dot(wqkv_ref[:, 2 * D :], grad_v)
    own = grad_first[:, :block] + dot(wqkv_ref[:, :D], grad_q)
    own_ref[0] = own
    own_ref[1] = grad_first[:, 2 * block : 3 * block]
    far_ref[0] = grad_first[:, block : 2 * block].astype(BF)
    far_ref[1] = grad_first[:, 3 * block :].astype(BF)
    grad_first = jnp.concatenate([own, grad_first[:, block:]], axis=1)
    matrix[:, :D] = dot_nt(first[:, :block], grad_q)
    matrix[:, D : 2 * D] = dot_nt(first, grad_k)
    matrix[:, 2 * D : 3 * D] = dot_nt(first, grad_v)
    matrix[:, 3 * D :] = jnp.zeros((D, SPARE), F32)
    vectors = jnp.concatenate(
        [
            *sums,
            dot_nt(ones, (grad_first * normal).astype(BF))[0:1],
            dot_nt(ones, grad_first.astype(BF))[0:1],
        ],
        axis=1,
    )
    for index in range(5 * D // SPARE):
        row = index // 4 * LATE_DEPTH + index % 4
        matrix[row : row + 1, 3 * D :] = vectors[:, index * SPARE : (index + 1) * SPARE]
    slot = slots()[0]
    for index in range(8):
        values = pack_late(matrix[index * LATE_DEPTH : (index + 1) * LATE_DEPTH, :]).astype(BF)
        stays = index // 4 == slot // 4
        store_block(keep_ref, send_ref, stays, (index ^ slot) % 4, values)


def pack_late(values):
    tiles = [values[:, i * LANES : (i + 1) * LANES] for i in range(LATE_COLS // LANES)]
    tiles = jnp.concatenate(tiles, axis=0)
    tiles = [tiles[i * LATE_ROWS : (i + 1) * LATE_ROWS] for i in range(SHARD_COLS // LANES)]
    return jnp.concatenate(tiles, axis=1)


def unpack_late(values):
    tiles = [values[:, i * LANES : (i + 1) * LANES] for i in range(SHARD_COLS // LANES)]
    tiles = jnp.concatenate(tiles, axis=0)
    tiles = [tiles[i * LATE_DEPTH : (i + 1) * LATE_DEPTH] for i in range(LATE_COLS // LANES)]
    return jnp.concatenate(tiles, axis=1)


def input_kernel(own_ref, core_ref, chip_ref, x_ref, ln1_gain_ref, gmid_ref, out_ref):
    grad = own_ref[0] + core_ref[0].astype(F32) + chip_ref[...].astype(F32)
    normal, scale = normed(x_ref[...].astype(F32), 0)
    gain = column(ln1_gain_ref[...])[:, 0:1]
    out_ref[...] = gmid_ref[...].T + norm_back(grad, normal, scale, gain, 0)


def output_kernel(*refs):
    sources, output_ref, loads, sems = refs[:4], refs[4], refs[5:9], refs[9]
    for copy in load_all(sources, loads, sems):
        copy.wait()
    middle_ref, active_ref, w_down_t_ref, b_down_ref = loads
    output = middle_ref[...] + dot_nt(active_ref[...], w_down_t_ref[...])
    output_ref[...] = (output + b_down_ref[...].reshape(1, -1)).T.astype(BF)


def plus(first, second):
    return (first.astype(F32) + second.astype(F32)).astype(BF)


def split_kernel(keep_ref, got_ref, *out_refs):
    for index, out_ref in enumerate(out_refs):
        out_ref[...] = plus(keep_ref[index], got_ref[index])


def part_kernel(index, keep_ref, got_ref, out_ref):
    out_ref[...] = plus(keep_ref[index], got_ref[...])


def four(refs):
    first, second, third, fourth = [ref[...].astype(F32) for ref in refs]
    return ((first + second) + (third + fourth)).astype(BF)


def square_kernel(*refs):
    refs[-1][...] = four(refs[:4])


def choose_kernel(*refs):
    kept_ref, send_ref = refs[-2:]
    total = four(refs[:4])
    odd = slots()[1]

    @pl.when(odd == 0)
    def _():
        kept_ref[...] = total[0]
        send_ref[...] = total[1]

    @pl.when(odd == 1)
    def _():
        kept_ref[...] = total[1]
        send_ref[...] = total[0]


def both_kernel(kept_ref, other_ref, a_ref, b_ref):
    odd = slots()[1]

    @pl.when(odd == 0)
    def _():
        a_ref[...] = kept_ref[...]
        b_ref[...] = other_ref[...]

    @pl.when(odd == 1)
    def _():
        a_ref[...] = other_ref[...]
        b_ref[...] = kept_ref[...]


def send_kernel(a_ref, got_a_ref, b_ref, got_b_ref, late_ref, x_ref, y_ref):
    rows = a_ref.shape[0]
    for out_ref, parts in ((x_ref, (a_ref, got_a_ref)), (y_ref, (b_ref, got_b_ref))):
        for index, part_ref in enumerate((*parts, late_ref)):
            out_ref[index * rows : index * rows + part_ref.shape[0], :] = part_ref[...]


def plus_kernel(first_ref, second_ref, *refs):
    refs[-1][...] = plus(first_ref[...], second_ref[...])


def early_rows(array, place):
    return slice((4 * array + place) * EARLY_ROWS, (4 * array + place + 1) * EARLY_ROWS)


def late_rows(place):
    start = 8 * EARLY_ROWS + place * LATE_ROWS
    return slice(start, start + LATE_ROWS)


GATHERED_ROWS = 8 * EARLY_ROWS + 4 * LATE_ROWS


def gather_kernel(own_x_ref, own_y_ref, got_x_ref, got_y_ref, got_xy_ref, out_ref):
    pair = 2 * EARLY_ROWS
    for array, (own_ref, got_ref) in enumerate(((own_x_ref, got_x_ref), (own_y_ref, got_y_ref))):
        start = array * 2 * pair
        out_ref[start : start + pair, :] = own_ref[:pair, :]
        out_ref[start + pair : start + 2 * pair, :] = got_ref[:pair, :]
    out_ref[late_rows(0), :] = own_x_ref[pair:, :]
    out_ref[late_rows(1), :] = got_y_ref[pair:, :]
    out_ref[late_rows(2), :] = got_x_ref[pair:, :]
    out_ref[late_rows(3), :] = got_xy_ref[...]


def place_blocks(core, blocks_ref, up_hbm, down_t_hbm, qkv, spare, extras, values, sems):
    slot = slots()[0]
    copies = []
    for place in range(4):
        row = pl.multiple_of(((core * 4 + place) ^ slot) * LATE_DEPTH, 8)
        block = unpack_late(blocks_ref[late_rows(place), :].astype(F32))
        qkv[pl.ds(row, LATE_DEPTH), :] = block[:, : 3 * D]
        spare[pl.ds(row, LATE_DEPTH), :] = block[:, LATE_COLS - LANES :]
    for array, out_hbm in enumerate((up_hbm, down_t_hbm)):
        for place in range(4):
            which = 4 * array + place
            index = (core * 4 + (place % 2 * 2 + place // 2 if array else place)) ^ slot
            row = pl.multiple_of(index % 4 * SHARD_ROWS, 16)
            col = pl.multiple_of(index // 4 * SHARD_COLS, LANES)
            block = blocks_ref[early_rows(array, place), :].astype(F32)
            values[which] = block[:SHARD_ROWS]
            extras[8 * array + index] = block[SHARD_ROWS:]
            target = out_hbm.at[pl.ds(row, SHARD_ROWS), pl.ds(col, SHARD_COLS)]
            copies.append(pltpu.make_async_copy(values.at[which], target, sems.at[which]))
            copies[-1].start()
    return copies


def unpack_own_kernel(blocks_ref, up_hbm, down_t_hbm, qkv, spare, extras, values, sems):
    for copy in place_blocks(0, blocks_ref, up_hbm, down_t_hbm, qkv, spare, extras, values, sems):
        copy.wait()


def unpack_far_kernel(blocks_ref, own_qkv, own_spare, own_extras, *refs):
    up_hbm, down_t_hbm, qkv, spare, extras, qkv_hbm, out_hbm = refs[2:9]
    vector_hbms, vector_refs = refs[9:17], refs[17:25]
    g_bqkv, g_ln1_gain, g_ln1_bias, g_bup, g_bout, g_ln2_gain, g_ln2_bias, g_bdown = vector_refs
    line, out, values, sems = refs[25:]
    copies = place_blocks(1, blocks_ref, up_hbm, down_t_hbm, qkv, spare, extras, values, sems)
    copies.append(pltpu.make_async_copy(qkv, qkv_hbm, sems.at[8]))
    copies[-1].start()
    for index in range(OUT_BLOCKS):
        row = 2 * EXTRA_ROWS * index
        out[row : row + EXTRA_ROWS, :] = extras[index, :, :D]
        out[row + EXTRA_ROWS : row + 2 * EXTRA_ROWS, :] = extras[index, :, D:]
    copies.append(pltpu.make_async_copy(out, out_hbm, sems.at[9]))
    copies[-1].start()
    for index in range(2):
        cols = slice(index * SHARD_COLS, (index + 1) * SHARD_COLS)
        line[0:1, cols] = extras[OUT_BLOCKS + index, 0:1, :]
    g_bup[...] = line[0:1, :FF].reshape(FF)
    g_bout[...] = extras[OUT_BLOCKS + 2, 0:1, :D].reshape(D)
    g_ln2_gain[...] = extras[OUT_BLOCKS + 2, 0:1, D:].reshape(D)
    g_ln2_bias[...] = extras[OUT_BLOCKS + 3, 0:1, :D].reshape(D)
    g_bdown[...] = extras[OUT_BLOCKS + 3, 0:1, D:].reshape(D)
    for index in range(5 * D // SPARE):
        row = index // 4 * LATE_DEPTH + index % 4
        line[1:2, index * SPARE : (index + 1) * SPARE] = spare[row : row + 1, LANES - SPARE :]
    g_bqkv[...] = line[1:2, : 3 * D].reshape(3 * D)
    g_ln1_gain[...] = line[1:2, 3 * D : 4 * D].reshape(D)
    g_ln1_bias[...] = line[1:2, 4 * D : 5 * D].reshape(D)
    copies += load_all(vector_refs, vector_hbms, sems.at[10:])
    for copy in copies:
        copy.wait()


def call(kernel, name, out_shape, scratch, *operands, vmem=16, loads=(), aliases=None, micros=0):
    operands = list(operands)
    specs = [pl.BlockSpec(memory_space=pltpu.VMEM) for entry in operands]
    operands += [pltpu.with_memory_space_constraint(entry, pltpu.HBM) for entry in loads]
    specs += [pl.BlockSpec(memory_space=pltpu.HBM) for entry in loads]
    return pl.pallas_call(
        kernel,
        name=name,
        out_shape=out_shape,
        in_specs=specs,
        out_specs=jax.tree.map(
            lambda entry: pl.BlockSpec(
                memory_space=pltpu.VMEM if isinstance(entry, jax.ShapeDtypeStruct) else pltpu.HBM
            ),
            out_shape,
        ),
        scratch_shapes=scratch,
        input_output_aliases=aliases or {},
        cost_estimate=pl.CostEstimate(flops=micros * 10**9, bytes_accessed=0, transcendentals=0)
        if micros
        else None,
        compiler_params=pltpu.CompilerParams(vmem_limit_bytes=vmem * MIB),
    )(*operands)


def shape(*dims, dtype=F32):
    return jax.ShapeDtypeStruct(dims, dtype)


def per_device(
    sizes,
    tokens,
    segment_ids,
    ln1_gain,
    ln1_bias,
    w_qkv,
    b_qkv,
    w_out,
    b_out,
    ln2_gain,
    ln2_bias,
    w_up,
    b_up,
    w_down,
    b_down,
    cotangent,
):
    dp_size, seq_size = sizes
    block = tokens.shape[1]
    length = segment_ids.shape[1]
    def swap(value, dp_bits, seq_bits):
        pairs = [
            (a * seq_size + b, (a ^ dp_bits) * seq_size + (b ^ seq_bits))
            for a in range(dp_size)
            for b in range(seq_size)
        ]
        return lax.ppermute(value, ("dp", "seq"), pairs)

    tie = lax.optimization_barrier

    x_t = tokens[0].T
    near = {bits: swap(x_t, 0, bits) for bits in (2, 1)}
    loads = (
        x_t,
        segment_ids,
        ln1_gain,
        ln1_bias,
        w_qkv,
        b_qkv,
        cotangent[0].T,
        w_up,
        w_down.T,
        w_out,
        b_out,
        ln2_gain,
        ln2_bias,
        b_up,
    )
    like = lambda entry: jax.ShapeDtypeStruct(entry.shape, entry.dtype)
    buffer = lambda entry: pltpu.VMEM(entry.shape, entry.dtype)
    out = call(
        prelude_kernel,
        "prelude",
        (like(x_t), *[like(entry) for entry in loads[6:]])
        + (
            shape(3 * D, D, dtype=BF),
            shape(5 * D, 8),
            shape(HEAD_DIM // 2, length),
            shape(HEAD_DIM // 2, length),
            shape(block, DP, dtype=BF),
            shape(D, block, dtype=BF),
            shape(DP, block, dtype=BF),
            shape(DP, block, dtype=BF),
            shape(LANES, length, dtype=BF),
            shape(block, LANES, dtype=BF),
        ),
        [buffer(entry) for entry in loads[1:6]] + [pltpu.SemaphoreType.DMA((len(loads),))],
        loads=loads,
    )
    near[2], *out = tie((near[2], *out))
    near[3] = swap(near[2], 0, 1)
    x0, ct_t, w_up, w_down_t, w_out, b_out, ln2_gain, ln2_bias, b_up = out[:9]
    wqkv_t, cols, cosine, sine, q, q_t, k_t, v_t, ke, qe = out[9:]
    early_block = shape(2, EARLY_ROWS, SHARD_COLS, dtype=BF)
    blocks = shape(4, *early_block.shape, dtype=BF)
    grad_middle, keep, *sends, k_t, v_t, probs, branch, attended, share, x_all, middle, active = call(
        forward_kernel,
        "layer_forward",
        (
            shape(block, D),
            blocks,
            *[early_block] * 4,
            shape(DP, length, dtype=BF),
            shape(DP, length, dtype=BF),
            shape(HEADS, block, length, dtype=BF),
            shape(block, D, dtype=BF),
            shape(block, DP),
            shape(block, DP),
            pltpu.HBM((4, D, block), BF),
            pltpu.HBM((block, D), F32),
            pltpu.HBM((block, FF), BF),
        ),
        [
            pltpu.VMEM((D, 3 * block), BF),
            pltpu.VMEM((block, D), F32),
            pltpu.VMEM((block, FF), BF),
            pltpu.SemaphoreType.DMA((4,)),
            pltpu.SemaphoreType.DMA((2,)),
        ],
        x0,
        near[1],
        near[2],
        near[3],
        k_t,
        v_t,
        q,
        q_t,
        ke,
        qe,
        cosine,
        sine,
        wqkv_t,
        cols,
        w_out,
        b_out,
        ln2_gain,
        ln2_bias,
        w_up,
        b_up,
        w_down_t,
        ct_t,
        vmem=28,
    )

    move_core, move_x, move_y, move_z, move_z2 = (0, 1), (1, 0), (0, 2), (2, 0), (4, 0)

    def add(first_term, second_term, *after):
        return call(plus_kernel, "add", like(first_term), [], first_term, second_term, *after)

    def far_sum(part):
        bit = 8
        while bit < dp_size:
            part = add(part, swap(part, bit, 0))
            bit *= 2
        return part

    def step(piece, after, grads, loads=()):
        operands = (cosine, sine, q_t, k_t, v_t, probs, share, inner, d_out, d_out_t)
        first = 1 + len(operands)
        heads = PIECES[piece]
        rows = len(heads) * HEAD_DIM
        tiles = heads[-1] // TILE_HEADS - heads[0] // TILE_HEADS + 1
        return call(
            functools.partial(piece_kernel, heads, len(loads)),
            f"attention_backward_{piece}",
            (
                shape(D, block, dtype=BF),
                shape(D, length, dtype=BF),
                shape(D, length, dtype=BF),
                *[like(entry) for entry in loads],
            ),
            [
                pltpu.VMEM((tiles * LANES, block), F32),
                pltpu.VMEM((rows, length), F32),
                pltpu.VMEM((rows, length), F32),
                pltpu.SemaphoreType.DMA((max(1, len(loads)),)),
            ],
            after,
            *operands,
            *grads,
            aliases={first + i: i for i in range(len(grads))},
            loads=loads,
            vmem=28,
        )

    def split(name, keep, got):
        return call(split_kernel, name, (like(keep[0]),) * 4, [], keep, got)

    moves = [move_y, move_x, (1, 2)]

    def square_swap(parts):
        return [swap(part, *move) for part, move in zip(parts, moves)]

    gots = {place: swap(sends[place], *move_core) for place in (1, 2, 3, 0)}
    d_out, d_out_t, inner = call(
        finish_kernel,
        "layer_finish",
        (shape(block, DP, dtype=BF), shape(D, block, dtype=BF), shape(block, DP)),
        [],
        branch,
        attended,
        share,
        w_out,
    )
    kept, *sends = [
        call(
            functools.partial(part_kernel, place), "add_core", early_block, [], keep, gots[place]
        )
        for place in range(4)
    ]
    gots = square_swap(sends)
    grads = step(0, sends[2], (), (x_all, w_qkv, ln1_gain, ln1_bias))
    *gots, first_grad = tie((*gots, grads[0]))
    grads = (first_grad, *grads[1:])
    half = shape(EARLY_ROWS, SHARD_COLS, dtype=BF)
    kept, sent = call(choose_kernel, "add_square", (half, half), [], kept, *gots)
    if dp_size > 2:
        got = swap(sent, *move_z)
    late_blocks = shape(4, LATE_ROWS, SHARD_COLS, dtype=BF)
    late_keep, late_send, own, far = call(
        projection_kernel,
        "projection",
        (late_blocks, late_blocks, shape(2, D, block), shape(2, D, block, dtype=BF)),
        [pltpu.VMEM((D, LATE_COLS), F32)],
        sent,
        *grads,
    )
    if dp_size > 2:
        got, late_send = tie((got, late_send))
        kept = add(kept, got)
    if dp_size > 4:
        got = swap(kept, *move_z2)
    core_far = swap(far, *move_core)
    late, *sends = split("add_late_core", late_keep, swap(late_send, *move_core))
    gots = square_swap(sends)
    if dp_size > 4:
        got, gots[0], gots[2] = tie((got, gots[0], gots[2]))
        kept = far_sum(add(kept, got))
    late = call(square_kernel, "add_late_square", like(late), [], late, *gots)
    other = swap(kept, *move_z) if dp_size > 2 else sent
    late, core_far = tie((late, core_far))
    chip_far = swap(plus(own[1], core_far[1]), *move_y)
    if dp_size > 2:
        got, chip_far = tie((swap(late, *move_z), chip_far))
        late = add(late, got)
    early_a, early_b = call(both_kernel, "early_both", (half, half), [], kept, other)
    input_grad = call(
        input_kernel,
        "input_gradient",
        shape(D, block),
        [],
        own,
        core_far,
        chip_far,
        x0,
        ln1_gain,
        grad_middle,
        micros=1,
    )
    got_a, got_b = swap(early_a, *move_y), swap(early_b, *move_x)
    if dp_size > 4:
        got, got_a, got_b, input_grad = tie((swap(late, *move_z2), got_a, got_b, input_grad))
        late = far_sum(add(late, got))
    both = shape(2 * EARLY_ROWS + LATE_ROWS, SHARD_COLS, dtype=BF)
    own_x, own_y = call(
        send_kernel, "send", (both, both), [], early_a, got_a, early_b, got_b, late
    )
    parts = (middle, active, w_down.T, b_down)
    output = call(
        output_kernel,
        "layer_output",
        shape(D, block, dtype=BF),
        [*[buffer(entry) for entry in parts], pltpu.SemaphoreType.DMA((len(parts),))],
        loads=parts,
    )
    *gots, output = tie(
        (swap(own_x, *move_x), swap(own_y, *move_y), swap(late, 1, 2), output)
    )
    gathered = shape(GATHERED_ROWS, SHARD_COLS, dtype=BF)
    blocks = call(gather_kernel, "gather_blocks", gathered, [], own_x, own_y, *gots)
    far_blocks = swap(blocks, *move_core)
    in_hbm = (pltpu.HBM((D, FF), F32), pltpu.HBM((D, FF), F32))
    assembled = (shape(D, 3 * D), shape(D, LANES), shape(16, EXTRA_ROWS, SHARD_COLS))
    values = pltpu.VMEM((8, SHARD_ROWS, SHARD_COLS), F32)
    g_up, g_down_t, *own_parts = call(
        unpack_own_kernel,
        "unpack_own",
        (*in_hbm, *assembled),
        [values, pltpu.SemaphoreType.DMA((8,))],
        blocks,
    )
    sizes = (3 * D, D, D, FF, D, D, D, D)
    vectors = [pltpu.HBM((size,), F32) for size in sizes]
    g_up, g_down_t, _, _, _, g_qkv, g_out, *vectors = call(
        unpack_far_kernel,
        "unpack_far",
        (*in_hbm, *assembled, pltpu.HBM((D, 3 * D), F32), pltpu.HBM((D, D), F32), *vectors),
        [
            *[pltpu.VMEM((size,), F32) for size in sizes],
            pltpu.VMEM((8, 5 * D), F32),
            pltpu.VMEM((D, D), F32),
            values,
            pltpu.SemaphoreType.DMA((18,)),
        ],
        far_blocks,
        *own_parts,
        loads=(g_up, g_down_t),
        aliases={4: 0, 5: 1, 1: 2, 2: 3, 3: 4},
    )
    g_bqkv, g_ln1_gain, g_ln1_bias, g_bup, g_bout, g_ln2_gain, g_ln2_bias, g_bdown = vectors
    return (
        output.T[None],
        input_grad.T[None],
        g_ln1_gain,
        g_ln1_bias,
        g_qkv,
        g_bqkv,
        g_out,
        g_bout,
        g_ln2_gain,
        g_ln2_bias,
        g_up,
        g_bup,
        g_down_t.T,
        g_bdown,
    )


def solution(mesh):
    split = P("dp", "seq", None)
    whole = P()
    return jax.shard_map(
        functools.partial(per_device, (mesh.shape["dp"], mesh.shape["seq"])),
        mesh=mesh,
        in_specs=(split, P("dp", None)) + (whole,) * 12 + (split,),
        out_specs=(split, split) + (whole,) * 12,
        check_vma=False,
    )
```

```python
import functools
import math

import jax
import jax.numpy as jnp
from jax import lax
from jax.experimental import pallas as pl
from jax.experimental.pallas import tpu as pltpu
from jax.sharding import PartitionSpec as P

HEADS = 20
HEAD_DIM = 16
D = HEADS * HEAD_DIM
FF = 4 * D
GENES = 4
LANES = 128
TILE_HEADS = LANES // HEAD_DIM
DP = 384
BAR = -1e30
SAFE = 40.0
EPS = 1e-05
SHARD_ROWS, SHARD_COLS, EXTRA_ROWS = D // 4, FF // 2, 16
EARLY_ROWS = SHARD_ROWS + EXTRA_ROWS
LATE_DEPTH, LATE_COLS = D // 8, 8 * LANES
LATE_ROWS = LATE_DEPTH * LATE_COLS // SHARD_COLS
SPARE = LATE_COLS - 3 * D
OUT_BLOCKS = D // (2 * EXTRA_ROWS)
PIECES = (range(HEADS),)
MIB = 1 << 20
BF = jnp.bfloat16
F32 = jnp.float32
ERFC_P = 0.3275911
ERFC = (1.061405429, -1.453152027, 1.421413741, -0.284496736, 0.254829592)


def dot(a, b, contract=((1,), (0,))):
    return lax.dot_general(a, b, (contract, ((), ())), preferred_element_type=F32)


def dot_nt(a, b):
    return dot(a, b, ((1,), (1,)))


def dot_tn(a, b):
    return dot(a, b, ((0,), (0,)))


def normal_cdf(x):
    bell = jnp.exp(-0.5 * x * x)
    t = 1.0 / (1.0 + (ERFC_P / math.sqrt(2.0)) * jnp.abs(x))
    tail = jnp.full_like(x, 0.5 * ERFC[0])
    for entry in ERFC[1:]:
        tail = tail * t + 0.5 * entry
    tail = tail * t * bell
    return jnp.where(x < 0.0, tail, 1.0 - tail), bell


def normed(values, axis):
    centered = values - jnp.mean(values, axis=axis, keepdims=True)
    spread = jnp.mean(centered * centered, axis=axis, keepdims=True)
    scale = lax.rsqrt(spread + EPS)
    return centered * scale, scale


def norm_back(grad, normal, scale, gain, axis):
    e = grad * gain
    return scale * (
        e
        - jnp.mean(e, axis=axis, keepdims=True)
        - normal * jnp.mean(e * normal, axis=axis, keepdims=True)
    )


def rotate_rows(values, cosine, sine):
    rows, cols = values.shape
    half = HEAD_DIM // 2
    parts = values.reshape(rows // HEAD_DIM, 2, half, cols)
    first, second = parts[:, 0], parts[:, 1]
    out = jnp.stack([first * cosine - second * sine, second * cosine + first * sine], axis=1)
    return out.reshape(rows, cols)


def pad_rows(values, rows):
    return jnp.concatenate(
        [values, jnp.zeros((rows - values.shape[0], values.shape[1]), values.dtype)], axis=0
    )


def pad_cols(values, cols):
    return jnp.concatenate(
        [values, jnp.zeros((values.shape[0], cols - values.shape[1]), values.dtype)], axis=1
    )


def slots():
    dp, seq = lax.axis_index("dp"), lax.axis_index("seq")
    core, chip_y, chip_x = seq & 1, seq >> 1, dp & 1
    return core * 4 + chip_x * 2 + chip_y, (dp >> 1) & 1, seq


def load_all(sources, targets, sems):
    copies = [
        pltpu.make_async_copy(source, target, sems.at[i])
        for i, (source, target) in enumerate(zip(sources, targets))
    ]
    for copy in copies:
        copy.start()
    return copies


def column(vector):
    return jnp.broadcast_to(vector.reshape(1, -1), (8, vector.shape[0])).T


def prelude_kernel(*refs):
    sources, outs, (local, sems) = refs[:14], refs[14:-6], (refs[-6:-1], refs[-1])
    kept, made = outs[:9], outs[9:]
    copies = load_all(sources, (kept[0], *local, *kept[1:]), sems)
    for copy in copies[:6]:
        copy.wait()
    prelude_body(kept[0], *local, *made)
    for copy in copies[6:]:
        copy.wait()


def prelude_body(
    x0_ref,
    seg_ref,
    ln1_gain_ref,
    ln1_bias_ref,
    wqkv_ref,
    bqkv_ref,
    wqkv_t_ref,
    cols_ref,
    cos_ref,
    sin_ref,
    q_ref,
    qt_ref,
    kt_ref,
    vt_ref,
    ke_ref,
    qe_ref,
):
    block = x0_ref.shape[1]
    length = 4 * block
    seq = slots()[2]
    genes = seg_ref[...]
    begins = [
        jnp.sum((genes < gene).astype(F32), axis=1, keepdims=True) for gene in range(1, GENES)
    ]
    index = lax.broadcasted_iota(jnp.int32, (1, block), 1).astype(F32)
    half = HEAD_DIM // 2
    step = lax.broadcasted_iota(jnp.int32, (half, block), 0).astype(F32)
    frequency = jnp.exp(step * (-2.0 * math.log(10000.0) / HEAD_DIM))
    row = lax.broadcasted_iota(jnp.int32, (LANES, block), 0)
    for distance in range(4):
        cols = slice(distance * block, (distance + 1) * block)
        chunk = seq ^ distance
        own = seg_ref[:, pl.ds(pl.multiple_of(chunk * block, block), block)]
        begin = jnp.zeros((1, block), F32)
        for gene in range(1, GENES):
            begin = jnp.where(own == gene, begins[gene - 1], begin)
        place = index + (chunk * block).astype(F32) - begin
        angle = place * frequency
        cos_ref[:, cols] = jnp.cos(angle)
        sin_ref[:, cols] = jnp.sin(angle)
        table = jnp.where(
            row < GENES, jnp.where(row == own, 0.0, BAR), jnp.where(row < GENES + 3, 1.0, 0.0)
        )
        ke_ref[:, cols] = table.astype(BF)
        if distance == 0:
            qe_ref[...] = jnp.where(row == own, 1.0, 0.0).T.astype(BF)

    wqkv_t_ref[...] = wqkv_ref[...].T
    cols_ref[: 3 * D, :] = column(bqkv_ref[...])
    cols_ref[3 * D : 4 * D, :] = column(ln1_gain_ref[...])
    cols_ref[4 * D :, :] = column(ln1_bias_ref[...])
    normal, _ = normed(x0_ref[...].astype(F32), 0)
    first = (normal * cols_ref[3 * D : 4 * D, 0:1] + cols_ref[4 * D :, 0:1]).astype(BF)
    raw = dot(wqkv_t_ref[...], first) + cols_ref[: 3 * D, 0:1]
    cosine, sine = cos_ref[:, :block], sin_ref[:, :block]
    q_t = rotate_rows(raw[:D], cosine, sine).astype(BF)
    qt_ref[...] = q_t
    q_ref[...] = pad_rows(q_t.astype(F32) * (1.0 / math.sqrt(HEAD_DIM)), DP).T.astype(BF)
    kt_ref[...] = pad_rows(rotate_rows(raw[D : 2 * D], cosine, sine).astype(BF), DP)
    vt_ref[...] = pad_rows(raw[2 * D :].astype(BF), DP)


def forward_kernel(
    x0_ref,
    x1_ref,
    x2_ref,
    x3_ref,
    k0_ref,
    v0_ref,
    q_ref,
    qt_ref,
    ke_ref,
    qe_ref,
    cos_ref,
    sin_ref,
    wqkv_t_ref,
    cols_ref,
    w_out_ref,
    b_out_ref,
    ln2_gain_ref,
    ln2_bias_ref,
    w_up_ref,
    b_up_ref,
    w_down_t_ref,
    ct_t_ref,
    gmid_ref,
    keep_ref,
    send0_ref,
    send1_ref,
    send2_ref,
    send3_ref,
    kt_ref,
    vt_ref,
    probs_ref,
    branch_ref,
    att_acc,
    share_ref,
    x_all_hbm,
    middle_hbm,
    active_hbm,
    xn_ref,
    middle_ref,
    active_ref,
    sems,
    out_sems,
):
    block = x0_ref.shape[1]
    send_refs = (send0_ref, send1_ref, send2_ref, send3_ref)
    chunks = (x0_ref, x1_ref, x2_ref, x3_ref)
    copies = load_all(chunks, [x_all_hbm.at[i] for i in range(4)], sems)
    gain, bias = cols_ref[3 * D : 4 * D, 0:1], cols_ref[4 * D :, 0:1]
    for index, chunk in enumerate((x1_ref, x2_ref, x3_ref)):
        normal, _ = normed(chunk[...].astype(F32), 0)
        xn_ref[:, index * block : (index + 1) * block] = (normal * gain + bias).astype(BF)
    first = xn_ref[...]
    kt_ref[:, :block] = k0_ref[...]
    vt_ref[:, :block] = v0_ref[...]
    raw = dot(wqkv_t_ref[D:, :], first) + cols_ref[D : 3 * D, 0:1]
    keys = rotate_rows(raw[:D], cos_ref[:, block:], sin_ref[:, block:])
    kt_ref[:, block:] = pad_rows(keys.astype(BF), DP)
    vt_ref[:, block:] = pad_rows(raw[D:].astype(BF), DP)

    lane = lax.broadcasted_iota(jnp.int32, (block, LANES), 1)
    att_acc[...] = jnp.zeros_like(att_acc)
    share_ref[...] = jnp.ones_like(share_ref)
    zero = jnp.zeros((), BF)

    def largest(values):
        squares = jnp.square(values).reshape(HEADS, HEAD_DIM, values.shape[1])
        return jnp.max(jnp.sum(squares, axis=1), axis=1, keepdims=True)

    key_sizes = jnp.maximum(largest(keys), largest(k0_ref[:D, :].astype(F32)))
    bound = jnp.max(largest(qt_ref[...].astype(F32)) * key_sizes, axis=0, keepdims=True)
    safe = bound[0, 0] * (1.02 / HEAD_DIM) < SAFE * SAFE

    def score(head, start):
        mask = lane // HEAD_DIM == head % TILE_HEADS
        left = jnp.concatenate(
            [jnp.where(mask, q_ref[:, pl.ds(start, LANES)], zero), qe_ref[...]], axis=1
        )
        right = jnp.concatenate([kt_ref[pl.ds(start, LANES), :], ke_ref[...]], axis=0)
        return mask, dot(left, right)

    def mix(start, mask, scores, head):
        tile = pl.ds(start, LANES)
        weights = jnp.exp(scores)
        mass = jnp.sum(weights, axis=1, keepdims=True)
        probs_ref[head] = weights.astype(BF)
        att_acc[:, tile] += jnp.where(mask, dot_nt(weights.astype(BF), vt_ref[tile, :]), 0.0)
        share_ref[:, tile] = jnp.where(mask, mass, share_ref[:, tile])

    @pl.when(safe)
    def _():
        scored = score(0, 0)
        for head in range(HEADS):
            ahead = score(head + 1, (head + 1) // TILE_HEADS * LANES) if head + 1 < HEADS else None
            mix(head // TILE_HEADS * LANES, *scored, head)
            scored = ahead

    @pl.when(jnp.logical_not(safe))
    def _():
        def attend(head, carry):
            start = pl.multiple_of(head // TILE_HEADS * LANES, LANES)
            mask, scores = score(head, start)
            scores = scores - jnp.max(scores, axis=1, keepdims=True)
            mix(start, mask, scores, head)
            return carry

        lax.fori_loop(0, HEADS, attend, 0, unroll=4)

    def line(ref):
        return ref[...].reshape(1, -1)

    share_ref[...] = 1.0 / share_ref[...]
    att_acc[...] = att_acc[...] * share_ref[...]
    attended = att_acc[:, :D].astype(BF)
    middle = x0_ref[...].T.astype(F32) + (dot(attended, w_out_ref[...]) + line(b_out_ref))
    normal2, scale2 = normed(middle, 1)
    gain2 = line(ln2_gain_ref)
    second = (normal2 * gain2 + line(ln2_bias_ref)).astype(BF)
    pre = dot(second, w_up_ref[...]) + line(b_up_ref)
    share, bell = normal_cdf(pre)
    active = (pre * share).astype(BF)
    slope = share + pre * (bell * (1.0 / math.sqrt(2.0 * math.pi)))
    middle_ref[...] = middle
    active_ref[...] = active
    copies += load_all((middle_ref, active_ref), (middle_hbm, active_hbm), out_sems)
    ct_t = ct_t_ref[...]
    ct = ct_t.T
    ct_wide = ct.astype(F32)
    grad_pre = (dot(ct, w_down_t_ref[...]) * slope).astype(BF)
    grad_second = dot_nt(grad_pre, w_up_ref[...])
    grad_middle = ct_wide + norm_back(grad_second, normal2, scale2, gain2, 1)
    gmid_ref[...] = grad_middle
    branch = grad_middle.astype(BF)
    branch_ref[...] = branch

    grad_up = dot_tn(second, grad_pre).astype(BF)
    grad_down = dot(ct_t, active).astype(BF)
    grad_out = dot_tn(attended, branch)

    def column_sum(values):
        return jnp.sum(values, axis=0, keepdims=True)

    lines = column_sum(grad_pre.astype(F32))
    lines = [
        lines[:, :SHARD_COLS],
        lines[:, SHARD_COLS:],
        jnp.concatenate([column_sum(branch.astype(F32)), column_sum(grad_second * normal2)], axis=1),
        jnp.concatenate([column_sum(grad_second), column_sum(ct_wide)], axis=1),
    ]

    def extra(index):
        if index < OUT_BLOCKS:
            row = 2 * EXTRA_ROWS * index
            upper = grad_out[row : row + EXTRA_ROWS]
            lower = grad_out[row + EXTRA_ROWS : row + 2 * EXTRA_ROWS]
            return jnp.concatenate([upper, lower], axis=1).astype(BF)
        if index < OUT_BLOCKS + len(lines):
            line = lines[index - OUT_BLOCKS]
            return jnp.broadcast_to(line, (EXTRA_ROWS, SHARD_COLS)).astype(BF)
        return jnp.zeros((EXTRA_ROWS, SHARD_COLS), BF)

    slot = slots()[0]
    for index in range(8):
        rows, cols = shard(index)
        stays = index // 4 == slot // 4
        for array, values in enumerate((grad_up, grad_down)):
            block_values = jnp.concatenate([values[rows, cols], extra(8 * array + index)], axis=0)
            place = (index ^ slot) % 4
            store_parts(keep_ref, send_refs, stays, place, array, block_values)
    for copy in copies:
        copy.wait()


def finish_kernel(branch_ref, att_ref, share_ref, w_out_ref, do_ref, dot_ref, inner_ref):
    grad_att = dot_nt(branch_ref[...], w_out_ref[...]).astype(BF)
    grad_att_wide = pad_cols(grad_att.astype(F32), DP)
    do_ref[...] = grad_att_wide.astype(BF)
    dot_ref[...] = (grad_att_wide * share_ref[...]).T[:D, :].astype(BF)
    inner_ref[...] = grad_att_wide * att_ref[...]


def store_parts(keep_ref, send_refs, stays, place, array, values):
    @pl.when(stays)
    def _():
        keep_ref[place, array] = values

    for index, send_ref in enumerate(send_refs):

        @pl.when(jnp.logical_and(jnp.logical_not(stays), place == index))
        def _():
            send_ref[array] = values


def store_block(keep_ref, send_ref, stays, place, values):
    @pl.when(stays)
    def _():
        keep_ref[place] = values

    @pl.when(jnp.logical_not(stays))
    def _():
        send_ref[place] = values


def shard(index):
    row, col = index % 4 * SHARD_ROWS, index // 4 * SHARD_COLS
    return slice(row, row + SHARD_ROWS), slice(col, col + SHARD_COLS)


def piece_kernel(
    heads,
    loads,
    after_ref,
    cos_ref,
    sin_ref,
    qt_ref,
    kt_ref,
    vt_ref,
    probs_ref,
    share_ref,
    inner_ref,
    do_ref,
    dot_ref,
    *refs,
):
    dq_acc, dk_acc, dv_acc, sems = refs[-4:]
    outs = refs[-4 - 3 - loads : -4]
    gq_ref, gk_ref, gv_ref = outs[:3]
    copies = load_all(refs[len(refs) - 4 - 3 - 2 * loads : len(refs) - 4 - 3 - loads], outs[3:], sems)
    block = do_ref.shape[0]
    lane = lax.broadcasted_iota(jnp.int32, (block, LANES), 1)
    first_tile, last_tile = heads[0] // TILE_HEADS, heads[-1] // TILE_HEADS

    def shift(head):
        tile = slice(head // TILE_HEADS * LANES, (head // TILE_HEADS + 1) * LANES)
        mask = lane // HEAD_DIM == head % TILE_HEADS
        left = jnp.where(mask, do_ref[:, tile], jnp.zeros((), BF))
        return head, tile, mask, dot(left, vt_ref[tile, :])

    def finish(head, tile, mask, grad_probs):
        rows = slice(head * HEAD_DIM, (head + 1) * HEAD_DIM)
        here = slice((head - heads[0]) * HEAD_DIM, (head - heads[0] + 1) * HEAD_DIM)
        probs = probs_ref[head - heads[0]]
        share = share_ref[:, rows.start : rows.start + 1]
        inner = jnp.sum(jnp.where(mask, inner_ref[:, tile], 0.0), axis=1, keepdims=True)
        grad_scores = (probs.astype(F32) * ((grad_probs - inner) * share)).astype(BF)
        dv_acc[here, :] = dot(dot_ref[rows, :], probs)
        dk_acc[here, :] = dot(qt_ref[rows, :], grad_scores)
        return jnp.where(mask, dot_nt(grad_scores, kt_ref[tile, :]), 0.0)

    totals = {}
    shifted = shift(heads[0])
    for head in heads:
        ahead = shift(head + 1) if head + 1 in heads else None
        index = head // TILE_HEADS - first_tile
        grad_queries = finish(*shifted)
        totals[index] = totals[index] + grad_queries if index in totals else grad_queries
        shifted = ahead
        if ahead is None or ahead[0] // TILE_HEADS - first_tile != index:
            dq_acc[index * LANES : (index + 1) * LANES, :] = totals[index].T

    cosine, sine = cos_ref[...], sin_ref[...]
    scale = 1.0 / math.sqrt(HEAD_DIM)
    rows = slice(heads[0] * HEAD_DIM, (heads[-1] + 1) * HEAD_DIM)
    skip = first_tile * LANES
    dq_t = (dq_acc[rows.start - skip : rows.stop - skip, :] * scale).astype(BF).astype(F32)
    gq_ref[rows, :] = rotate_rows(dq_t, cosine[:, :block], -sine[:, :block]).astype(BF)
    gk_ref[rows, :] = rotate_rows(dk_acc[...] * scale, cosine, -sine).astype(BF)
    gv_ref[rows, :] = dv_acc[...].astype(BF)
    for copy in copies:
        copy.wait()


def projection_kernel(
    after_ref,
    gq_ref,
    gk_ref,
    gv_ref,
    x_ref,
    wqkv_ref,
    ln1_gain_ref,
    ln1_bias_ref,
    keep_ref,
    send_ref,
    own_ref,
    far_ref,
    matrix,
):
    block = x_ref.shape[2]
    length = 4 * block
    ones = jnp.ones((16, length), BF)
    grad_q, grad_k, grad_v = gq_ref[...], gk_ref[...], gv_ref[...]
    sums = [
        dot_nt(ones[:, :block], grad_q)[0:1],
        dot_nt(ones, grad_k)[0:1],
        dot_nt(ones, grad_v)[0:1],
    ]
    gain, bias = column(ln1_gain_ref[...])[:, 0:1], column(ln1_bias_ref[...])[:, 0:1]
    normal = jnp.concatenate([normed(x_ref[i].astype(F32), 0)[0] for i in range(4)], axis=1)
    first = (normal * gain + bias).astype(BF)
    grad_first = dot(wqkv_ref[:, D : 2 * D], grad_k) + dot(wqkv_ref[:, 2 * D :], grad_v)
    own = grad_first[:, :block] + dot(wqkv_ref[:, :D], grad_q)
    own_ref[0] = own
    own_ref[1] = grad_first[:, 2 * block : 3 * block]
    far_ref[0] = grad_first[:, block : 2 * block].astype(BF)
    far_ref[1] = grad_first[:, 3 * block :].astype(BF)
    grad_first = jnp.concatenate([own, grad_first[:, block:]], axis=1)
    matrix[:, :D] = dot_nt(first[:, :block], grad_q)
    matrix[:, D : 2 * D] = dot_nt(first, grad_k)
    matrix[:, 2 * D : 3 * D] = dot_nt(first, grad_v)
    matrix[:, 3 * D :] = jnp.zeros((D, SPARE), F32)
    vectors = jnp.concatenate(
        [
            *sums,
            dot_nt(ones, (grad_first * normal).astype(BF))[0:1],
            dot_nt(ones, grad_first.astype(BF))[0:1],
        ],
        axis=1,
    )
    for index in range(5 * D // SPARE):
        row = index // 4 * LATE_DEPTH + index % 4
        matrix[row : row + 1, 3 * D :] = vectors[:, index * SPARE : (index + 1) * SPARE]
    slot = slots()[0]
    for index in range(8):
        values = pack_late(matrix[index * LATE_DEPTH : (index + 1) * LATE_DEPTH, :]).astype(BF)
        stays = index // 4 == slot // 4
        store_block(keep_ref, send_ref, stays, (index ^ slot) % 4, values)


def pack_late(values):
    tiles = [values[:, i * LANES : (i + 1) * LANES] for i in range(LATE_COLS // LANES)]
    tiles = jnp.concatenate(tiles, axis=0)
    tiles = [tiles[i * LATE_ROWS : (i + 1) * LATE_ROWS] for i in range(SHARD_COLS // LANES)]
    return jnp.concatenate(tiles, axis=1)


def unpack_late(values):
    tiles = [values[:, i * LANES : (i + 1) * LANES] for i in range(SHARD_COLS // LANES)]
    tiles = jnp.concatenate(tiles, axis=0)
    tiles = [tiles[i * LATE_DEPTH : (i + 1) * LATE_DEPTH] for i in range(LATE_COLS // LANES)]
    return jnp.concatenate(tiles, axis=1)


def input_kernel(own_ref, core_ref, chip_ref, x_ref, ln1_gain_ref, gmid_ref, out_ref):
    grad = own_ref[0] + core_ref[0].astype(F32) + chip_ref[...].astype(F32)
    normal, scale = normed(x_ref[...].astype(F32), 0)
    gain = column(ln1_gain_ref[...])[:, 0:1]
    out_ref[...] = gmid_ref[...].T + norm_back(grad, normal, scale, gain, 0)


def output_kernel(*refs):
    sources, output_ref, loads, sems = refs[:4], refs[4], refs[5:9], refs[9]
    for copy in load_all(sources, loads, sems):
        copy.wait()
    middle_ref, active_ref, w_down_t_ref, b_down_ref = loads
    output = middle_ref[...] + dot_nt(active_ref[...], w_down_t_ref[...])
    output_ref[...] = (output + b_down_ref[...].reshape(1, -1)).T.astype(BF)


def plus(first, second):
    return (first.astype(F32) + second.astype(F32)).astype(BF)


def split_kernel(keep_ref, got_ref, *out_refs):
    for index, out_ref in enumerate(out_refs):
        out_ref[...] = plus(keep_ref[index], got_ref[index])


def part_kernel(index, keep_ref, got_ref, out_ref):
    out_ref[...] = plus(keep_ref[index], got_ref[...])


def four(refs):
    first, second, third, fourth = [ref[...].astype(F32) for ref in refs]
    return ((first + second) + (third + fourth)).astype(BF)


def square_kernel(*refs):
    refs[-1][...] = four(refs[:4])


def choose_kernel(*refs):
    kept_ref, send_ref = refs[-2:]
    total = four(refs[:4])
    odd = slots()[1]

    @pl.when(odd == 0)
    def _():
        kept_ref[...] = total[0]
        send_ref[...] = total[1]

    @pl.when(odd == 1)
    def _():
        kept_ref[...] = total[1]
        send_ref[...] = total[0]


def both_kernel(kept_ref, other_ref, a_ref, b_ref):
    odd = slots()[1]

    @pl.when(odd == 0)
    def _():
        a_ref[...] = kept_ref[...]
        b_ref[...] = other_ref[...]

    @pl.when(odd == 1)
    def _():
        a_ref[...] = other_ref[...]
        b_ref[...] = kept_ref[...]


def send_kernel(a_ref, got_a_ref, b_ref, got_b_ref, late_ref, x_ref, y_ref):
    rows = a_ref.shape[0]
    for out_ref, parts in ((x_ref, (a_ref, got_a_ref)), (y_ref, (b_ref, got_b_ref))):
        for index, part_ref in enumerate((*parts, late_ref)):
            out_ref[index * rows : index * rows + part_ref.shape[0], :] = part_ref[...]


def plus_kernel(first_ref, second_ref, *refs):
    refs[-1][...] = plus(first_ref[...], second_ref[...])


def early_rows(array, place):
    return slice((4 * array + place) * EARLY_ROWS, (4 * array + place + 1) * EARLY_ROWS)


def late_rows(place):
    start = 8 * EARLY_ROWS + place * LATE_ROWS
    return slice(start, start + LATE_ROWS)


GATHERED_ROWS = 8 * EARLY_ROWS + 4 * LATE_ROWS


def gather_kernel(own_x_ref, own_y_ref, got_x_ref, got_y_ref, got_xy_ref, out_ref):
    pair = 2 * EARLY_ROWS
    for array, (own_ref, got_ref) in enumerate(((own_x_ref, got_x_ref), (own_y_ref, got_y_ref))):
        start = array * 2 * pair
        out_ref[start : start + pair, :] = own_ref[:pair, :]
        out_ref[start + pair : start + 2 * pair, :] = got_ref[:pair, :]
    out_ref[late_rows(0), :] = own_x_ref[pair:, :]
    out_ref[late_rows(1), :] = got_y_ref[pair:, :]
    out_ref[late_rows(2), :] = got_x_ref[pair:, :]
    out_ref[late_rows(3), :] = got_xy_ref[...]


def place_blocks(core, blocks_ref, up_hbm, down_t_hbm, qkv_hbm, spare, extras, qkv, values, sems):
    slot = slots()[0]
    copies = []
    for place in range(4):
        row = pl.multiple_of(((core * 4 + place) ^ slot) * LATE_DEPTH, 8)
        block = unpack_late(blocks_ref[late_rows(place), :].astype(F32))
        qkv[place] = block[:, : 3 * D]
        target = qkv_hbm.at[pl.ds(row, LATE_DEPTH), :]
        copies.append(pltpu.make_async_copy(qkv.at[place], target, sems.at[8 + place]))
        copies[-1].start()
        spare[pl.ds(row, LATE_DEPTH), :] = block[:, LATE_COLS - LANES :]
    for array, out_hbm in enumerate((up_hbm, down_t_hbm)):
        for place in range(4):
            which = 4 * array + place
            index = (core * 4 + (place % 2 * 2 + place // 2 if array else place)) ^ slot
            row = pl.multiple_of(index % 4 * SHARD_ROWS, 16)
            col = pl.multiple_of(index // 4 * SHARD_COLS, LANES)
            block = blocks_ref[early_rows(array, place), :].astype(F32)
            values[which] = block[:SHARD_ROWS]
            extras[8 * array + index] = block[SHARD_ROWS:]
            target = out_hbm.at[pl.ds(row, SHARD_ROWS), pl.ds(col, SHARD_COLS)]
            copies.append(pltpu.make_async_copy(values.at[which], target, sems.at[which]))
            copies[-1].start()
    return copies


def unpack_own_kernel(*refs):
    for copy in place_blocks(0, *refs):
        copy.wait()


def unpack_far_kernel(blocks_ref, own_spare, own_extras, *refs):
    in_hbms, spare, extras, out_hbm = refs[3:6], refs[6], refs[7], refs[8]
    vector_hbms, vector_refs = refs[9:17], refs[17:25]
    g_bqkv, g_ln1_gain, g_ln1_bias, g_bup, g_bout, g_ln2_gain, g_ln2_bias, g_bdown = vector_refs
    line, out, qkv, values, sems = refs[25:]
    copies = place_blocks(1, blocks_ref, *in_hbms, spare, extras, qkv, values, sems)
    for index in range(OUT_BLOCKS):
        row = 2 * EXTRA_ROWS * index
        out[row : row + EXTRA_ROWS, :] = extras[index, :, :D]
        out[row + EXTRA_ROWS : row + 2 * EXTRA_ROWS, :] = extras[index, :, D:]
    copies.append(pltpu.make_async_copy(out, out_hbm, sems.at[12]))
    copies[-1].start()
    for index in range(2):
        cols = slice(index * SHARD_COLS, (index + 1) * SHARD_COLS)
        line[0:1, cols] = extras[OUT_BLOCKS + index, 0:1, :]
    g_bup[...] = line[0:1, :FF].reshape(FF)
    g_bout[...] = extras[OUT_BLOCKS + 2, 0:1, :D].reshape(D)
    g_ln2_gain[...] = extras[OUT_BLOCKS + 2, 0:1, D:].reshape(D)
    g_ln2_bias[...] = extras[OUT_BLOCKS + 3, 0:1, :D].reshape(D)
    g_bdown[...] = extras[OUT_BLOCKS + 3, 0:1, D:].reshape(D)
    for index in range(5 * D // SPARE):
        row = index // 4 * LATE_DEPTH + index % 4
        line[1:2, index * SPARE : (index + 1) * SPARE] = spare[row : row + 1, LANES - SPARE :]
    g_bqkv[...] = line[1:2, : 3 * D].reshape(3 * D)
    g_ln1_gain[...] = line[1:2, 3 * D : 4 * D].reshape(D)
    g_ln1_bias[...] = line[1:2, 4 * D : 5 * D].reshape(D)
    copies += load_all(vector_refs, vector_hbms, sems.at[13:])
    for copy in copies:
        copy.wait()


def call(kernel, name, out_shape, scratch, *operands, vmem=16, loads=(), aliases=None, micros=0):
    operands = list(operands)
    specs = [pl.BlockSpec(memory_space=pltpu.VMEM) for entry in operands]
    operands += [pltpu.with_memory_space_constraint(entry, pltpu.HBM) for entry in loads]
    specs += [pl.BlockSpec(memory_space=pltpu.HBM) for entry in loads]
    return pl.pallas_call(
        kernel,
        name=name,
        out_shape=out_shape,
        in_specs=specs,
        out_specs=jax.tree.map(
            lambda entry: pl.BlockSpec(
                memory_space=pltpu.VMEM if isinstance(entry, jax.ShapeDtypeStruct) else pltpu.HBM
            ),
            out_shape,
        ),
        scratch_shapes=scratch,
        input_output_aliases=aliases or {},
        cost_estimate=pl.CostEstimate(flops=micros * 10**9, bytes_accessed=0, transcendentals=0)
        if micros
        else None,
        compiler_params=pltpu.CompilerParams(vmem_limit_bytes=vmem * MIB),
    )(*operands)


def shape(*dims, dtype=F32):
    return jax.ShapeDtypeStruct(dims, dtype)


def per_device(
    sizes,
    tokens,
    segment_ids,
    ln1_gain,
    ln1_bias,
    w_qkv,
    b_qkv,
    w_out,
    b_out,
    ln2_gain,
    ln2_bias,
    w_up,
    b_up,
    w_down,
    b_down,
    cotangent,
):
    dp_size, seq_size = sizes
    block = tokens.shape[1]
    length = segment_ids.shape[1]
    def swap(value, dp_bits, seq_bits):
        pairs = [
            (a * seq_size + b, (a ^ dp_bits) * seq_size + (b ^ seq_bits))
            for a in range(dp_size)
            for b in range(seq_size)
        ]
        return lax.ppermute(value, ("dp", "seq"), pairs)

    tie = lax.optimization_barrier

    x_t = tokens[0].T
    near = {bits: swap(x_t, 0, bits) for bits in (2, 1)}
    loads = (
        x_t,
        segment_ids,
        ln1_gain,
        ln1_bias,
        w_qkv,
        b_qkv,
        cotangent[0].T,
        w_up,
        w_down.T,
        w_out,
        b_out,
        ln2_gain,
        ln2_bias,
        b_up,
    )
    like = lambda entry: jax.ShapeDtypeStruct(entry.shape, entry.dtype)
    buffer = lambda entry: pltpu.VMEM(entry.shape, entry.dtype)
    out = call(
        prelude_kernel,
        "prelude",
        (like(x_t), *[like(entry) for entry in loads[6:]])
        + (
            shape(3 * D, D, dtype=BF),
            shape(5 * D, 8),
            shape(HEAD_DIM // 2, length),
            shape(HEAD_DIM // 2, length),
            shape(block, DP, dtype=BF),
            shape(D, block, dtype=BF),
            shape(DP, block, dtype=BF),
            shape(DP, block, dtype=BF),
            shape(LANES, length, dtype=BF),
            shape(block, LANES, dtype=BF),
        ),
        [buffer(entry) for entry in loads[1:6]] + [pltpu.SemaphoreType.DMA((len(loads),))],
        loads=loads,
    )
    near[2], *out = tie((near[2], *out))
    near[3] = swap(near[2], 0, 1)
    x0, ct_t, w_up, w_down_t, w_out, b_out, ln2_gain, ln2_bias, b_up = out[:9]
    wqkv_t, cols, cosine, sine, q, q_t, k_t, v_t, ke, qe = out[9:]
    early_block = shape(2, EARLY_ROWS, SHARD_COLS, dtype=BF)
    blocks = shape(4, *early_block.shape, dtype=BF)
    grad_middle, keep, *sends, k_t, v_t, probs, branch, attended, share, x_all, middle, active = call(
        forward_kernel,
        "layer_forward",
        (
            shape(block, D),
            blocks,
            *[early_block] * 4,
            shape(DP, length, dtype=BF),
            shape(DP, length, dtype=BF),
            shape(HEADS, block, length, dtype=BF),
            shape(block, D, dtype=BF),
            shape(block, DP),
            shape(block, DP),
            pltpu.HBM((4, D, block), BF),
            pltpu.HBM((block, D), F32),
            pltpu.HBM((block, FF), BF),
        ),
        [
            pltpu.VMEM((D, 3 * block), BF),
            pltpu.VMEM((block, D), F32),
            pltpu.VMEM((block, FF), BF),
            pltpu.SemaphoreType.DMA((4,)),
            pltpu.SemaphoreType.DMA((2,)),
        ],
        x0,
        near[1],
        near[2],
        near[3],
        k_t,
        v_t,
        q,
        q_t,
        ke,
        qe,
        cosine,
        sine,
        wqkv_t,
        cols,
        w_out,
        b_out,
        ln2_gain,
        ln2_bias,
        w_up,
        b_up,
        w_down_t,
        ct_t,
        vmem=28,
    )

    move_core, move_x, move_y, move_z, move_z2 = (0, 1), (1, 0), (0, 2), (2, 0), (4, 0)

    def add(first_term, second_term, *after):
        return call(plus_kernel, "add", like(first_term), [], first_term, second_term, *after)

    def far_sum(part):
        bit = 8
        while bit < dp_size:
            part = add(part, swap(part, bit, 0))
            bit *= 2
        return part

    def step(piece, after, grads, loads=()):
        operands = (cosine, sine, q_t, k_t, v_t, probs, share, inner, d_out, d_out_t)
        first = 1 + len(operands)
        heads = PIECES[piece]
        rows = len(heads) * HEAD_DIM
        tiles = heads[-1] // TILE_HEADS - heads[0] // TILE_HEADS + 1
        return call(
            functools.partial(piece_kernel, heads, len(loads)),
            f"attention_backward_{piece}",
            (
                shape(D, block, dtype=BF),
                shape(D, length, dtype=BF),
                shape(D, length, dtype=BF),
                *[like(entry) for entry in loads],
            ),
            [
                pltpu.VMEM((tiles * LANES, block), F32),
                pltpu.VMEM((rows, length), F32),
                pltpu.VMEM((rows, length), F32),
                pltpu.SemaphoreType.DMA((max(1, len(loads)),)),
            ],
            after,
            *operands,
            *grads,
            aliases={first + i: i for i in range(len(grads))},
            loads=loads,
            vmem=28,
        )

    def split(name, keep, got):
        return call(split_kernel, name, (like(keep[0]),) * 4, [], keep, got)

    moves = [move_y, move_x, (1, 2)]

    def square_swap(parts):
        return [swap(part, *move) for part, move in zip(parts, moves)]

    gots = {place: swap(sends[place], *move_core) for place in (1, 2, 3, 0)}
    d_out, d_out_t, inner = call(
        finish_kernel,
        "layer_finish",
        (shape(block, DP, dtype=BF), shape(D, block, dtype=BF), shape(block, DP)),
        [],
        branch,
        attended,
        share,
        w_out,
    )
    kept, *sends = [
        call(
            functools.partial(part_kernel, place), "add_core", early_block, [], keep, gots[place]
        )
        for place in range(4)
    ]
    gots = square_swap(sends)
    grads = step(0, sends[2], (), (x_all, w_qkv, ln1_gain, ln1_bias))
    *gots, first_grad = tie((*gots, grads[0]))
    grads = (first_grad, *grads[1:])
    half = shape(EARLY_ROWS, SHARD_COLS, dtype=BF)
    kept, sent = call(choose_kernel, "add_square", (half, half), [], kept, *gots)
    if dp_size > 2:
        got = swap(sent, *move_z)
    late_blocks = shape(4, LATE_ROWS, SHARD_COLS, dtype=BF)
    late_keep, late_send, own, far = call(
        projection_kernel,
        "projection",
        (late_blocks, late_blocks, shape(2, D, block), shape(2, D, block, dtype=BF)),
        [pltpu.VMEM((D, LATE_COLS), F32)],
        sent,
        *grads,
    )
    if dp_size > 2:
        got, late_send = tie((got, late_send))
        kept = add(kept, got)
    if dp_size > 4:
        got = swap(kept, *move_z2)
    core_far = swap(far, *move_core)
    late, *sends = split("add_late_core", late_keep, swap(late_send, *move_core))
    gots = square_swap(sends)
    if dp_size > 4:
        gots[2], gots[0], got = tie((gots[2], gots[0], got))
        kept = far_sum(add(kept, got))
    late = call(square_kernel, "add_late_square", like(late), [], late, *gots)
    other = swap(kept, *move_z) if dp_size > 2 else sent
    late, core_far = tie((late, core_far))
    chip_far = swap(plus(own[1], core_far[1]), *move_y)
    if dp_size > 2:
        got, chip_far = tie((swap(late, *move_z), chip_far))
        late = add(late, got)
    early_a, early_b = call(both_kernel, "early_both", (half, half), [], kept, other)
    input_grad = call(
        input_kernel,
        "input_gradient",
        shape(D, block),
        [],
        own,
        core_far,
        chip_far,
        x0,
        ln1_gain,
        grad_middle,
        micros=1,
    )
    got_a, got_b = swap(early_a, *move_y), swap(early_b, *move_x)
    if dp_size > 4:
        got, got_a, got_b, input_grad = tie((swap(late, *move_z2), got_a, got_b, input_grad))
        late = far_sum(add(late, got))
    both = shape(2 * EARLY_ROWS + LATE_ROWS, SHARD_COLS, dtype=BF)
    own_x, own_y = call(
        send_kernel, "send", (both, both), [], early_a, got_a, early_b, got_b, late
    )
    parts = (middle, active, w_down.T, b_down)
    output = call(
        output_kernel,
        "layer_output",
        shape(D, block, dtype=BF),
        [*[buffer(entry) for entry in parts], pltpu.SemaphoreType.DMA((len(parts),))],
        loads=parts,
    )
    *gots, output = tie(
        (swap(own_x, *move_x), swap(own_y, *move_y), swap(late, 1, 2), output)
    )
    gathered = shape(GATHERED_ROWS, SHARD_COLS, dtype=BF)
    blocks = call(gather_kernel, "gather_blocks", gathered, [], own_x, own_y, *gots)
    far_blocks = swap(blocks, *move_core)
    in_hbm = (pltpu.HBM((D, FF), F32), pltpu.HBM((D, FF), F32), pltpu.HBM((D, 3 * D), F32))
    assembled = (shape(D, LANES), shape(16, EXTRA_ROWS, SHARD_COLS))
    values = [pltpu.VMEM((4, LATE_DEPTH, 3 * D), F32), pltpu.VMEM((8, SHARD_ROWS, SHARD_COLS), F32)]
    g_up, g_down_t, g_qkv, *own_parts = call(
        unpack_own_kernel,
        "unpack_own",
        (*in_hbm, *assembled),
        [*values, pltpu.SemaphoreType.DMA((12,))],
        blocks,
    )
    sizes = (3 * D, D, D, FF, D, D, D, D)
    vectors = [pltpu.HBM((size,), F32) for size in sizes]
    g_up, g_down_t, g_qkv, _, _, g_out, *vectors = call(
        unpack_far_kernel,
        "unpack_far",
        (*in_hbm, *assembled, pltpu.HBM((D, D), F32), *vectors),
        [
            *[pltpu.VMEM((size,), F32) for size in sizes],
            pltpu.VMEM((8, 5 * D), F32),
            pltpu.VMEM((D, D), F32),
            *values,
            pltpu.SemaphoreType.DMA((21,)),
        ],
        far_blocks,
        *own_parts,
        loads=(g_up, g_down_t, g_qkv),
        aliases={3: 0, 4: 1, 5: 2, 1: 3, 2: 4},
    )
    g_bqkv, g_ln1_gain, g_ln1_bias, g_bup, g_bout, g_ln2_gain, g_ln2_bias, g_bdown = vectors
    return (
        output.T[None],
        input_grad.T[None],
        g_ln1_gain,
        g_ln1_bias,
        g_qkv,
        g_bqkv,
        g_out,
        g_bout,
        g_ln2_gain,
        g_ln2_bias,
        g_up,
        g_bup,
        g_down_t.T,
        g_bdown,
    )


def solution(mesh):
    split = P("dp", "seq", None)
    whole = P()
    return jax.shard_map(
        functools.partial(per_device, (mesh.shape["dp"], mesh.shape["seq"])),
        mesh=mesh,
        in_specs=(split, P("dp", None)) + (whole,) * 12 + (split,),
        out_specs=(split, split) + (whole,) * 12,
        check_vma=False,
    )
```
